32 devices in a mesh: group: 8 (over y, x, core), ctx: 4 (over z).
Axes of the slice: x: 2, y: 2, z: 4, core: 2. Of those that a mesh axis runs over, the one named last changes fastest.
Arguments:
- query: bfloat16 [8, 4, 32, 8192], P('group', None, None, 'ctx'), may hold values from -160 to 160
- cache_keys: bfloat16 [8, 4, 2048, 1024], P('group', None, 'ctx'), may hold values from -6 to 6
- cache_values: bfloat16 [8, 4, 2048, 1024], P('group', None, 'ctx'), may hold values from -6 to 6
- new_keys: bfloat16 [8, 4, 32, 1024], P('group', None, 'ctx'), may hold values from -6 to 6
- new_values: bfloat16 [8, 4, 32, 1024], P('group', None, 'ctx'), may hold values from -6 to 6
- masks: int32 [3], replicated, may hold values from 1 to 7
- movers: int32 [3, 8], replicated, may hold values from 0 to 3
- block_lists: int32 [3, 8, 4], replicated, may hold values from 0 to 3, as said below
- lengths: int32 [8, 4], replicated, may hold values from 1 to 2048
Outputs:
- attended: bfloat16 [8, 4, 32, 8192], P('group', None, None, 'ctx')
- keys_after: bfloat16 [8, 4, 2048, 1024], P('group', None, 'ctx')
- values_after: bfloat16 [8, 4, 2048, 1024], P('group', None, 'ctx')
The draws below stay inside these ranges and needn't reach their ends.
Inputs may be any that keep to these rules, and one draw needn't show every extreme that they name: `block_lists`: each row is a permutation of the 4 blocks.
All inputs are finite; a program needn't handle non-finite values.
Results may differ from the reference program's by a relative error of at most 0.005.
Values may be sent and summed in bfloat16 or wider, within the bound.
No kernel may reach another device: no remote copies, remote signals or barrier semaphores. Data moves between devices by JAX's collectives and lax.ppermute only.
A program may use at most 192 MiB of HBM per device.

```python
import jax
import jax.numpy as jnp
from jax import lax

QH = 64
KVH = 8
HD = 128
R = 4
NEW = 32
MATCHINGS = 3
BLOCK = 128
GQ = 8
NB = 4
MOVE = 4
LEN = 2048
GROUPS = 8
N_GROUP = 8
N_CTX = 4


def anchors(key):
    base = jax.random.fold_in(key, 11)
    parts = jax.random.split(base, 4)
    lead_levels = jax.random.randint(parts[0], (KVH, HD), -32, 33).astype(jnp.float32)
    lead_nudges = jax.random.randint(parts[1], (KVH, HD), -1, 2).astype(jnp.float32)
    side_levels = jax.random.randint(parts[2], (KVH, HD), -24, 25).astype(jnp.float32)
    side_nudges = jax.random.randint(parts[3], (KVH, HD), -1, 2).astype(jnp.float32)
    leading = lead_levels / 16.0
    nearby = (lead_levels + lead_nudges) / 16.0
    side = side_levels / 16.0
    side_near = (side_levels + side_nudges) / 16.0
    return (leading, nearby, side, side_near)


def paired_draw(key):
    leading, nearby, side, side_near = anchors(key)
    base = jax.random.fold_in(key, 7)
    parts = jax.random.split(base, 7)
    fresh = jnp.clip(jax.random.normal(parts[0], (GROUPS, R, NEW, KVH, HD), jnp.float32), -6.0, 6.0)
    lead_rows = jnp.broadcast_to(leading[None, None, None], (GROUPS, R, 1, KVH, HD))
    near_rows = jnp.broadcast_to(nearby[None, None, None], (GROUPS, R, 1, KVH, HD))
    fresh = jnp.concatenate([lead_rows, near_rows, fresh[:, :, 2:]], axis=2)
    asked = jnp.clip(2.0 * jax.random.normal(parts[1], (GROUPS, R, NEW, KVH, QH // KVH, HD), jnp.float32), -12.0, 12.0)
    strength = 4.0 * jax.random.randint(parts[3], (GROUPS, R, NEW, KVH, QH // KVH, 1), 3, 7).astype(jnp.float32)
    later = (jnp.arange(NEW) >= 1)[None, None, :, None, None, None]
    picked = jnp.logical_and(jax.random.bernoulli(parts[4], 0.06, (GROUPS, R, NEW, KVH, QH // KVH, 1)), later)
    asked = jnp.where(picked, strength * leading[None, None, None, :, None, :], asked)
    side_strength = 4.0 * jax.random.randint(parts[5], (GROUPS, R, NEW, KVH, QH // KVH, 1), 5, 8).astype(jnp.float32)
    side_picked = jnp.logical_and(jax.random.bernoulli(parts[6], 0.06, (GROUPS, R, NEW, KVH, QH // KVH, 1)), jnp.logical_not(picked))
    asked = jnp.where(side_picked, side_strength * side[None, None, None, :, None, :], asked)
    return (asked.reshape(GROUPS, R, NEW, QH * HD), fresh.reshape(GROUPS, R, NEW, KVH * HD))


def draw_query(key, part):
    return paired_draw(key)[0].astype(jnp.bfloat16)


def draw_new_keys(key, part):
    return paired_draw(key)[1].astype(jnp.bfloat16)


def draw_cache_keys(key, part):
    leading, nearby, side, side_near = anchors(key)
    inner = jax.random.fold_in(key, 13)
    rest = jnp.clip(jax.random.normal(inner, (GROUPS, R, LEN, KVH, HD), jnp.float32), -6.0, 6.0)
    within = (jnp.arange(LEN, dtype=jnp.int32) % BLOCK)[None, None, :, None, None]
    rest = jnp.where(within == 2, side_near[None, None, None], rest)
    rest = jnp.where(within == 1, side[None, None, None], rest)
    rest = jnp.where(within == 0, leading[None, None, None], rest)
    return rest.reshape(GROUPS, R, LEN, KVH * HD).astype(jnp.bfloat16)


def draw_block_lists(key, part):
    scores = jax.random.randint(jax.random.fold_in(key, 3), (MATCHINGS, GROUPS, NB), 0, 1 << 20) * NB
    scores = scores + jnp.arange(NB, dtype=jnp.int32)
    order = jnp.argsort(scores, axis=-1)
    return order[..., :MOVE].astype(jnp.int32)


def plant(array, own_key, least, high):
    spot = [jax.random.randint(jax.random.fold_in(own_key, axis), (), 0, length) for axis, length in enumerate(array.shape)]
    widest = array.shape.index(max(array.shape))
    neighbour = spot[:widest] + [(spot[widest] + 1) % array.shape[widest]] + spot[widest + 1:]
    return array.at[tuple(spot)].set(least).at[tuple(neighbour)].set(high)


def block_scale(key, shape, cuts, low, high):
    level, own = 1.0, jax.random.fold_in(key, 6)
    for dim, blocks in cuts:
        draws = jnp.exp(jax.random.uniform(jax.random.fold_in(own, dim), (blocks,), jnp.float32, low / len(cuts), high / len(cuts)))
        level = level * jnp.repeat(draws, shape[dim] // blocks).reshape([-1 if axis == dim else 1 for axis in range(len(shape))])
    return level


def gaussian(own_key, dims, deviation, bound, shards=(), kind=jnp.bfloat16):
    result = jax.random.normal(own_key, dims, jnp.float32) * deviation
    if len(shards) > 0:
        result = block_scale(own_key, dims, shards, -0.22, 0.18) * result
    return jnp.clip(result, min=-bound, max=bound).astype(kind)


def setup_inputs(seed: int = 0) -> dict:
    key_of = jax.random.split(jax.random.key(seed), 10)
    return {
        "query": draw_query(jax.random.fold_in(key_of[9], 71), 0),
        "cache_keys": draw_cache_keys(jax.random.fold_in(key_of[9], 71), 0),
        "cache_values": gaussian(key_of[2], (GROUPS, R, LEN, KVH * HD), 1.0, 6.0, ((0, 8), (2, 4))),
        "new_keys": draw_new_keys(jax.random.fold_in(key_of[9], 71), 0),
        "new_values": gaussian(key_of[4], (GROUPS, R, NEW, KVH * HD), 1.0, 6.0, ((0, 8), (2, 4))),
        "masks": jax.random.randint(key_of[5], (MATCHINGS,), 1, N_GROUP).astype(jnp.int32),
        "movers": plant(jax.random.randint(key_of[6], (MATCHINGS, GROUPS), 0, R), jax.random.fold_in(key_of[6], 1), 0, R - 1).astype(jnp.int32),
        "block_lists": draw_block_lists(jax.random.fold_in(key_of[9], 71), 0),
        "lengths": plant(jax.random.randint(key_of[8], (GROUPS, R), 1, LEN + 1), jax.random.fold_in(key_of[8], 1), 1, LEN).astype(jnp.int32),
    }


def attend_group(args):
    query, keys, values, fresh_keys, fresh_values, counts = args
    scale = 1.0 / (HD ** 0.5)
    heads_q = query.astype(jnp.float32).reshape(R, NEW, KVH, GQ, HD)
    keys_h = keys.astype(jnp.float32).reshape(R, LEN, KVH, HD)
    values_h = values.astype(jnp.float32).reshape(R, LEN, KVH, HD)
    fresh_k = fresh_keys.astype(jnp.float32).reshape(R, NEW, KVH, HD)
    fresh_v = fresh_values.astype(jnp.float32).reshape(R, NEW, KVH, HD)
    older = jnp.einsum('rtkgd,rskd->rkgts', heads_q, keys_h, precision=lax.Precision.HIGHEST) * scale
    newer = jnp.einsum('rtkgd,rskd->rkgts', heads_q, fresh_k, precision=lax.Precision.HIGHEST) * scale
    valid_old = (jnp.arange(LEN, dtype=jnp.int32)[None, :] < counts[:, None])[:, None, None, None, :]
    valid_new = (jnp.arange(NEW, dtype=jnp.int32)[None, :] <= jnp.arange(NEW, dtype=jnp.int32)[:, None])[None, None, None, :, :]
    older = jnp.where(valid_old, older, -jnp.inf)
    newer = jnp.where(valid_new, newer, -jnp.inf)
    top = jnp.maximum(jnp.max(older, axis=-1), jnp.max(newer, axis=-1))
    exp_old = jnp.where(valid_old, jnp.exp(older - top[..., None]), 0.0)
    exp_new = jnp.where(valid_new, jnp.exp(newer - top[..., None]), 0.0)
    total = jnp.sum(exp_old, axis=-1) + jnp.sum(exp_new, axis=-1)
    weight_old = exp_old.astype(jnp.bfloat16).astype(jnp.float32)
    weight_new = exp_new.astype(jnp.bfloat16).astype(jnp.float32)
    summed = jnp.einsum('rkgts,rskd->rtkgd', weight_old, values_h, precision=lax.Precision.HIGHEST)
    summed = summed + jnp.einsum('rkgts,rskd->rtkgd', weight_new, fresh_v, precision=lax.Precision.HIGHEST)
    summed = summed / jnp.transpose(total, (0, 3, 1, 2))[..., None]
    return summed.reshape(R, NEW, QH * HD).astype(jnp.bfloat16)


def reference(query, cache_keys, cache_values, new_keys, new_values, masks, movers, block_lists, lengths):
    every = jnp.arange(GROUPS, dtype=jnp.int32)
    features = KVH * HD
    keys = cache_keys.reshape(GROUPS, R, N_CTX, NB, BLOCK, features)
    values = cache_values.reshape(GROUPS, R, N_CTX, NB, BLOCK, features)
    counts = lengths
    for step in range(MATCHINGS):
        partner = jnp.bitwise_xor(every, masks[step]).astype(jnp.int32)
        slots = movers[step]
        chosen = block_lists[step]
        row_index = every[:, None]
        slot_index = slots[:, None]
        sent_keys = keys[row_index, slot_index, :, chosen]
        sent_values = values[row_index, slot_index, :, chosen]
        keys = keys.at[row_index, slot_index, :, chosen].set(sent_keys[partner])
        values = values.at[row_index, slot_index, :, chosen].set(sent_values[partner])
        counts = counts.at[every, slots].set(counts[partner, slots[partner]])
    keys_after = keys.reshape(GROUPS, R, LEN, features)
    values_after = values.reshape(GROUPS, R, LEN, features)
    attended = lax.map(attend_group, (query, keys_after, values_after, new_keys, new_values, counts))
    return attended, keys_after, values_after
```

```python
import functools
import math

import jax
import jax.numpy as jnp
from jax import lax
from jax.experimental import pallas as pl
from jax.experimental.pallas import tpu as pltpu
from jax.sharding import PartitionSpec as P

HD = 128
LANES = 128
MASKED = -1e30
FLOOR = -1e29
BF16 = jnp.bfloat16
F32 = jnp.float32
ANY = pl.BlockSpec(memory_space=pl.ANY)
SMEM = pl.BlockSpec(memory_space=pltpu.SMEM)
VMEM = pl.BlockSpec(memory_space=pltpu.VMEM)


def exchange(block, axis, mask):
    return lax.ppermute(block, axis, [(i, i ^ mask) for i in range(lax.axis_size(axis))])


class Layout:
    def __init__(self, requests, nblocks, matchings):
        self.slot = 0
        self.last = requests
        self.count = 2 * requests
        self.perm = 3 * requests
        self.home = self.perm + requests * nblocks
        self.mover = self.home + requests * nblocks
        self.source = self.mover + matchings
        self.place = self.source + matchings
        self.size = self.place + 1


def plan_kernel(
    at, masks, movers, lists, lengths, keys, values, plan, key_out, value_out, sems
):
    matchings, groups, nblocks = lists.shape
    requests = lengths.shape[1]
    here = lax.axis_index("group")
    first = movers[0, here]
    copies = [
        pltpu.make_async_copy(keys.at[0, first], key_out, sems.at[0]),
        pltpu.make_async_copy(values.at[0, first], value_out, sems.at[1]),
    ]
    for copy in copies:
        copy.start()
    plan[at.place] = lax.axis_index("ctx")
    traced = []
    for slot in range(requests):
        group, where = here, jnp.int32(slot)
        last = jnp.int32(-1)
        blocks = [jnp.int32(b) for b in range(nblocks)]
        for step in reversed(range(matchings)):
            hit = movers[step, group] == where
            partner = group ^ masks[step]
            last = jnp.where(jnp.logical_and(hit, last < 0), step, last)
            moved = []
            for block in blocks:
                origin = block
                for j in range(nblocks):
                    origin = jnp.where(
                        lists[step, group, j] == block, lists[step, partner, j], origin
                    )
                moved.append(jnp.where(hit, origin, block))
            blocks = moved
            where = jnp.where(hit, movers[step, partner], where)
            group = jnp.where(hit, partner, group)
        traced.append((last, lengths[group, where], blocks))
    for slot in range(requests):
        last, count, blocks = traced[slot]
        rank = jnp.int32(0)
        for other in range(requests):
            if other != slot:
                ahead = traced[other][0] * requests + other < last * requests + slot
                rank = rank + ahead.astype(jnp.int32)
        plan[at.slot + rank] = jnp.int32(slot)
        plan[at.last + rank] = last
        plan[at.count + rank] = count
        for b in range(nblocks):
            plan[at.perm + rank * nblocks + b] = blocks[b]
            plan[at.home + rank * nblocks + blocks[b]] = jnp.int32(b)
    for step in range(matchings):
        mover = movers[step, here]
        source = jnp.int32(-1)
        for earlier in range(step):
            source = jnp.where(movers[earlier, here] == mover, earlier, source)
        plan[at.mover + step] = mover
        plan[at.source + step] = source
    for copy in copies:
        copy.wait()


def pick_kernel(at, step, plan, *refs):
    sources, (key_out, value_out), sems = refs[: 2 * step + 2], refs[-3:-1], refs[-1]
    mover, source = plan[at.mover + step], plan[at.source + step]
    for code in range(-1, step):
        pair = sources[2 * code + 2 : 2 * code + 4]

        @pl.when(source == code)
        def _():
            views = [ref.at[0, mover] for ref in pair] if code < 0 else pair
            copies = [
                pltpu.make_async_copy(view, out, sems.at[n])
                for n, (view, out) in enumerate(zip(views, (key_out, value_out)))
            ]
            for copy in copies:
                copy.start()
            for copy in copies:
                copy.wait()


def settle_kernel(at, ready, plan, *refs):
    sources, (keys_after, values_after), sems = refs[:-3], refs[-3:-1], refs[-1]
    _, requests, segment, _ = keys_after.shape
    nblocks = (at.home - at.perm) // requests
    rows = segment // nblocks
    for position in range(requests):
        slot, last = plan[at.slot + position], plan[at.last + position]
        for code in range(-1, ready[position] + 1):
            pair = sources[2 * code + 2 : 2 * code + 4]

            @pl.when(last == code)
            def _():
                views = [ref.at[0, slot] for ref in pair] if code < 0 else pair
                for n, (view, out) in enumerate(zip(views, (keys_after, values_after))):
                    for b in range(nblocks):
                        origin = plan[at.perm + position * nblocks + b]
                        begin = pl.multiple_of(origin * rows, rows)
                        pltpu.make_async_copy(
                            view.at[pl.ds(begin, rows)],
                            out.at[0, slot, pl.ds(b * rows, rows)],
                            sems.at[n, position],
                        ).start()

    for position in range(requests):
        for n, out in enumerate((keys_after, values_after)):
            whole = out.at[0, plan[at.slot + position]]
            pltpu.make_async_copy(whole, whole, sems.at[n, position]).wait()


def attend_kernel(at, positions, ready, width, tokens, plan, *refs):
    count = len(positions)
    q_refs, refs = refs[:width], refs[width:]
    (new_k, new_v), refs = refs[:2], refs[2:]
    outs, (kbuf, vbuf, qbuf, sems) = refs[-4 - width : -4], refs[-4:]
    sources = refs[: -4 - width]
    requests, local_new, features = new_k.shape
    segment = kbuf.shape[1] - LANES
    nblocks = (at.home - at.perm) // requests
    rows = segment // nblocks
    own = q_refs[0].shape[3] // HD
    shared = own * width * HD // features
    kv_own = own // shared
    place = plan[at.place]
    fresh = local_new_of(tokens, width)

    for n, position in enumerate(positions):
        slot, last = plan[at.slot + position], plan[at.last + position]
        for code in range(-1, ready[position] + 1):
            pair = sources[2 * code + 2 : 2 * code + 4]

            @pl.when(last == code)
            def _():
                views = [ref.at[0, slot] for ref in pair] if code < 0 else pair
                for view, buf, sem in zip(views, (kbuf, vbuf), (0, 1)):
                    pltpu.make_async_copy(
                        view, buf.at[n, pl.ds(0, segment)], sems.at[sem, n]
                    ).start()

        for i in range(width):
            pltpu.make_async_copy(q_refs[i].at[0, slot], qbuf.at[n, i], sems.at[2, n]).start()

    for n, position in enumerate(positions):
        slot = plan[at.slot + position]
        for buf, new in ((kbuf, new_k), (vbuf, new_v)):
            buf[n, segment:, :] = jnp.zeros((LANES, features), BF16)
            buf[n, segment : segment + local_new, :] = new[slot]

    lane = lax.broadcasted_iota(jnp.int32, (1, LANES), 1)
    queries = shared * tokens
    token = lax.broadcasted_iota(jnp.int32, (queries, LANES), 0) % tokens
    column = lax.broadcasted_iota(jnp.int32, (queries, LANES), 1)
    allowed = jnp.logical_and(column < fresh, column + place * fresh <= token)
    new_bias = jnp.where(allowed, 0.0, MASKED).astype(F32)
    stat_lane = lax.broadcasted_iota(jnp.int32, (tokens, LANES), 1)
    scale = math.log2(math.e) / HD**0.5

    for n, position in enumerate(positions):
        length = plan[at.count + position]
        biases = []
        for b in range(nblocks):
            home = plan[at.home + position * nblocks + b]
            limit = length - place * segment - home * rows
            for part in range(rows // LANES):
                biases.append(jnp.where(lane + part * LANES < limit, 0.0, MASKED).astype(F32))
        bias = jnp.concatenate(biases, axis=1)
        for buf, sem in ((kbuf, 0), (vbuf, 1)):
            view = buf.at[n, pl.ds(0, segment)]
            pltpu.make_async_copy(view, view, sems.at[sem, n]).wait()
        pltpu.make_async_copy(qbuf.at[n], qbuf.at[n], sems.at[2, n]).wait()
        for i in range(width):
            tops = jnp.zeros((tokens, LANES), F32)
            totals = jnp.zeros((tokens, LANES), F32)
            for j in range(kv_own):
                head = (place ^ i) * kv_own + j
                cols = pl.ds(pl.multiple_of(head * HD, HD), HD)
                base = j * shared * HD
                asked = jnp.concatenate(
                    [
                        qbuf[n, i, :, base + s * HD : base + (s + 1) * HD]
                        for s in range(shared)
                    ],
                    axis=0,
                )
                scores = lax.dot_general(
                    asked,
                    kbuf[n, :, cols],
                    (((1,), (1,)), ((), ())),
                    preferred_element_type=F32,
                )
                older = scores[:, :segment] * scale + bias
                newer = scores[:, segment:] * scale + new_bias
                top = jnp.maximum(
                    jnp.max(older, axis=1, keepdims=True),
                    jnp.max(newer, axis=1, keepdims=True),
                )
                top = jnp.maximum(top, FLOOR)
                older = jnp.exp2(older - top)
                newer = jnp.exp2(newer - top)
                total = jnp.sum(older, axis=1, keepdims=True) + jnp.sum(
                    newer, axis=1, keepdims=True
                )
                weights = jnp.concatenate([older.astype(BF16), newer.astype(BF16)], axis=1)
                summed = jnp.dot(
                    weights, vbuf[n, :, cols], preferred_element_type=F32
                ).astype(BF16)
                for s in range(shared):
                    part = slice(s * tokens, (s + 1) * tokens)
                    outs[i][n, :, base + s * HD : base + (s + 1) * HD] = summed[part]
                    chosen = stat_lane == j * shared + s
                    tops = jnp.where(chosen, top[part], tops)
                    totals = jnp.where(chosen, total[part], totals)
            outs[i][n, :, own * HD :] = pack_stats(tops, totals, own).astype(BF16)


def local_new_of(tokens, width):
    return tokens // width


def split(value, parts):
    result = []
    for _ in range(parts):
        result.append(value.astype(BF16).astype(F32))
        value = value - result[-1]
    return result


def pack_stats(tops, totals, own):
    packed = jnp.zeros_like(tops)
    for n, part in enumerate(split(tops, 3) + split(totals, 2)):
        packed = packed + (pltpu.roll(part, n * own, 1) if n else part)
    return packed


def unpack_stats(packed, own):
    parts = [pltpu.roll(packed, LANES - n * own, 1) if n else packed for n in range(5)]
    return (parts[0] + parts[1]) + parts[2], parts[3] + parts[4]


def combine_kernel(at, width, lots, plan, *refs):
    out = refs[-1]
    own = out.shape[3] // HD
    for lot, positions in enumerate(lots):
        pieces = refs[lot * width : (lot + 1) * width]
        for n, position in enumerate(positions):
            slot = plan[at.slot + position]
            stats = [
                unpack_stats(piece[n, :, own * HD :].astype(F32), own) for piece in pieces
            ]
            peak = functools.reduce(jnp.maximum, [top for top, _ in stats])
            factors = [jnp.exp2(top - peak) for top, _ in stats]
            denom = sum(total * factor for (_, total), factor in zip(stats, factors))
            shares = [factor / denom for factor in factors]
            for h in range(own):
                cols = slice(h * HD, (h + 1) * HD)
                mixed = sum(
                    piece[n, :, cols].astype(F32) * share[:, h : h + 1]
                    for piece, share in zip(pieces, shares)
                )
                out[0, slot, :, cols] = mixed.astype(BF16)


def shards(
    query, cache_keys, cache_values, new_keys, new_values, masks, movers, block_lists, lengths
):
    groups = lax.axis_size("group")
    width = lax.axis_size("ctx")
    _, requests, segment, features = cache_keys.shape
    tokens = query.shape[2]
    matchings, _, nblocks = block_lists.shape
    own = query.shape[3] // HD
    at = Layout(requests, nblocks, matchings)
    ready = [max(-1, n - (requests - matchings)) for n in range(requests)]
    request = jax.ShapeDtypeStruct((segment, features), BF16)
    big = pltpu.CompilerParams(vmem_limit_bytes=48 * 1024 * 1024)
    request_bytes = 2 * segment * features * 2

    plan, moving_keys, moving_values = pl.pallas_call(
        functools.partial(plan_kernel, at),
        out_shape=(jax.ShapeDtypeStruct((at.size,), jnp.int32), request, request),
        in_specs=[SMEM] * 4 + [ANY] * 2,
        out_specs=(SMEM, ANY, ANY),
        scratch_shapes=[pltpu.SemaphoreType.DMA((2,))],
        name="plan",
    )(masks, movers, block_lists, lengths, cache_keys, cache_values)

    def pick(step, sources):
        return pl.pallas_call(
            functools.partial(pick_kernel, at, step),
            out_shape=(request, request),
            in_specs=[SMEM] + [ANY] * (2 * step + 2),
            out_specs=(ANY, ANY),
            scratch_shapes=[pltpu.SemaphoreType.DMA((2,))],
            cost_estimate=pl.CostEstimate(
                flops=0, bytes_accessed=2 * request_bytes, transcendentals=0
            ),
            name=f"pick_{step}",
        )(plan, *sources[: 2 * step + 2])

    def attend(positions, asked, fresh, sources):
        count = len(positions)
        used = 2 * (max(ready[n] for n in positions) + 2)
        rows = own * width * tokens * count
        results = pl.pallas_call(
            functools.partial(attend_kernel, at, positions, ready, width, tokens),
            out_shape=[jax.ShapeDtypeStruct((count, tokens, own * HD + LANES), BF16)] * width,
            in_specs=[SMEM] + [ANY] * width + [VMEM] * 2 + [ANY] * used,
            out_specs=[VMEM] * width,
            scratch_shapes=[
                pltpu.VMEM((count, segment + LANES, features), BF16),
                pltpu.VMEM((count, segment + LANES, features), BF16),
                pltpu.VMEM((count, width, tokens, own * HD), BF16),
                pltpu.SemaphoreType.DMA((3, count)),
            ],
            compiler_params=big,
            cost_estimate=pl.CostEstimate(
                flops=4 * rows * segment * HD,
                bytes_accessed=count * request_bytes,
                transcendentals=rows * segment,
            ),
            name="attend_" + "_".join(map(str, positions)),
        )(plan, *asked, *fresh, *sources[:used])
        return results

    def send_home(results):
        return [results[0]] + [exchange(results[i], "ctx", i) for i in range(1, width)]

    def ask():
        return [query] + [exchange(query, "ctx", i) for i in range(1, width)]

    def pad_new():
        rows = new_keys.shape[2]
        extra = -rows % 16
        return [jnp.pad(new[0], ((0, 0), (0, extra), (0, 0))) for new in (new_keys, new_values)]

    sources = [cache_keys, cache_values]
    lots, pieces = [], []
    asked = fresh = None
    for step in range(matchings):
        if step:
            moving_keys, moving_values = pick(step, sources)
        positions = [n for n in range(requests) if ready[n] == step - 1 or (step == 1 and ready[n] < 0)]

        def branch(mask, moved, state):
            arrived = [exchange(block, "group", mask) for block in moved]
            if step == 0:
                return arrived, ask(), pad_new()
            asked, fresh, sources = state
            return arrived, send_home(attend(positions, asked, fresh, sources))

        result = lax.switch(
            masks[step] - 1,
            [functools.partial(branch, mask) for mask in range(1, groups)],
            [moving_keys, moving_values],
            (asked, fresh, sources),
        )
        sources = sources + result[0]
        if step == 0:
            asked, fresh = result[1:]
        else:
            lots.append(positions)
            pieces += result[1]

    positions = [n for n in range(requests) if ready[n] == matchings - 1]
    lots.append(positions)
    pieces += send_home(attend(positions, asked, fresh, sources))

    keys_after, values_after = pl.pallas_call(
        functools.partial(settle_kernel, at, ready),
        out_shape=[jax.ShapeDtypeStruct(cache_keys.shape, BF16)] * 2,
        in_specs=[SMEM] + [ANY] * len(sources),
        out_specs=[ANY, ANY],
        scratch_shapes=[pltpu.SemaphoreType.DMA((2, requests))],
        cost_estimate=pl.CostEstimate(
            flops=0, bytes_accessed=2 * requests * request_bytes, transcendentals=0
        ),
        name="settle",
    )(plan, *sources)

    attended = pl.pallas_call(
        functools.partial(combine_kernel, at, width, lots),
        out_shape=jax.ShapeDtypeStruct(query.shape, BF16),
        in_specs=[SMEM] + [VMEM] * len(pieces),
        out_specs=VMEM,
        compiler_params=big,
        name="combine",
    )(plan, *pieces)
    return attended, keys_after, values_after


def solution(mesh):
    placed = (
        P("group", None, None, "ctx"),
        P("group", None, "ctx", None),
        P("group", None, "ctx", None),
        P("group", None, "ctx", None),
        P("group", None, "ctx", None),
        P(),
        P(),
        P(),
        P(),
    )
    return jax.shard_map(
        shards,
        mesh=mesh,
        in_specs=placed,
        out_specs=(
            P("group", None, None, "ctx"),
            P("group", None, "ctx", None),
            P("group", None, "ctx", None),
        ),
        check_vma=False,
    )
```

```python
import functools
import math

import jax
import jax.numpy as jnp
from jax import lax
from jax.experimental import pallas as pl
from jax.experimental.pallas import tpu as pltpu
from jax.sharding import PartitionSpec as P

HD = 128
LANES = 128
HALF_HEADS = 1
MASKED = -1e30
FLOOR = -1e29
BF16 = jnp.bfloat16
F32 = jnp.float32
ANY = pl.BlockSpec(memory_space=pl.ANY)
SMEM = pl.BlockSpec(memory_space=pltpu.SMEM)
VMEM = pl.BlockSpec(memory_space=pltpu.VMEM)


def exchange(block, axis, mask):
    return lax.ppermute(block, axis, [(i, i ^ mask) for i in range(lax.axis_size(axis))])


class Layout:
    def __init__(self, requests, nblocks, matchings):
        self.slot = 0
        self.last = requests
        self.count = 2 * requests
        self.perm = 3 * requests
        self.home = self.perm + requests * nblocks
        self.mover = self.home + requests * nblocks
        self.source = self.mover + matchings
        self.place = self.source + matchings
        self.size = self.place + 1


def plan_kernel(
    at, masks, movers, lists, lengths, keys, values, plan, key_out, value_out, sems
):
    matchings, groups, nblocks = lists.shape
    requests = lengths.shape[1]
    here = lax.axis_index("group")
    first = movers[0, here]
    copies = [
        pltpu.make_async_copy(keys.at[0, first], key_out, sems.at[0]),
        pltpu.make_async_copy(values.at[0, first], value_out, sems.at[1]),
    ]
    for copy in copies:
        copy.start()
    plan[at.place] = lax.axis_index("ctx")
    traced = []
    for slot in range(requests):
        group, where = here, jnp.int32(slot)
        last = jnp.int32(-1)
        blocks = [jnp.int32(b) for b in range(nblocks)]
        for step in reversed(range(matchings)):
            hit = movers[step, group] == where
            partner = group ^ masks[step]
            last = jnp.where(jnp.logical_and(hit, last < 0), step, last)
            moved = []
            for block in blocks:
                origin = block
                for j in range(nblocks):
                    origin = jnp.where(
                        lists[step, group, j] == block, lists[step, partner, j], origin
                    )
                moved.append(jnp.where(hit, origin, block))
            blocks = moved
            where = jnp.where(hit, movers[step, partner], where)
            group = jnp.where(hit, partner, group)
        traced.append((last, lengths[group, where], blocks))
    for slot in range(requests):
        last, count, blocks = traced[slot]
        rank = jnp.int32(0)
        for other in range(requests):
            if other != slot:
                ahead = traced[other][0] * requests + other < last * requests + slot
                rank = rank + ahead.astype(jnp.int32)
        plan[at.slot + rank] = jnp.int32(slot)
        plan[at.last + rank] = last
        plan[at.count + rank] = count
        for b in range(nblocks):
            plan[at.perm + rank * nblocks + b] = blocks[b]
            plan[at.home + rank * nblocks + blocks[b]] = jnp.int32(b)
    for step in range(matchings):
        mover = movers[step, here]
        source = jnp.int32(-1)
        for earlier in range(step):
            source = jnp.where(movers[earlier, here] == mover, earlier, source)
        plan[at.mover + step] = mover
        plan[at.source + step] = source
    for copy in copies:
        copy.wait()


def pick_kernel(at, step, plan, *refs):
    sources, outs, sems = refs[: 2 * step + 2], refs[2 * step + 2 : -1], refs[-1]
    features = sources[0].shape[-1]
    halves = len(outs) // 2
    mover, source = plan[at.mover + step], plan[at.source + step]
    for code in range(-1, step):
        pair = sources[2 * code + 2 : 2 * code + 4]

        @pl.when(source == code)
        def _():
            for n, ref in enumerate(pair):
                view = ref.at[0, mover] if code < 0 else ref
                for half in range(halves):
                    out = outs[2 * half + n]
                    for cols, whole in columns_of(out.shape[1], features, half, halves):
                        pltpu.make_async_copy(
                            view.at[:, whole], out.at[:, cols], sems.at[half, n]
                        ).start()

    for half in range(halves):
        for n in range(2):
            out = outs[2 * half + n]
            pltpu.make_async_copy(out, out, sems.at[half, n]).wait()


def settle_kernel(at, ready, halves, plan, *refs):
    sources, refs = refs[:-5], refs[-5:]
    outs, bufs, sems = refs[:2], refs[2:4], refs[4]
    _, requests, segment, features = outs[0].shape
    nblocks = (at.home - at.perm) // requests
    rows = segment // nblocks
    final = len(sources) - 2 * halves
    for position in reversed(range(requests)):
        slot, last = plan[at.slot + position], plan[at.last + position]
        newest = ready[position]
        chunked = newest == max(ready)
        for code in range(newest if chunked else -1, newest + 1):

            @pl.when(last == code)
            def _():
                for n in range(2):
                    buf = bufs[n].at[position]
                    if chunked:
                        views = [sources[final + 2 * half + n] for half in range(halves)]
                    else:
                        views = [sources[2 * code + 2 + n]]
                        views = [views[0].at[0, slot] if code < 0 else views[0]]
                    for b in range(nblocks):
                        origin = plan[at.perm + position * nblocks + b]
                        begin = pl.multiple_of(origin * rows, rows)
                        into = pl.ds(b * rows, rows)
                        for half, view in enumerate(views):
                            for cols, whole in columns_of(view.shape[1], features, half, len(views)):
                                pltpu.make_async_copy(
                                    view.at[pl.ds(begin, rows), cols],
                                    buf.at[into, whole],
                                    sems.at[n, position],
                                ).start()

    for position in reversed(range(requests)):
        slot = plan[at.slot + position]
        for n in range(2):
            buf = bufs[n].at[position]
            pltpu.make_async_copy(buf, buf, sems.at[n, position]).wait()
            pltpu.make_async_copy(buf, outs[n].at[0, slot], sems.at[n, position]).start()
    for position in range(requests):
        slot = plan[at.slot + position]
        for n in range(2):
            pltpu.make_async_copy(
                bufs[n].at[position], outs[n].at[0, slot], sems.at[n, position]
            ).wait()


def columns_of(held, features, half, halves):
    if halves == 1:
        return [(pl.ds(0, held), pl.ds(0, features))]
    wide = HD * HALF_HEADS
    return [
        (pl.ds(n * wide, wide), pl.ds((n * halves + half) * wide, wide))
        for n in range(held // wide)
    ]


def attend_kernel(at, first, count, newest, half, halves, width, tokens, plan, *refs):
    q_refs, refs = refs[:width], refs[width:]
    (new_k, new_v), refs = refs[:2], refs[2:]
    outs, (kbuf, vbuf, qbuf, obuf, sems) = refs[-5 - width : -5], refs[-5:]
    sources = refs[: -5 - width]
    requests, local_new, features = new_k.shape
    segment = kbuf.shape[1] - LANES
    held = kbuf.shape[2]
    nblocks = (at.home - at.perm) // requests
    rows = segment // nblocks
    own = q_refs[0].shape[3] // HD
    shared = own * width * HD // features
    kv_own = own // shared
    kv_held = kv_own // halves
    wide = kv_held * shared * HD
    place = plan[at.place]
    fresh = tokens // width

    def start(view, buf, sem):
        pltpu.make_async_copy(view, buf.at[pl.ds(0, segment)], sem).start()

    for n in range(count):
        slot, last = plan[at.slot + first + n], plan[at.last + first + n]
        bufs = (kbuf.at[n], vbuf.at[n])
        if halves > 1:
            for m in range(2):
                start(sources[m], bufs[m], sems.at[m, n])
        else:
            for code in range(-1, newest[n] + 1):

                @pl.when(last == code)
                def _():
                    for m in range(2):
                        view = sources[2 * code + 2 + m]
                        start(view.at[0, slot] if code < 0 else view, bufs[m], sems.at[m, n])

        for i in range(width):
            pltpu.make_async_copy(
                q_refs[i].at[0, slot, :, pl.ds(half * wide, wide)], qbuf.at[n, i], sems.at[2, n]
            ).start()

    for n in range(count):
        slot = plan[at.slot + first + n]
        for buf, new in ((kbuf, new_k), (vbuf, new_v)):
            buf[n, segment:, :] = jnp.zeros((LANES, held), BF16)
            for cols, whole in columns_of(held, features, half, halves):
                buf[n, segment : segment + local_new, cols] = new[slot, :, whole]

    lane = lax.broadcasted_iota(jnp.int32, (1, LANES), 1)
    queries = shared * tokens
    token = lax.broadcasted_iota(jnp.int32, (queries, LANES), 0) % tokens
    column = lax.broadcasted_iota(jnp.int32, (queries, LANES), 1)
    allowed = jnp.logical_and(column < fresh, column + place * fresh <= token)
    new_bias = jnp.where(allowed, 0.0, MASKED).astype(F32)
    stat_lane = lax.broadcasted_iota(jnp.int32, (tokens, LANES), 1)
    scale = math.log2(math.e) / HD**0.5

    def request(n, carry):
        length = plan[at.count + first + n]
        biases = []
        for b in range(nblocks):
            home = plan[at.home + (first + n) * nblocks + b]
            limit = length - place * segment - home * rows
            for part in range(rows // LANES):
                biases.append(jnp.where(lane + part * LANES < limit, 0.0, MASKED).astype(F32))
        bias = jnp.concatenate(biases, axis=1)
        for m, buf in enumerate((kbuf, vbuf)):
            view = buf.at[n, pl.ds(0, segment)]
            pltpu.make_async_copy(view, view, sems.at[m, n]).wait()
        pltpu.make_async_copy(qbuf.at[n], qbuf.at[n], sems.at[2, n]).wait()

        def owner(i, carry):
            tops = jnp.zeros((tokens, LANES), F32)
            totals = jnp.zeros((tokens, LANES), F32)
            for j in range(kv_held):
                head = (place ^ i) * kv_held + j
                cols = pl.ds(pl.multiple_of(head * HD, HD), HD)
                base = j * shared * HD
                asked = jnp.concatenate(
                    [
                        qbuf[n, i, :, base + s * HD : base + (s + 1) * HD]
                        for s in range(shared)
                    ],
                    axis=0,
                )
                scores = lax.dot_general(
                    asked,
                    kbuf[n, :, cols],
                    (((1,), (1,)), ((), ())),
                    preferred_element_type=F32,
                )
                older = scores[:, :segment] * scale + bias
                newer = scores[:, segment:] * scale + new_bias
                top = jnp.maximum(
                    jnp.max(older, axis=1, keepdims=True),
                    jnp.max(newer, axis=1, keepdims=True),
                )
                top = jnp.maximum(top, FLOOR)
                older = jnp.exp2(older - top)
                newer = jnp.exp2(newer - top)
                total = jnp.sum(older, axis=1, keepdims=True) + jnp.sum(
                    newer, axis=1, keepdims=True
                )
                weights = jnp.concatenate([older.astype(BF16), newer.astype(BF16)], axis=1)
                summed = jnp.dot(
                    weights, vbuf[n, :, cols], preferred_element_type=F32
                ).astype(BF16)
                for s in range(shared):
                    part = slice(s * tokens, (s + 1) * tokens)
                    obuf[i, n, :, base + s * HD : base + (s + 1) * HD] = summed[part]
                    chosen = stat_lane == j * shared + s
                    tops = jnp.where(chosen, top[part], tops)
                    totals = jnp.where(chosen, total[part], totals)
            obuf[i, n, :, wide:] = pack_stats(tops, totals, kv_held * shared).astype(BF16)
            return carry

        return lax.fori_loop(0, width, owner, carry)

    lax.fori_loop(0, count, request, 0)
    copies = [pltpu.make_async_copy(obuf.at[i], outs[i], sems.at[3, i]) for i in range(width)]
    for copy in copies:
        copy.start()
    for copy in copies:
        copy.wait()


def split(value, parts):
    result = []
    for _ in range(parts):
        result.append(value.astype(BF16).astype(F32))
        value = value - result[-1]
    return result


def pack_stats(tops, totals, own):
    packed = jnp.zeros_like(tops)
    for n, part in enumerate(split(tops, 3) + split(totals, 2)):
        packed = packed + (pltpu.roll(part, n * own, 1) if n else part)
    return packed


def unpack_stats(packed, own):
    parts = [pltpu.roll(packed, LANES - n * own, 1) if n else packed for n in range(5)]
    return (parts[0] + parts[1]) + parts[2], parts[3] + parts[4]


def combined(pieces, n, heads):
    stats = [unpack_stats(piece[n, :, heads * HD :].astype(F32), heads) for piece in pieces]
    peak = functools.reduce(jnp.maximum, [top for top, _ in stats])
    factors = [jnp.exp2(top - peak) for top, _ in stats]
    denom = sum(total * factor for (_, total), factor in zip(stats, factors))
    shares = [factor / denom for factor in factors]
    for h in range(heads):
        cols = slice(h * HD, (h + 1) * HD)
        yield cols, sum(
            piece[n, :, cols].astype(F32) * share[:, h : h + 1]
            for piece, share in zip(pieces, shares)
        ).astype(BF16)


def combine_kernel(at, width, lots, halves, plan, *refs):
    out = refs[-1]
    own = out.shape[3] // HD
    for lot, (first, count, half) in enumerate(lots):
        pieces = refs[lot * width : (lot + 1) * width]
        heads = (pieces[0].shape[2] - LANES) // HD
        for n in range(count):
            slot = plan[at.slot + first + n]
            for cols, mixed in combined(pieces, n, heads):
                begin = half * heads * HD
                out[0, slot, :, begin + cols.start : begin + cols.stop] = mixed


def finish_kernel(at, width, position, half, plan, *refs):
    pieces, (out, buf, sem) = refs[:width], refs[-3:]
    heads = (pieces[0].shape[2] - LANES) // HD
    for cols, mixed in combined(pieces, 0, heads):
        buf[:, cols] = mixed
    view = out.at[0, plan[at.slot + position], :, pl.ds(half * heads * HD, heads * HD)]
    copy = pltpu.make_async_copy(buf, view, sem)
    copy.start()
    copy.wait()


def shards(
    query, cache_keys, cache_values, new_keys, new_values, masks, movers, block_lists, lengths
):
    groups = lax.axis_size("group")
    width = lax.axis_size("ctx")
    _, requests, segment, features = cache_keys.shape
    tokens = query.shape[2]
    matchings, _, nblocks = block_lists.shape
    own = query.shape[3] // HD
    shared = own * width * HD // features
    kv_own = own // shared
    halves = 2 if kv_own == 2 * HALF_HEADS else 1
    at = Layout(requests, nblocks, matchings)
    ready = [max(-1, n - (requests - matchings)) for n in range(requests)]
    request = jax.ShapeDtypeStruct((segment, features), BF16)
    part = jax.ShapeDtypeStruct((segment, features // halves), BF16)
    big = pltpu.CompilerParams(vmem_limit_bytes=40 * 1024 * 1024)
    request_bytes = 2 * segment * features * 2

    plan, *moving = pl.pallas_call(
        functools.partial(plan_kernel, at),
        out_shape=(jax.ShapeDtypeStruct((at.size,), jnp.int32), request, request),
        in_specs=[SMEM] * 4 + [ANY] * 2,
        out_specs=(SMEM, VMEM, VMEM),
        scratch_shapes=[pltpu.SemaphoreType.DMA((2,))],
        name="plan",
    )(masks, movers, block_lists, lengths, cache_keys, cache_values)

    def pick(step, sources):
        pieces = halves if step == matchings - 1 else 1
        return pl.pallas_call(
            functools.partial(pick_kernel, at, step),
            out_shape=[part if pieces > 1 else request] * (2 * pieces),
            in_specs=[SMEM] + [ANY] * (2 * step + 2),
            out_specs=[VMEM] * (2 * pieces),
            scratch_shapes=[pltpu.SemaphoreType.DMA((pieces, 2))],
            cost_estimate=pl.CostEstimate(
                flops=0, bytes_accessed=2 * request_bytes, transcendentals=0
            ),
            name=f"pick_{step}",
        )(plan, *sources[: 2 * step + 2])

    def attend(first, count, asked, fresh, sources, half=0, parts=1):
        newest = ready[first : first + count]
        sources = sources if parts > 1 else sources[: 2 * (max(newest) + 2)]
        heads = own // parts
        rows = heads * width * tokens * count
        return pl.pallas_call(
            functools.partial(
                attend_kernel, at, first, count, newest, half, parts, width, tokens
            ),
            out_shape=[jax.ShapeDtypeStruct((count, tokens, heads * HD + LANES), BF16)] * width,
            in_specs=[SMEM] + [ANY] * width + [VMEM] * 2 + [ANY] * len(sources),
            out_specs=[ANY] * width,
            scratch_shapes=[
                pltpu.VMEM((count, segment + LANES, features // parts), BF16),
                pltpu.VMEM((count, segment + LANES, features // parts), BF16),
                pltpu.VMEM((count, width, tokens, heads * HD), BF16),
                pltpu.VMEM((width, count, tokens, heads * HD + LANES), BF16),
                pltpu.SemaphoreType.DMA((4, max(width, count))),
            ],
            compiler_params=big,
            cost_estimate=pl.CostEstimate(
                flops=4 * rows * segment * HD,
                bytes_accessed=count * request_bytes // parts,
                transcendentals=rows * segment,
            ),
            name=f"attend_{first}_{count}_{half}",
        )(plan, *asked, *fresh, *sources)

    def send_home(results):
        return [results[0]] + [exchange(results[i], "ctx", i) for i in range(1, width)]

    def pad_new():
        extra = -new_keys.shape[2] % 16
        return [jnp.pad(new[0], ((0, 0), (0, extra), (0, 0))) for new in (new_keys, new_values)]

    asked = [query] + [exchange(query, "ctx", i) for i in range(1, width)]
    sources = [cache_keys, cache_values]
    lots, pieces = [], []
    fresh = None
    for step in range(matchings):
        final = step == matchings - 1
        if step:
            moving = pick(step, sources)
        if step == 1:
            first, count = 0, ready.index(0) + 1
        else:
            first, count = ready.index(max(step - 1, 0)), 1

        def branch(mask, moved, state):
            arrived = [exchange(block, "group", mask) for block in moved]
            if step == 0:
                return arrived, pad_new(), []
            asked, fresh, sources = state
            done = send_home(attend(first, count, asked, fresh, sources))
            early = []
            if final and halves > 1:
                early = send_home(
                    attend(requests - 1, 1, asked, fresh, arrived[:2], 0, halves)
                )
            return arrived, done, early

        arrived, done, early = lax.switch(
            masks[step] - 1,
            [functools.partial(branch, mask) for mask in range(1, groups)],
            moving,
            (asked, fresh, sources),
        )
        sources = sources + arrived
        if step == 0:
            fresh = done
        else:
            lots.append((first, count, 0))
            pieces += done
        if early:
            lots.append((requests - 1, 1, 0))
            pieces += early

    last = sources[-2:] if halves > 1 else sources
    late = send_home(attend(requests - 1, 1, asked, fresh, last, halves - 1, halves))

    keys_after, values_after = pl.pallas_call(
        functools.partial(settle_kernel, at, ready, halves),
        out_shape=[jax.ShapeDtypeStruct(cache_keys.shape, BF16)] * 2,
        in_specs=[SMEM] + [ANY] * len(sources),
        out_specs=[ANY, ANY],
        scratch_shapes=[
            pltpu.VMEM((requests, segment, features), BF16),
            pltpu.VMEM((requests, segment, features), BF16),
            pltpu.SemaphoreType.DMA((2, requests)),
        ],
        compiler_params=big,
        cost_estimate=pl.CostEstimate(
            flops=0, bytes_accessed=2 * requests * request_bytes, transcendentals=0
        ),
        name="settle",
    )(plan, *sources)

    attended = pl.pallas_call(
        functools.partial(combine_kernel, at, width, lots, halves),
        out_shape=jax.ShapeDtypeStruct(query.shape, BF16),
        in_specs=[SMEM] + [VMEM] * len(pieces),
        out_specs=VMEM,
        compiler_params=big,
        cost_estimate=pl.CostEstimate(
            flops=0, bytes_accessed=(width + 1) * requests * tokens * own * HD * 2, transcendentals=0
        ),
        name="combine",
    )(plan, *pieces)
    heads = own // halves
    attended = pl.pallas_call(
        functools.partial(finish_kernel, at, width, requests - 1, halves - 1),
        out_shape=jax.ShapeDtypeStruct(query.shape, BF16),
        in_specs=[SMEM] + [VMEM] * width + [ANY],
        out_specs=ANY,
        scratch_shapes=[pltpu.VMEM((tokens, heads * HD), BF16), pltpu.SemaphoreType.DMA],
        input_output_aliases={width + 1: 0},
        compiler_params=big,
        name="finish",
    )(plan, *late, attended)
    return attended, keys_after, values_after


def solution(mesh):
    placed = (
        P("group", None, None, "ctx"),
        P("group", None, "ctx", None),
        P("group", None, "ctx", None),
        P("group", None, "ctx", None),
        P("group", None, "ctx", None),
        P(),
        P(),
        P(),
        P(),
    )
    return jax.shard_map(
        shards,
        mesh=mesh,
        in_specs=placed,
        out_specs=(
            P("group", None, None, "ctx"),
            P("group", None, "ctx", None),
            P("group", None, "ctx", None),
        ),
        check_vma=False,
    )
```

```python
import functools
import math

import jax
import jax.numpy as jnp
from jax import lax
from jax.experimental import pallas as pl
from jax.experimental.pallas import tpu as pltpu
from jax.sharding import PartitionSpec as P

HD = 128
LANES = 128
MASKED = -1e30
FLOOR = -1e29
BF16 = jnp.bfloat16
F32 = jnp.float32
ANY = pl.BlockSpec(memory_space=pl.ANY)
SMEM = pl.BlockSpec(memory_space=pltpu.SMEM)
VMEM = pl.BlockSpec(memory_space=pltpu.VMEM)


def exchange(block, axis, mask):
    return lax.ppermute(block, axis, [(i, i ^ mask) for i in range(lax.axis_size(axis))])


class Layout:
    def __init__(self, requests, nblocks, matchings):
        self.nblocks = nblocks
        self.slot = 0
        self.last = requests
        self.count = 2 * requests
        self.perm = 3 * requests
        self.home = self.perm + requests * nblocks
        self.mover = self.home + requests * nblocks
        self.source = self.mover + matchings
        self.place = self.source + matchings
        self.size = self.place + 1


def plan_kernel(
    at, masks, movers, lists, lengths, keys, values, plan, key_out, value_out, sems
):
    matchings, nblocks, _ = lists.shape
    requests = lengths.shape[0]
    here = lax.axis_index("group")
    first = movers[0, here]
    copies = [
        pltpu.make_async_copy(keys.at[0, first], key_out, sems.at[0]),
        pltpu.make_async_copy(values.at[0, first], value_out, sems.at[1]),
    ]
    for copy in copies:
        copy.start()
    plan[at.place] = lax.axis_index("ctx")
    traced = []
    for slot in range(requests):
        group, where = here, jnp.int32(slot)
        last = jnp.int32(-1)
        blocks = [jnp.int32(b) for b in range(nblocks)]
        for step in reversed(range(matchings)):
            hit = movers[step, group] == where
            partner = group ^ masks[step]
            last = jnp.where(jnp.logical_and(hit, last < 0), step, last)
            moved = []
            for block in blocks:
                origin = block
                for j in range(nblocks):
                    origin = jnp.where(
                        lists[step, j, group] == block, lists[step, j, partner], origin
                    )
                moved.append(jnp.where(hit, origin, block))
            blocks = moved
            where = jnp.where(hit, movers[step, partner], where)
            group = jnp.where(hit, partner, group)
        traced.append((last, lengths[where, group], blocks))
    for slot in range(requests):
        last, count, blocks = traced[slot]
        rank = jnp.int32(0)
        for other in range(requests):
            if other != slot:
                ahead = traced[other][0] * requests + other < last * requests + slot
                rank = rank + ahead.astype(jnp.int32)
        plan[at.slot + rank] = jnp.int32(slot)
        plan[at.last + rank] = last
        plan[at.count + rank] = count
        for b in range(nblocks):
            plan[at.perm + rank * nblocks + b] = blocks[b]
            plan[at.home + rank * nblocks + blocks[b]] = jnp.int32(b)
    for step in range(matchings):
        mover = movers[step, here]
        source = jnp.int32(-1)
        for earlier in range(step):
            source = jnp.where(movers[earlier, here] == mover, earlier, source)
        plan[at.mover + step] = mover
        plan[at.source + step] = source
    for copy in copies:
        copy.wait()


def pick_kernel(at, step, choices, plan, *refs):
    sources, outs, sems = refs[: 2 * step + 2], refs[-1 - len(choices) : -1], refs[-1]
    mover, source, place = plan[at.mover + step], plan[at.source + step], plan[at.place]
    for code in range(-1, step):

        @pl.when(source == code)
        def _():
            for c, (out, (kinds, pieces)) in enumerate(zip(outs, choices)):
                for m, kind in enumerate(kinds):
                    view = sources[2 * code + 2 + kind]
                    view = view.at[0, mover] if code < 0 else view
                    if pieces is None:
                        pltpu.make_async_copy(view, out, sems.at[c]).start()
                        continue
                    wide = out.shape[2] // len(pieces)
                    for p, piece in enumerate(pieces):
                        begin = pl.multiple_of((place ^ piece) * wide, wide)
                        pltpu.make_async_copy(
                            view.at[:, pl.ds(begin, wide)],
                            out.at[m, :, pl.ds(p * wide, wide)],
                            sems.at[c],
                        ).start()

    for c, out in enumerate(outs):
        pltpu.make_async_copy(out, out, sems.at[c]).wait()


def stage(at, plan, position, newest, sources, bufs, sems):
    rows = bufs[0].shape[0] // at.nblocks
    slot, last = plan[at.slot + position], plan[at.last + position]
    for code in range(-1, newest + 1):

        @pl.when(last == code)
        def _():
            views = sources[2 * code + 2 : 2 * code + 4]
            views = [view.at[0, slot] if code < 0 else view for view in views]

            def block(b, carry):
                begin = pl.multiple_of(plan[at.perm + position * at.nblocks + b] * rows, rows)
                into = pl.ds(pl.multiple_of(b * rows, rows), rows)
                for n in range(2):
                    pltpu.make_async_copy(
                        views[n].at[pl.ds(begin, rows)], bufs[n].at[into], sems[n]
                    ).start()
                return carry

            lax.fori_loop(0, at.nblocks, block, 0)


def settle_kernel(at, ready, plan, *refs):
    sources, outs, buf, sems = refs[:-4], refs[-4:-2], refs[-2], refs[-1]
    for position, newest in enumerate(ready):
        bufs = [buf.at[n, position] for n in range(2)]
        stage(at, plan, position, newest, sources, bufs, [sems.at[n, position] for n in range(2)])
    for position in range(len(ready)):
        slot = plan[at.slot + position]
        for n in range(2):
            view, sem = buf.at[n, position], sems.at[n, position]
            pltpu.make_async_copy(view, view, sem).wait()
            pltpu.make_async_copy(view, outs[n].at[0, slot], sem).start()
    for position in range(len(ready)):
        slot = plan[at.slot + position]
        for n in range(2):
            view, sem = buf.at[n, position], sems.at[n, position]
            pltpu.make_async_copy(view, outs[n].at[0, slot], sem).wait()


class Heads:
    def __init__(self, width, tokens, own, features, segment):
        self.width = width
        self.tokens = tokens
        self.own = own
        self.shared = own * width * HD // features
        self.kv_own = own // self.shared
        self.wide = self.kv_own * HD
        self.segment = segment


def place_new(new, slot, buf, spans):
    segment, rows = buf.shape[0] - LANES, new.shape[1]
    buf[segment:, :] = jnp.zeros((LANES, buf.shape[1]), BF16)
    for cols, origin in spans:
        buf[segment : segment + rows, cols] = new[slot, :, origin]


def new_bias_of(size, place):
    fresh = size.tokens // size.width
    queries = size.shared * size.tokens
    token = lax.broadcasted_iota(jnp.int32, (queries, LANES), 0) % size.tokens
    column = lax.broadcasted_iota(jnp.int32, (queries, LANES), 1)
    allowed = jnp.logical_and(column < fresh, column + place * fresh <= token)
    return jnp.where(allowed, 0.0, MASKED).astype(F32)


def bias_of(at, size, plan, position, place):
    lane = lax.broadcasted_iota(jnp.int32, (1, LANES), 1)
    length = plan[at.count + position]
    rows = size.segment // at.nblocks
    biases = []
    for b in range(at.nblocks):
        home = plan[at.home + position * at.nblocks + b]
        limit = length - place * size.segment - home * rows
        for part in range(rows // LANES):
            biases.append(jnp.where(lane + part * LANES < limit, 0.0, MASKED).astype(F32))
    return jnp.concatenate(biases, axis=1)


def attend_owner(size, asked, keys, values, column, bias, new_bias, out, unroll=False):
    tokens, shared, segment = size.tokens, size.shared, size.segment
    scale = math.log2(math.e) / HD**0.5
    stat_lane = lax.broadcasted_iota(jnp.int32, (tokens, LANES), 1)

    def head(j, stats):
        tops, totals = stats
        cols = pl.ds(pl.multiple_of(column + j * HD, HD), HD)
        spans = [
            pl.ds(pl.multiple_of((j * shared + s) * HD, HD), HD) for s in range(shared)
        ]
        scores = lax.dot_general(
            jnp.concatenate([asked[:, span] for span in spans], axis=0),
            keys[:, cols],
            (((1,), (1,)), ((), ())),
            preferred_element_type=F32,
        )
        older = scores[:, :segment] * scale + bias
        newer = scores[:, segment:] * scale + new_bias
        top = jnp.maximum(
            jnp.max(older, axis=1, keepdims=True), jnp.max(newer, axis=1, keepdims=True)
        )
        top = jnp.maximum(top, FLOOR)
        older = jnp.exp2(older - top)
        newer = jnp.exp2(newer - top)
        total = jnp.sum(older, axis=1, keepdims=True) + jnp.sum(newer, axis=1, keepdims=True)
        weights = jnp.concatenate([older.astype(BF16), newer.astype(BF16)], axis=1)
        summed = jnp.dot(weights, values[:, cols], preferred_element_type=F32).astype(BF16)
        for s, span in enumerate(spans):
            part = slice(s * tokens, (s + 1) * tokens)
            out[:, span] = summed[part]
            chosen = stat_lane == j * shared + s
            tops = jnp.where(chosen, top[part], tops)
            totals = jnp.where(chosen, total[part], totals)
        return tops, totals

    stats = (jnp.zeros((tokens, LANES), F32), jnp.zeros((tokens, LANES), F32))
    stats = lax.fori_loop(0, size.kv_own, head, stats, unroll=unroll)
    out[:, size.own * HD :] = pack_stats(*stats, size.own).astype(BF16)


def attend_kernel(at, size, first, newest, pieces, kinds, plan, *refs):
    count, some = len(newest), len(pieces)
    q_refs, (new_k, new_v), refs = refs[:some], refs[some : some + 2], refs[some + 2 :]
    outs, (kbuf, vbuf, qbuf, obuf, sems) = refs[-5 - some : -5], refs[-5:]
    sources = refs[: -5 - some]
    partial = kinds is not None
    place = plan[at.place]

    def start(view, buf, sem):
        pltpu.make_async_copy(view, buf.at[pl.ds(0, size.segment)], sem).start()

    for n in range(count):
        slot, last = plan[at.slot + first + n], plan[at.last + first + n]
        bufs = (kbuf.at[n], vbuf.at[n])
        if partial:
            for held, ref in zip(kinds, sources):
                for m, kind in enumerate(held):
                    start(ref.at[m], bufs[kind], sems.at[kind, n])
        else:
            for code in range(-1, newest[n] + 1):

                @pl.when(last == code)
                def _():
                    for m in range(2):
                        view = sources[2 * code + 2 + m]
                        start(view.at[0, slot] if code < 0 else view, bufs[m], sems.at[m, n])

        for p in range(some):
            pltpu.make_async_copy(q_refs[p].at[0, slot], qbuf.at[n, p], sems.at[2, n]).start()

    for n in range(count):
        slot = plan[at.slot + first + n]
        spans = [(slice(None), slice(None))]
        if partial:
            spans = [own_columns(size, place, p, piece) for p, piece in enumerate(pieces)]
        place_new(new_k, slot, kbuf.at[n], spans)
        place_new(new_v, slot, vbuf.at[n], spans)

    new_bias = new_bias_of(size, place)

    def request(n, carry):
        bias = bias_of(at, size, plan, first + n, place)
        for m, buf in enumerate((kbuf, vbuf)):
            view = buf.at[n, pl.ds(0, size.segment)]
            pltpu.make_async_copy(view, view, sems.at[m, n]).wait()
        pltpu.make_async_copy(qbuf.at[n], qbuf.at[n], sems.at[2, n]).wait()

        def owner(p, carry):
            column = p * size.wide if partial else (place ^ (p + pieces[0])) * size.wide
            attend_owner(
                size,
                qbuf.at[n, p],
                kbuf.at[n],
                vbuf.at[n],
                column,
                bias,
                new_bias,
                obuf.at[p, n],
            )
            return carry

        return lax.fori_loop(0, some, owner, carry)

    lax.fori_loop(0, count, request, 0)
    copies = [pltpu.make_async_copy(obuf.at[p], outs[p], sems.at[3, p]) for p in range(some)]
    for copy in copies:
        copy.start()
    for copy in copies:
        copy.wait()


def own_columns(size, place, p, piece):
    begin = pl.multiple_of((place ^ piece) * size.wide, size.wide)
    return pl.ds(p * size.wide, size.wide), pl.ds(begin, size.wide)


def split(value, parts):
    result = []
    for _ in range(parts):
        result.append(value.astype(BF16).astype(F32))
        value = value - result[-1]
    return result


def pack_stats(tops, totals, own):
    packed = jnp.zeros_like(tops)
    for n, part in enumerate(split(tops, 3) + split(totals, 2)):
        packed = packed + (pltpu.roll(part, n * own, 1) if n else part)
    return packed


def unpack_stats(packed, own):
    parts = [pltpu.roll(packed, LANES - n * own, 1) if n else packed for n in range(5)]
    return (parts[0] + parts[1]) + parts[2], parts[3] + parts[4]


def combined(pieces, heads, out):
    stats = [unpack_stats(piece[:, heads * HD :].astype(F32), heads) for piece in pieces]
    peak = functools.reduce(jnp.maximum, [top for top, _ in stats])
    factors = [jnp.exp2(top - peak) for top, _ in stats]
    denom = sum(total * factor for (_, total), factor in zip(stats, factors))
    shares = [factor / denom for factor in factors]
    for h in range(heads):
        cols = slice(h * HD, (h + 1) * HD)
        out[:, cols] = sum(
            piece[:, cols].astype(F32) * share[:, h : h + 1] for piece, share in zip(pieces, shares)
        ).astype(BF16)


def finish_kernel(at, size, parcels, lots, settled, ready, plan, *refs):
    count = sum(lots)
    some = len(parcels)
    arrived, refs = refs[:some], refs[some:]
    sources, refs = refs[: 2 * len(parcels_before(ready))], refs[2 * len(parcels_before(ready)) :]
    query, new_k, new_v = refs[:3]
    pieces, refs = refs[3:-13], refs[-11:]
    attended, after = refs[0], refs[1:3]
    kbuf, vbuf, qbuf, pbuf, full, sems, out_sems, in_sems = refs[3:]
    place, slot = plan[at.place], plan[at.slot + count]
    copies = [
        pltpu.make_async_copy(view, buf.at[pl.ds(0, size.segment)], in_sems.at[m])
        for m, (view, buf) in enumerate(zip(own_parcel(parcels, arrived), (kbuf, vbuf)))
    ]
    copies.append(pltpu.make_async_copy(query.at[0, slot], qbuf, in_sems.at[2]))
    for copy in copies:
        copy.start()
    before = 0
    for lot, each in enumerate([*lots, 1]):
        for i in range(size.width):
            if lot < len(lots) or i:
                piece = pieces[lot * size.width + i - lot // len(lots)]
                into = pbuf.at[i, pl.ds(before, each)]
                pltpu.make_async_copy(piece, into, in_sems.at[3]).start()
        before += each
    for position in range(settled, count):
        bufs = [full.at[n, position - settled] for n in range(2)]
        marks = [sems.at[n, position - settled] for n in range(2)]
        stage(at, plan, position, ready[position], sources, bufs, marks)
    rows = size.segment // at.nblocks

    def block(b, carry):
        begin = pl.multiple_of(plan[at.perm + count * at.nblocks + b] * rows, rows)
        into = pl.ds(pl.multiple_of(b * rows, rows), rows)
        for (kinds, parcel), ref in zip(parcels, arrived):
            for m, n in enumerate(kinds):
                for p, piece in enumerate(parcel):
                    cols, whole = own_columns(size, place, p, piece)
                    pltpu.make_async_copy(
                        ref.at[m, pl.ds(begin, rows), cols],
                        full.at[n, count - settled, into, whole],
                        sems.at[n, count - settled],
                    ).start()
        return carry

    lax.fori_loop(0, at.nblocks, block, 0)
    spans = [own_columns(size, place, 0, 0)]
    place_new(new_k, slot, kbuf, spans)
    place_new(new_v, slot, vbuf, spans)
    bias = bias_of(at, size, plan, count, place)
    new_bias = new_bias_of(size, place)
    for copy in copies:
        copy.wait()
    attend_owner(size, qbuf, kbuf, vbuf, 0, bias, new_bias, pbuf.at[0, count], True)
    for position in range(settled, count + 1):
        there = plan[at.slot + position]
        for n in range(2):
            view, sem = full.at[n, position - settled], sems.at[n, position - settled]
            pltpu.make_async_copy(view, view, sem).wait()
            pltpu.make_async_copy(
                view, after[n].at[0, there], out_sems.at[n, position - settled]
            ).start()
    theirs = (pbuf.at[0, pl.ds(0, count)], pbuf.at[pl.ds(1, size.width - 1)])
    for view in theirs:
        pltpu.make_async_copy(view, view, in_sems.at[3]).wait()

    def request(n, carry):
        parts = [pbuf.at[i, n] for i in range(size.width)]
        combined(parts, size.own, attended.at[0, plan[at.slot + n]])
        return carry

    lax.fori_loop(0, count + 1, request, 0)
    for position in range(settled, count + 1):
        there = plan[at.slot + position]
        for n in range(2):
            view = full.at[n, position - settled]
            pltpu.make_async_copy(
                view, after[n].at[0, there], out_sems.at[n, position - settled]
            ).wait()


def parcels_before(ready):
    return range(-1, max(ready))


def own_parcel(parcels, arrived):
    for n in range(2):
        for (kinds, parcel), ref in zip(parcels, arrived):
            if parcel == (0,) and n in kinds:
                yield ref.at[kinds.index(n)]


def shards(
    query, cache_keys, cache_values, new_keys, new_values, masks, movers, block_lists, lengths
):
    groups = lax.axis_size("group")
    width = lax.axis_size("ctx")
    _, requests, segment, features = cache_keys.shape
    tokens = query.shape[2]
    matchings, _, nblocks = block_lists.shape
    own = query.shape[3] // HD
    size = Heads(width, tokens, own, features, segment)
    at = Layout(requests, nblocks, matchings)
    ready = [max(-1, n - (requests - matchings)) for n in range(requests)]
    caches = (cache_keys, cache_values)
    big = pltpu.CompilerParams(vmem_limit_bytes=40 * 1024 * 1024)
    result = jax.ShapeDtypeStruct((tokens, own * HD + LANES), BF16)
    everyone = tuple(range(width))
    far, near = everyone[(width + 1) // 2 :], everyone[1 : (width + 1) // 2]
    parcels = [((0,), far), ((1,), far), ((0, 1), near), ((0, 1), (0,))]

    request = jax.ShapeDtypeStruct((segment, features), BF16)
    plan, *moving = pl.pallas_call(
        functools.partial(plan_kernel, at),
        out_shape=(jax.ShapeDtypeStruct((at.size,), jnp.int32), request, request),
        in_specs=[SMEM] * 4 + [ANY] * 2,
        out_specs=(SMEM, VMEM, VMEM),
        scratch_shapes=[pltpu.SemaphoreType.DMA((2,))],
        name="plan",
    )(masks, movers, block_lists.transpose(0, 2, 1), lengths.T, *caches)

    def lasting(microseconds):
        return pl.CostEstimate(
            flops=0, bytes_accessed=int(microseconds * 3.7e6), transcendentals=0
        )

    def pick(step, choices, sources, after=()):
        shapes = [
            (len(kinds), segment, len(pieces) * size.wide) if pieces else (segment, features)
            for kinds, pieces in choices
        ]
        wanted = {kind for kinds, _ in choices for kind in kinds}
        used = [
            sources[2 * n + (kind if kind in wanted else 1 - kind)]
            for n in range(step + 1)
            for kind in range(2)
        ]
        return pl.pallas_call(
            functools.partial(pick_kernel, at, step, choices),
            out_shape=[jax.ShapeDtypeStruct(shape, BF16) for shape in shapes],
            in_specs=[SMEM] + [ANY] * (len(used) + len(after)),
            out_specs=[VMEM] * len(choices),
            scratch_shapes=[pltpu.SemaphoreType.DMA((len(choices),))],
            cost_estimate=lasting(2.5),
            name=f"pick_{step}",
        )(plan, *used, *after)

    def attend(first, count, pieces, asked, fresh, sources, kinds=None, after=()):
        newest = ready[first : first + count]
        if kinds is None:
            sources = sources[: 2 * (max(newest) + 2)]
        held = sources[0].shape[-1]
        some = len(pieces)
        return pl.pallas_call(
            functools.partial(attend_kernel, at, size, first, newest, pieces, kinds),
            out_shape=[jax.ShapeDtypeStruct((count, *result.shape), BF16)] * some,
            in_specs=[SMEM] + [ANY] * some + [VMEM] * 2 + [ANY] * (len(sources) + len(after)),
            out_specs=[ANY] * some,
            scratch_shapes=[
                pltpu.VMEM((count, segment + LANES, held), BF16),
                pltpu.VMEM((count, segment + LANES, held), BF16),
                pltpu.VMEM((count, some, tokens, own * HD), BF16),
                pltpu.VMEM((some, count, *result.shape), BF16),
                pltpu.SemaphoreType.DMA((4, max(some, count))),
            ],
            compiler_params=big,
            cost_estimate=lasting(1 + 1.5 * some * count),
            name=f"attend_{first}_{count}_{some}",
        )(plan, *[asked[piece] for piece in pieces], *fresh, *sources, *after)

    def send_home(pieces, results):
        return [exchange(part, "ctx", piece) if piece else part for piece, part in zip(pieces, results)]

    def settle(positions, sources):
        count = len(positions)
        newest = [ready[n] for n in positions]
        used = sources[: 2 * (max(newest) + 2)]
        return pl.pallas_call(
            functools.partial(settle_kernel, at, newest),
            out_shape=[jax.ShapeDtypeStruct(cache_keys.shape, BF16)] * 2,
            in_specs=[SMEM] + [ANY] * len(used),
            out_specs=[ANY] * 2,
            scratch_shapes=[
                pltpu.VMEM((2, count, segment, features), BF16),
                pltpu.SemaphoreType.DMA((2, count)),
            ],
            compiler_params=big,
            cost_estimate=lasting(2 * count),
            name="settle",
        )(plan, *used)

    def pad_new():
        extra = -new_keys.shape[2] % 16
        return [jnp.pad(new[0], ((0, 0), (0, extra), (0, 0))) for new in (new_keys, new_values)]

    def choices(step):
        return parcels if step == matchings - 1 else [((0,), None), ((1,), None)]

    def prepare(step, sources):
        return pick(step, choices(step)[:1], sources)[0]

    def first_branch(mask):
        arrived = [exchange(block, "group", mask) for block in moving]
        asked = [query] + [exchange(query, "ctx", piece) for piece in everyone[1:]]
        return arrived, prepare(1, [*caches, *arrived]), asked, pad_new()

    def middle_branch(step, positions, prepared, asked, fresh, sources, mask):
        moving = [prepared, *pick(step, choices(step)[1:], sources)]
        arrived = [exchange(block, "group", mask) for block in moving]
        done = send_home(
            everyone, attend(positions[0], len(positions), everyone, asked, fresh, sources)
        )
        after = settle(positions, sources) if step == 1 else []
        return arrived, prepare(step + 1, sources + arrived), done, after

    def last_branch(step, first, prepared, asked, fresh, sources, mask):
        second = pick(step, parcels[1:2], sources)
        moving = [prepared, *second, *pick(step, parcels[2:], sources, second)]
        arrived = [exchange(block, "group", mask) for block in moving]
        done = send_home(everyone, attend(first, 1, everyone, asked, fresh, sources))
        most = attend(
            requests - 1, 1, far, asked, fresh, arrived[:2], [(0,), (1,)], done[:1]
        )
        parts = dict(zip(far, send_home(far, most)))
        if near:
            rest = attend(
                requests - 1, 1, near, asked, fresh, arrived[2:3], [(0, 1)], most[:1]
            )
            parts.update(zip(near, send_home(near, rest)))
        return arrived, done, [parts[piece] for piece in everyone[1:]]

    indices = masks - 1

    def switch(step, branch, *given):
        return lax.switch(
            indices[step],
            [functools.partial(branch, *given, mask) for mask in range(1, groups)],
        )

    arrived, prepared, asked, fresh = switch(0, first_branch)
    sources = [*caches, *arrived]
    lots, done, after = [], [], None
    for step in range(1, matchings - 1):
        first = sum(lots)
        positions = range(first, ready.index(step - 1) + 1)
        arrived, prepared, part, settled = switch(
            step, middle_branch, step, positions, prepared, asked, fresh, sources
        )
        after = after or settled
        sources = sources + arrived
        lots.append(len(positions))
        done += part
    arrived, part, pieces = switch(
        matchings - 1, last_branch, matchings - 1, sum(lots), prepared, asked, fresh, sources
    )
    lots.append(1)
    pieces = [*done, *part, *pieces]
    ahead = 1 + len(arrived) + len(sources) + 3 + len(pieces)
    left = requests - lots[0]
    return pl.pallas_call(
        functools.partial(finish_kernel, at, size, parcels, lots, lots[0], ready),
        out_shape=[
            jax.ShapeDtypeStruct(array.shape, BF16) for array in (query, cache_keys, cache_values)
        ],
        in_specs=[SMEM]
        + [ANY] * (len(arrived) + len(sources) + 1)
        + [VMEM] * 2
        + [ANY] * (len(pieces) + 2),
        out_specs=[VMEM, ANY, ANY],
        scratch_shapes=[
            pltpu.VMEM((segment + LANES, size.wide), BF16),
            pltpu.VMEM((segment + LANES, size.wide), BF16),
            pltpu.VMEM((tokens, own * HD), BF16),
            pltpu.VMEM((width, requests, *result.shape), BF16),
            pltpu.VMEM((2, left, segment, features), BF16),
            pltpu.SemaphoreType.DMA((2, left)),
            pltpu.SemaphoreType.DMA((2, left)),
            pltpu.SemaphoreType.DMA((4,)),
        ],
        input_output_aliases={ahead: 1, ahead + 1: 2},
        compiler_params=big,
        name="finish",
    )(plan, *arrived, *sources, query, *fresh, *pieces, *after)


def solution(mesh):
    placed = (
        P("group", None, None, "ctx"),
        P("group", None, "ctx", None),
        P("group", None, "ctx", None),
        P("group", None, "ctx", None),
        P("group", None, "ctx", None),
        P(),
        P(),
        P(),
        P(),
    )
    return jax.shard_map(
        shards,
        mesh=mesh,
        in_specs=placed,
        out_specs=(
            P("group", None, None, "ctx"),
            P("group", None, "ctx", None),
            P("group", None, "ctx", None),
        ),
        check_vma=False,
    )
```

```python
import functools
import math

import jax
import jax.numpy as jnp
from jax import lax
from jax.experimental import pallas as pl
from jax.experimental.pallas import tpu as pltpu
from jax.sharding import PartitionSpec as P

HD = 128
LANES = 128
MASKED = -1e30
FLOOR = -1e29
BF16 = jnp.bfloat16
F32 = jnp.float32
ANY = pl.BlockSpec(memory_space=pl.ANY)
SMEM = pl.BlockSpec(memory_space=pltpu.SMEM)
VMEM = pl.BlockSpec(memory_space=pltpu.VMEM)


def exchange(block, axis, mask):
    return lax.ppermute(block, axis, [(i, i ^ mask) for i in range(lax.axis_size(axis))])


class Layout:
    def __init__(self, requests, nblocks, matchings):
        self.nblocks = nblocks
        self.slot = 0
        self.last = requests
        self.count = 2 * requests
        self.perm = 3 * requests
        self.home = self.perm + requests * nblocks
        self.mover = self.home + requests * nblocks
        self.source = self.mover + matchings
        self.place = self.source + matchings
        self.size = self.place + 1


def copy_pieces(views, out, sem, place, first):
    wide = views[0].shape[1] // lax.axis_size("ctx")

    def piece(p, carry):
        begin = pl.multiple_of((place ^ (first + p)) * wide, wide)
        into = pl.ds(pl.multiple_of(p * wide, wide), wide)
        for m, view in enumerate(views):
            pltpu.make_async_copy(view.at[:, pl.ds(begin, wide)], out.at[m, :, into], sem).start()
        return carry

    lax.fori_loop(0, out.shape[2] // wide, piece, 0)


def place_pieces(parcel, bufs, sems, place, first, rows=None, into=None):
    rows = pl.ds(0, parcel.shape[1]) if rows is None else rows
    into = rows if into is None else into
    wide = bufs[0].shape[1] // lax.axis_size("ctx")

    def piece(p, carry):
        begin = pl.multiple_of((place ^ (first + p)) * wide, wide)
        origin = pl.ds(pl.multiple_of(p * wide, wide), wide)
        for m, buf in enumerate(bufs):
            pltpu.make_async_copy(
                parcel.at[m, rows, origin], buf.at[into, pl.ds(begin, wide)], sems[m]
            ).start()
        return carry

    lax.fori_loop(0, parcel.shape[2] // wide, piece, 0)


def plan_kernel(
    at, parcels, masks, movers, lists, lengths, keys, values, plan, *refs
):
    some = len(parcels)
    indices, outs, sems = refs[: -1 - some], refs[-1 - some : -1], refs[-1]
    matchings, nblocks, _ = lists.shape
    requests = lengths.shape[0]
    here = lax.axis_index("group")
    place = lax.axis_index("ctx")
    views = [keys.at[0, movers[0, here]], values.at[0, movers[0, here]]]
    for c, (out, pieces) in enumerate(zip(outs, parcels)):
        copy_pieces(views, out, sems.at[c], place, pieces[0])
    for step, index in enumerate(indices):
        index[0] = masks[step] - 1
    plan[at.place] = place
    traced = []
    for slot in range(requests):
        group, where = here, jnp.int32(slot)
        last = jnp.int32(-1)
        blocks = [jnp.int32(b) for b in range(nblocks)]
        for step in reversed(range(matchings)):
            hit = movers[step, group] == where
            partner = group ^ masks[step]
            last = jnp.where(jnp.logical_and(hit, last < 0), step, last)
            moved = []
            for block in blocks:
                origin = block
                for j in range(nblocks):
                    origin = jnp.where(
                        lists[step, j, group] == block, lists[step, j, partner], origin
                    )
                moved.append(jnp.where(hit, origin, block))
            blocks = moved
            where = jnp.where(hit, movers[step, partner], where)
            group = jnp.where(hit, partner, group)
        traced.append((last, lengths[where, group], blocks))
    for slot in range(requests):
        last, count, blocks = traced[slot]
        rank = jnp.int32(0)
        for other in range(requests):
            if other != slot:
                ahead = traced[other][0] * requests + other < last * requests + slot
                rank = rank + ahead.astype(jnp.int32)
        plan[at.slot + rank] = jnp.int32(slot)
        plan[at.last + rank] = last
        plan[at.count + rank] = count
        for b in range(nblocks):
            plan[at.perm + rank * nblocks + b] = blocks[b]
            plan[at.home + rank * nblocks + blocks[b]] = jnp.int32(b)
    for step in range(matchings):
        mover = movers[step, here]
        source = jnp.int32(-1)
        for earlier in range(step):
            source = jnp.where(movers[earlier, here] == mover, earlier, source)
        plan[at.mover + step] = mover
        plan[at.source + step] = source
    for c, out in enumerate(outs):
        pltpu.make_async_copy(out, out, sems.at[c]).wait()


def pick_kernel(at, step, choices, plan, *refs):
    sources, outs, sems = refs[: 2 * step + 2], refs[-1 - len(choices) : -1], refs[-1]
    mover, source, place = plan[at.mover + step], plan[at.source + step], plan[at.place]
    half = lax.axis_size("ctx") // 2
    for code in range(-1, step):
        pair = sources[2 * code + 2 : 2 * code + 4]

        @pl.when(source == code)
        def _():
            for c, (out, pieces) in enumerate(zip(outs, choices)):
                if code < 0:
                    views = [view.at[0, mover] for view in pair]
                    copy_pieces(views, out, sems.at[c], place, pieces[0])
                else:
                    far = pieces[0] >= half
                    begin = (pieces[0] - half * far) * (out.shape[2] // len(pieces))
                    view = pair[0 if far else 1].at[:, :, pl.ds(begin, out.shape[2])]
                    pltpu.make_async_copy(view, out, sems.at[c]).start()

    for c, out in enumerate(outs):
        pltpu.make_async_copy(out, out, sems.at[c]).wait()


def stage(at, plan, position, newest, sources, bufs, sems):
    rows = bufs[0].shape[0] // at.nblocks
    slot, last, place = plan[at.slot + position], plan[at.last + position], plan[at.place]
    half = lax.axis_size("ctx") // 2
    for code in range(-1, newest + 1):

        @pl.when(last == code)
        def _():
            pair = sources[2 * code + 2 : 2 * code + 4]

            def block(b, carry):
                begin = pl.multiple_of(plan[at.perm + position * at.nblocks + b] * rows, rows)
                into = pl.ds(pl.multiple_of(b * rows, rows), rows)
                if code < 0:
                    for n in range(2):
                        pltpu.make_async_copy(
                            pair[n].at[0, slot, pl.ds(begin, rows)], bufs[n].at[into], sems[n]
                        ).start()
                else:
                    for parcel, first in zip(pair, (half, 0)):
                        place_pieces(parcel, bufs, sems, place, first, pl.ds(begin, rows), into)
                return carry

            lax.fori_loop(0, at.nblocks, block, 0)


def settle_kernel(at, ready, plan, *refs):
    sources, outs, buf, sems = refs[:-4], refs[-4:-2], refs[-2], refs[-1]
    for position, newest in enumerate(ready):
        bufs = [buf.at[n, position] for n in range(2)]
        stage(at, plan, position, newest, sources, bufs, [sems.at[n, position] for n in range(2)])
    for position in range(len(ready)):
        slot = plan[at.slot + position]
        for n in range(2):
            view, sem = buf.at[n, position], sems.at[n, position]
            pltpu.make_async_copy(view, view, sem).wait()
            pltpu.make_async_copy(view, outs[n].at[0, slot], sem).start()
    for position in range(len(ready)):
        slot = plan[at.slot + position]
        for n in range(2):
            view, sem = buf.at[n, position], sems.at[n, position]
            pltpu.make_async_copy(view, outs[n].at[0, slot], sem).wait()


class Heads:
    def __init__(self, width, tokens, own, features, segment):
        self.width = width
        self.tokens = tokens
        self.own = own
        self.shared = own * width * HD // features
        self.kv_own = own // self.shared
        self.wide = self.kv_own * HD
        self.segment = segment


def place_new(new, slot, buf, spans):
    segment, rows = buf.shape[0] - LANES, new.shape[1]
    buf[segment:, :] = jnp.zeros((LANES, buf.shape[1]), BF16)
    for cols, origin in spans:
        buf[segment : segment + rows, cols] = new[slot, :, origin]


def new_bias_of(size, place):
    fresh = size.tokens // size.width
    queries = size.shared * size.tokens
    token = lax.broadcasted_iota(jnp.int32, (queries, LANES), 0) % size.tokens
    column = lax.broadcasted_iota(jnp.int32, (queries, LANES), 1)
    allowed = jnp.logical_and(column < fresh, column + place * fresh <= token)
    return jnp.where(allowed, 0.0, MASKED).astype(F32)


def bias_of(at, size, plan, position, place):
    lane = lax.broadcasted_iota(jnp.int32, (1, LANES), 1)
    length = plan[at.count + position]
    rows = size.segment // at.nblocks
    biases = []
    for b in range(at.nblocks):
        home = plan[at.home + position * at.nblocks + b]
        limit = length - place * size.segment - home * rows
        for part in range(rows // LANES):
            biases.append(jnp.where(lane + part * LANES < limit, 0.0, MASKED).astype(F32))
    return jnp.concatenate(biases, axis=1)


def attend_owner(size, asked, keys, values, column, bias, new_bias, out, unroll=False):
    tokens, shared, segment = size.tokens, size.shared, size.segment
    scale = math.log2(math.e) / HD**0.5
    stat_lane = lax.broadcasted_iota(jnp.int32, (tokens, LANES), 1)

    def head(j, stats):
        tops, totals = stats
        cols = pl.ds(pl.multiple_of(column + j * HD, HD), HD)
        spans = [
            pl.ds(pl.multiple_of((j * shared + s) * HD, HD), HD) for s in range(shared)
        ]
        scores = lax.dot_general(
            jnp.concatenate([asked[:, span] for span in spans], axis=0),
            keys[:, cols],
            (((1,), (1,)), ((), ())),
            preferred_element_type=F32,
        )
        older = scores[:, :segment] * scale + bias
        newer = scores[:, segment:] * scale + new_bias
        top = jnp.maximum(
            jnp.max(older, axis=1, keepdims=True), jnp.max(newer, axis=1, keepdims=True)
        )
        top = jnp.maximum(top, FLOOR)
        older = jnp.exp2(older - top)
        newer = jnp.exp2(newer - top)
        total = jnp.sum(older, axis=1, keepdims=True) + jnp.sum(newer, axis=1, keepdims=True)
        weights = jnp.concatenate([older.astype(BF16), newer.astype(BF16)], axis=1)
        summed = jnp.dot(weights, values[:, cols], preferred_element_type=F32).astype(BF16)
        for s, span in enumerate(spans):
            part = slice(s * tokens, (s + 1) * tokens)
            out[:, span] = summed[part]
            chosen = stat_lane == j * shared + s
            tops = jnp.where(chosen, top[part], tops)
            totals = jnp.where(chosen, total[part], totals)
        return tops, totals

    stats = (jnp.zeros((tokens, LANES), F32), jnp.zeros((tokens, LANES), F32))
    stats = lax.fori_loop(0, size.kv_own, head, stats, unroll=unroll)
    out[:, size.own * HD :] = pack_stats(*stats, size.own).astype(BF16)


def attend_kernel(at, size, first, newest, pieces, partial, plan, *refs):
    count, some = len(newest), len(pieces)
    q_refs, (new_k, new_v), refs = refs[:some], refs[some : some + 2], refs[some + 2 :]
    outs, (kbuf, vbuf, qbuf, obuf, sems) = refs[-5 - some : -5], refs[-5:]
    sources = refs[: -5 - some]
    place = plan[at.place]
    half = size.width // 2

    for n in range(count):
        slot, last = plan[at.slot + first + n], plan[at.last + first + n]
        bufs = [buf.at[n, pl.ds(0, size.segment)] for buf in (kbuf, vbuf)]
        marks = [sems.at[m, n] for m in range(2)]
        if partial:
            for m in range(2):
                pltpu.make_async_copy(sources[0].at[m], bufs[m], marks[m]).start()
        else:
            for code in range(-1, newest[n] + 1):

                @pl.when(last == code)
                def _():
                    pair = sources[2 * code + 2 : 2 * code + 4]
                    if code < 0:
                        for m in range(2):
                            pltpu.make_async_copy(pair[m].at[0, slot], bufs[m], marks[m]).start()
                    else:
                        for parcel, begin in zip(pair, (half, 0)):
                            place_pieces(parcel, bufs, marks, place, begin)

        for p in range(some):
            pltpu.make_async_copy(q_refs[p].at[0, slot], qbuf.at[n, p], sems.at[2, n]).start()

    for n in range(count):
        slot = plan[at.slot + first + n]
        spans = [(slice(None), slice(None))]
        if partial:
            spans = [own_columns(size, place, p, piece) for p, piece in enumerate(pieces)]
        place_new(new_k, slot, kbuf.at[n], spans)
        place_new(new_v, slot, vbuf.at[n], spans)

    new_bias = new_bias_of(size, place)

    def request(n, carry):
        bias = bias_of(at, size, plan, first + n, place)
        for m, buf in enumerate((kbuf, vbuf)):
            view = buf.at[n, pl.ds(0, size.segment)]
            pltpu.make_async_copy(view, view, sems.at[m, n]).wait()
        pltpu.make_async_copy(qbuf.at[n], qbuf.at[n], sems.at[2, n]).wait()

        def owner(p, carry):
            column = p * size.wide if partial else (place ^ (p + pieces[0])) * size.wide
            attend_owner(
                size,
                qbuf.at[n, p],
                kbuf.at[n],
                vbuf.at[n],
                column,
                bias,
                new_bias,
                obuf.at[p, n],
            )
            return carry

        return lax.fori_loop(0, some, owner, carry)

    lax.fori_loop(0, count, request, 0)
    copies = [pltpu.make_async_copy(obuf.at[p], outs[p], sems.at[3, p]) for p in range(some)]
    for copy in copies:
        copy.start()
    for copy in copies:
        copy.wait()


def own_columns(size, place, p, piece):
    begin = pl.multiple_of((place ^ piece) * size.wide, size.wide)
    return pl.ds(p * size.wide, size.wide), pl.ds(begin, size.wide)


def split(value, parts):
    result = []
    for _ in range(parts):
        result.append(value.astype(BF16).astype(F32))
        value = value - result[-1]
    return result


def pack_stats(tops, totals, own):
    packed = jnp.zeros_like(tops)
    for n, part in enumerate(split(tops, 3) + split(totals, 2)):
        packed = packed + (pltpu.roll(part, n * own, 1) if n else part)
    return packed


def unpack_stats(packed, own):
    parts = [pltpu.roll(packed, LANES - n * own, 1) if n else packed for n in range(5)]
    return (parts[0] + parts[1]) + parts[2], parts[3] + parts[4]


def combined(pieces, heads, out):
    stats = [unpack_stats(piece[:, heads * HD :].astype(F32), heads) for piece in pieces]
    peak = functools.reduce(jnp.maximum, [top for top, _ in stats])
    factors = [jnp.exp2(top - peak) for top, _ in stats]
    denom = sum(total * factor for (_, total), factor in zip(stats, factors))
    shares = [factor / denom for factor in factors]
    for h in range(heads):
        cols = slice(h * HD, (h + 1) * HD)
        out[:, cols] = sum(
            piece[:, cols].astype(F32) * share[:, h : h + 1] for piece, share in zip(pieces, shares)
        ).astype(BF16)


def finish_kernel(at, size, parcels, lots, settled, ready, plan, *refs):
    count = sum(lots)
    some = len(parcels)
    arrived, refs = refs[:some], refs[some:]
    sources, refs = refs[: 2 * len(parcels_before(ready))], refs[2 * len(parcels_before(ready)) :]
    query, new_k, new_v = refs[:3]
    pieces, refs = refs[3:-14], refs[-12:]
    attended, after = refs[0], refs[1:3]
    kbuf, vbuf, qbuf, pbuf, mixed, full, sems, out_sems, in_sems = refs[3:]
    place, slot = plan[at.place], plan[at.slot + count]
    copies = [
        pltpu.make_async_copy(arrived[-1].at[m], buf.at[pl.ds(0, size.segment)], in_sems.at[m])
        for m, buf in enumerate((kbuf, vbuf))
    ]
    copies.append(pltpu.make_async_copy(query.at[0, slot], qbuf, in_sems.at[2]))
    for copy in copies:
        copy.start()
    before = 0
    for lot, each in enumerate([*lots, 1]):
        for i in range(size.width):
            if lot < len(lots) or i:
                piece = pieces[lot * size.width + i - lot // len(lots)]
                into = pbuf.at[i, pl.ds(before, each)]
                pltpu.make_async_copy(piece, into, in_sems.at[3]).start()
        before += each
    for position in range(settled, count):
        bufs = [full.at[n, position - settled] for n in range(2)]
        marks = [sems.at[n, position - settled] for n in range(2)]
        stage(at, plan, position, ready[position], sources, bufs, marks)
    rows = size.segment // at.nblocks
    bufs = [full.at[n, count - settled] for n in range(2)]
    marks = [sems.at[n, count - settled] for n in range(2)]

    def block(b, carry):
        begin = pl.multiple_of(plan[at.perm + count * at.nblocks + b] * rows, rows)
        into = pl.ds(pl.multiple_of(b * rows, rows), rows)
        for parcel, ref in zip(parcels, arrived):
            place_pieces(ref, bufs, marks, place, parcel[0], pl.ds(begin, rows), into)
        return carry

    lax.fori_loop(0, at.nblocks, block, 0)
    spans = [own_columns(size, place, 0, 0)]
    place_new(new_k, slot, kbuf, spans)
    place_new(new_v, slot, vbuf, spans)
    bias = bias_of(at, size, plan, count, place)
    new_bias = new_bias_of(size, place)
    theirs = (pbuf.at[0, pl.ds(0, count)], pbuf.at[pl.ds(1, size.width - 1)])
    for view in theirs:
        pltpu.make_async_copy(view, view, in_sems.at[3]).wait()

    def request(n, carry):
        parts = [pbuf.at[i, n] for i in range(size.width)]
        combined(parts, size.own, mixed.at[n])
        there = attended.at[0, plan[at.slot + n]]
        pltpu.make_async_copy(mixed.at[n], there, in_sems.at[4]).start()
        return carry

    lax.fori_loop(0, count, request, 0)
    for position in range(settled, count + 1):
        there = plan[at.slot + position]
        for n in range(2):
            view, sem = full.at[n, position - settled], sems.at[n, position - settled]
            pltpu.make_async_copy(view, view, sem).wait()
            pltpu.make_async_copy(
                view, after[n].at[0, there], out_sems.at[n, position - settled]
            ).start()
    for copy in copies:
        copy.wait()
    attend_owner(size, qbuf, kbuf, vbuf, 0, bias, new_bias, pbuf.at[0, count], True)
    lax.fori_loop(count, count + 1, request, 0)
    for position in range(settled, count + 1):
        there = plan[at.slot + position]
        for n in range(2):
            view = full.at[n, position - settled]
            pltpu.make_async_copy(
                view, after[n].at[0, there], out_sems.at[n, position - settled]
            ).wait()
    pltpu.make_async_copy(mixed, mixed, in_sems.at[4]).wait()


def parcels_before(ready):
    return range(-1, max(ready))


def shards(
    query, cache_keys, cache_values, new_keys, new_values, masks, movers, block_lists, lengths
):
    groups = lax.axis_size("group")
    width = lax.axis_size("ctx")
    _, requests, segment, features = cache_keys.shape
    tokens = query.shape[2]
    matchings, _, nblocks = block_lists.shape
    own = query.shape[3] // HD
    size = Heads(width, tokens, own, features, segment)
    at = Layout(requests, nblocks, matchings)
    ready = [max(-1, n - (requests - matchings)) for n in range(requests)]
    caches = (cache_keys, cache_values)
    big = pltpu.CompilerParams(vmem_limit_bytes=40 * 1024 * 1024)
    result = jax.ShapeDtypeStruct((tokens, own * HD + LANES), BF16)
    everyone = tuple(range(width))
    halves = [part for part in (everyone[width // 2 :], everyone[: width // 2]) if part]
    parcels = [part for part in (halves[0], everyone[1 : width // 2], (0,)) if part]

    def held(pieces):
        return jax.ShapeDtypeStruct((2, segment, len(pieces) * size.wide), BF16)

    plan, *scalars = pl.pallas_call(
        functools.partial(plan_kernel, at, halves),
        out_shape=(
            jax.ShapeDtypeStruct((at.size,), jnp.int32),
            *[jax.ShapeDtypeStruct((1,), jnp.int32)] * matchings,
            *map(held, halves),
        ),
        in_specs=[SMEM] * 4 + [ANY] * 2,
        out_specs=(SMEM, *[SMEM] * matchings, *[VMEM] * len(halves)),
        scratch_shapes=[pltpu.SemaphoreType.DMA((len(halves),))],
        name="plan",
    )(masks, movers, block_lists.transpose(0, 2, 1), lengths.T, *caches)
    indices, initial = scalars[:matchings], scalars[matchings:]

    def lasting(microseconds):
        return pl.CostEstimate(
            flops=0, bytes_accessed=int(microseconds * 3.7e6), transcendentals=0
        )

    def pick(step, choices, sources, after=()):
        return pl.pallas_call(
            functools.partial(pick_kernel, at, step, choices),
            out_shape=list(map(held, choices)),
            in_specs=[SMEM] + [ANY] * (len(sources) + len(after)),
            out_specs=[VMEM] * len(choices),
            scratch_shapes=[pltpu.SemaphoreType.DMA((len(choices),))],
            cost_estimate=lasting(2.5),
            name=f"pick_{step}",
        )(plan, *sources, *after)

    def attend(first, count, pieces, asked, fresh, sources, partial=False, after=()):
        newest = ready[first : first + count]
        if not partial:
            sources = sources[: 2 * (max(newest) + 2)]
        some = len(pieces)
        held = some * size.wide if partial else features
        return pl.pallas_call(
            functools.partial(attend_kernel, at, size, first, newest, pieces, partial),
            out_shape=[jax.ShapeDtypeStruct((count, *result.shape), BF16)] * some,
            in_specs=[SMEM] + [ANY] * some + [VMEM] * 2 + [ANY] * (len(sources) + len(after)),
            out_specs=[ANY] * some,
            scratch_shapes=[
                pltpu.VMEM((count, segment + LANES, held), BF16),
                pltpu.VMEM((count, segment + LANES, held), BF16),
                pltpu.VMEM((count, some, tokens, own * HD), BF16),
                pltpu.VMEM((some, count, *result.shape), BF16),
                pltpu.SemaphoreType.DMA((4, max(some, count))),
            ],
            compiler_params=big,
            cost_estimate=lasting(1 + 1.5 * some * count),
            name=f"attend_{first}_{count}_{some}",
        )(plan, *[asked[piece] for piece in pieces], *fresh, *sources, *after)

    def send_home(pieces, results):
        return [exchange(part, "ctx", piece) if piece else part for piece, part in zip(pieces, results)]

    def settle(positions, sources):
        count = len(positions)
        newest = [ready[n] for n in positions]
        used = sources[: 2 * (max(newest) + 2)]
        return pl.pallas_call(
            functools.partial(settle_kernel, at, newest),
            out_shape=[jax.ShapeDtypeStruct(cache_keys.shape, BF16)] * 2,
            in_specs=[SMEM] + [ANY] * len(used),
            out_specs=[ANY] * 2,
            scratch_shapes=[
                pltpu.VMEM((2, count, segment, features), BF16),
                pltpu.SemaphoreType.DMA((2, count)),
            ],
            compiler_params=big,
            cost_estimate=lasting(2 * count),
            name="settle",
        )(plan, *used)

    def pad_new():
        extra = -new_keys.shape[2] % 16
        return [jnp.pad(new[0], ((0, 0), (0, extra), (0, 0))) for new in (new_keys, new_values)]

    def prepare(step, sources, arrived):
        return pick(step, halves[:1], [*sources, arrived[0], arrived[0]])[0]

    def first_branch(mask):
        arrived = [exchange(block, "group", mask) for block in initial]
        asked = [query] + [exchange(query, "ctx", piece) for piece in everyone[1:-1]]
        return arrived, prepare(1, caches, arrived), asked, pad_new()

    def middle_branch(step, positions, prepared, asked, fresh, sources, mask):
        moving = [prepared, *pick(step, halves[1:], sources)]
        arrived = [exchange(block, "group", mask) for block in moving]
        done = send_home(
            everyone, attend(positions[0], len(positions), everyone, asked, fresh, sources)
        )
        after = settle(positions, sources) if step == 1 else []
        return arrived, prepare(step + 1, sources, arrived), done, after

    def last_branch(step, first, prepared, asked, fresh, sources, mask):
        whole = attend(first, 1, everyone, asked, fresh, sources)
        moving = [prepared, *pick(step, parcels[1:], sources, whole[:1])]
        arrived = [exchange(block, "group", mask) for block in moving]
        done = send_home(everyone, whole)
        parts, after = {}, done[:1]
        for parcel, block in zip(parcels[:-1], arrived):
            part = attend(requests - 1, 1, parcel, asked, fresh, [block], True, after)
            parts.update(zip(parcel, send_home(parcel, part)))
            after = [*part[:1], *done[1:]]
        return arrived, done, [parts[piece] for piece in everyone[1:]]

    def switch(step, branch, *given):
        return lax.switch(
            indices[step].reshape(()),
            [functools.partial(branch, *given, mask) for mask in range(1, groups)],
        )

    ahead = exchange(query, "ctx", width - 1)
    arrived, prepared, asked, fresh = switch(0, first_branch)
    asked = [*asked, ahead]
    sources = [*caches, *arrived]
    lots, done, after = [], [], None
    for step in range(1, matchings - 1):
        first = sum(lots)
        positions = range(first, ready.index(step - 1) + 1)
        arrived, prepared, part, settled = switch(
            step, middle_branch, step, positions, prepared, asked, fresh, sources
        )
        after = after or settled
        sources = sources + arrived
        lots.append(len(positions))
        done += part
    arrived, part, pieces = switch(
        matchings - 1, last_branch, matchings - 1, sum(lots), prepared, asked, fresh, sources
    )
    lots.append(1)
    pieces = [*done, *part, *pieces]
    ahead = 1 + len(arrived) + len(sources) + 3 + len(pieces)
    left = requests - lots[0]
    return pl.pallas_call(
        functools.partial(finish_kernel, at, size, parcels, lots, lots[0], ready),
        out_shape=[
            jax.ShapeDtypeStruct(array.shape, BF16) for array in (query, cache_keys, cache_values)
        ],
        in_specs=[SMEM]
        + [ANY] * (len(arrived) + len(sources) + 1)
        + [VMEM] * 2
        + [ANY] * (len(pieces) + 2),
        out_specs=[ANY] * 3,
        scratch_shapes=[
            pltpu.VMEM((segment + LANES, size.wide), BF16),
            pltpu.VMEM((segment + LANES, size.wide), BF16),
            pltpu.VMEM((tokens, own * HD), BF16),
            pltpu.VMEM((width, requests, *result.shape), BF16),
            pltpu.VMEM((requests, tokens, own * HD), BF16),
            pltpu.VMEM((2, left, segment, features), BF16),
            pltpu.SemaphoreType.DMA((2, left)),
            pltpu.SemaphoreType.DMA((2, left)),
            pltpu.SemaphoreType.DMA((5,)),
        ],
        input_output_aliases={ahead: 1, ahead + 1: 2},
        compiler_params=big,
        name="finish",
    )(plan, *arrived, *sources, query, *fresh, *pieces, *after)


def solution(mesh):
    placed = (
        P("group", None, None, "ctx"),
        P("group", None, "ctx", None),
        P("group", None, "ctx", None),
        P("group", None, "ctx", None),
        P("group", None, "ctx", None),
        P(),
        P(),
        P(),
        P(),
    )
    return jax.shard_map(
        shards,
        mesh=mesh,
        in_specs=placed,
        out_specs=(
            P("group", None, None, "ctx"),
            P("group", None, "ctx", None),
            P("group", None, "ctx", None),
        ),
        check_vma=False,
    )
```

```python
import functools
import math

import jax
import jax.numpy as jnp
from jax import lax
from jax.experimental import pallas as pl
from jax.experimental.pallas import tpu as pltpu
from jax.sharding import PartitionSpec as P

HD = 128
LANES = 128
PARTS = 5
STATS = 16
MASKED = -1e30
FLOOR = -1e29
BF16 = jnp.bfloat16
F32 = jnp.float32
ANY = pl.BlockSpec(memory_space=pl.ANY)
SMEM = pl.BlockSpec(memory_space=pltpu.SMEM)
VMEM = pl.BlockSpec(memory_space=pltpu.VMEM)


def exchange(block, axis, mask):
    return lax.ppermute(block, axis, [(i, i ^ mask) for i in range(lax.axis_size(axis))])


class Layout:
    def __init__(self, requests, nblocks, matchings):
        self.nblocks = nblocks
        self.slot = 0
        self.last = requests
        self.count = 2 * requests
        self.perm = 3 * requests
        self.home = self.perm + requests * nblocks
        self.mover = self.home + requests * nblocks
        self.source = self.mover + matchings
        self.place = self.source + matchings
        self.size = self.place + 1


def copy_pieces(views, out, sem, place, first):
    wide = views[0].shape[1] // lax.axis_size("ctx")

    def piece(p, carry):
        begin = pl.multiple_of((place ^ (first + p)) * wide, wide)
        into = pl.ds(pl.multiple_of(p * wide, wide), wide)
        for m, view in enumerate(views):
            pltpu.make_async_copy(view.at[:, pl.ds(begin, wide)], out.at[m, :, into], sem).start()
        return carry

    lax.fori_loop(0, out.shape[2] // wide, piece, 0)


def place_pieces(parcel, bufs, sems, place, first, rows=None, into=None):
    rows = pl.ds(0, parcel.shape[1]) if rows is None else rows
    into = rows if into is None else into
    wide = bufs[0].shape[1] // lax.axis_size("ctx")

    def piece(p, carry):
        begin = pl.multiple_of((place ^ (first + p)) * wide, wide)
        origin = pl.ds(pl.multiple_of(p * wide, wide), wide)
        for m, buf in enumerate(bufs):
            pltpu.make_async_copy(
                parcel.at[m, rows, origin], buf.at[into, pl.ds(begin, wide)], sems[m]
            ).start()
        return carry

    lax.fori_loop(0, parcel.shape[2] // wide, piece, 0)


def plan_kernel(
    at, parcels, masks, movers, lists, lengths, keys, values, plan, *refs
):
    some = len(parcels)
    indices, outs, sems = refs[: -1 - some], refs[-1 - some : -1], refs[-1]
    matchings, nblocks, _ = lists.shape
    requests = lengths.shape[0]
    here = lax.axis_index("group")
    place = lax.axis_index("ctx")
    views = [keys.at[0, movers[0, here]], values.at[0, movers[0, here]]]
    for c, (out, pieces) in enumerate(zip(outs, parcels)):
        copy_pieces(views, out, sems.at[c], place, pieces[0])
    for step, index in enumerate(indices):
        index[0] = masks[step] - 1
    plan[at.place] = place
    traced = []
    for slot in range(requests):
        group, where = here, jnp.int32(slot)
        last = jnp.int32(-1)
        blocks = [jnp.int32(b) for b in range(nblocks)]
        for step in reversed(range(matchings)):
            hit = movers[step, group] == where
            partner = group ^ masks[step]
            last = jnp.where(jnp.logical_and(hit, last < 0), step, last)
            moved = []
            for block in blocks:
                origin = block
                for j in range(nblocks):
                    origin = jnp.where(
                        lists[step, j, group] == block, lists[step, j, partner], origin
                    )
                moved.append(jnp.where(hit, origin, block))
            blocks = moved
            where = jnp.where(hit, movers[step, partner], where)
            group = jnp.where(hit, partner, group)
        traced.append((last, lengths[where, group], blocks))
    for slot in range(requests):
        last, count, blocks = traced[slot]
        rank = jnp.int32(0)
        for other in range(requests):
            if other != slot:
                ahead = traced[other][0] * requests + other < last * requests + slot
                rank = rank + ahead.astype(jnp.int32)
        plan[at.slot + rank] = jnp.int32(slot)
        plan[at.last + rank] = last
        plan[at.count + rank] = count
        for b in range(nblocks):
            plan[at.perm + rank * nblocks + b] = blocks[b]
            plan[at.home + rank * nblocks + blocks[b]] = jnp.int32(b)
    for step in range(matchings):
        mover = movers[step, here]
        source = jnp.int32(-1)
        for earlier in range(step):
            source = jnp.where(movers[earlier, here] == mover, earlier, source)
        plan[at.mover + step] = mover
        plan[at.source + step] = source
    for c, out in enumerate(outs):
        pltpu.make_async_copy(out, out, sems.at[c]).wait()


def pick_kernel(at, step, choices, plan, *refs):
    sources, outs, sems = refs[: 2 * step + 2], refs[-1 - len(choices) : -1], refs[-1]
    mover, source, place = plan[at.mover + step], plan[at.source + step], plan[at.place]
    half = lax.axis_size("ctx") // 2
    for code in range(-1, step):
        pair = sources[2 * code + 2 : 2 * code + 4]

        @pl.when(source == code)
        def _():
            for c, (out, pieces) in enumerate(zip(outs, choices)):
                if code < 0:
                    views = [view.at[0, mover] for view in pair]
                    copy_pieces(views, out, sems.at[c], place, pieces[0])
                else:
                    far = pieces[0] >= half
                    begin = (pieces[0] - half * far) * (out.shape[2] // len(pieces))
                    view = pair[0 if far else 1].at[:, :, pl.ds(begin, out.shape[2])]
                    pltpu.make_async_copy(view, out, sems.at[c]).start()

    for c, out in enumerate(outs):
        pltpu.make_async_copy(out, out, sems.at[c]).wait()


def stage(at, plan, position, newest, sources, bufs, sems):
    rows = bufs[0].shape[0] // at.nblocks
    slot, last, place = plan[at.slot + position], plan[at.last + position], plan[at.place]
    half = lax.axis_size("ctx") // 2
    for code in range(-1, newest + 1):

        @pl.when(last == code)
        def _():
            pair = sources[2 * code + 2 : 2 * code + 4]

            def block(b, carry):
                begin = pl.multiple_of(plan[at.perm + position * at.nblocks + b] * rows, rows)
                into = pl.ds(pl.multiple_of(b * rows, rows), rows)
                if code < 0:
                    for n in range(2):
                        pltpu.make_async_copy(
                            pair[n].at[0, slot, pl.ds(begin, rows)], bufs[n].at[into], sems[n]
                        ).start()
                else:
                    for parcel, first in zip(pair, (half, 0)):
                        place_pieces(parcel, bufs, sems, place, first, pl.ds(begin, rows), into)
                return carry

            lax.fori_loop(0, at.nblocks, block, 0)


def settle_kernel(at, ready, plan, *refs):
    sources, outs, buf, sems = refs[:-4], refs[-4:-2], refs[-2], refs[-1]
    for position, newest in enumerate(ready):
        bufs = [buf.at[n, position] for n in range(2)]
        stage(at, plan, position, newest, sources, bufs, [sems.at[n, position] for n in range(2)])
    for position in range(len(ready)):
        slot = plan[at.slot + position]
        for n in range(2):
            view, sem = buf.at[n, position], sems.at[n, position]
            pltpu.make_async_copy(view, view, sem).wait()
            pltpu.make_async_copy(view, outs[n].at[0, slot], sem).start()
    for position in range(len(ready)):
        slot = plan[at.slot + position]
        for n in range(2):
            view, sem = buf.at[n, position], sems.at[n, position]
            pltpu.make_async_copy(view, outs[n].at[0, slot], sem).wait()


class Heads:
    def __init__(self, width, tokens, own, features, segment):
        self.width = width
        self.tokens = tokens
        self.own = own
        self.shared = own * width * HD // features
        self.kv_own = own // self.shared
        self.wide = self.kv_own * HD
        self.segment = segment


def place_new(new, slot, buf, spans):
    rows = new.shape[1]
    for cols, origin in spans:
        buf[buf.shape[0] - rows :, cols] = new[slot, :, origin]


def place_new_bias(size, place, bias):
    fresh = size.tokens // size.width
    shape = bias[size.segment :].shape
    row = lax.broadcasted_iota(jnp.int32, shape, 0)
    token = lax.broadcasted_iota(jnp.int32, shape, 1) % size.tokens
    allowed = jnp.logical_and(row < fresh, row + place * fresh <= token)
    bias[size.segment :] = jnp.where(allowed, 0.0, MASKED).astype(F32)


def place_bias(at, size, plan, position, place, bias):
    rows = size.segment // at.nblocks
    length = plan[at.count + position]
    row = lax.broadcasted_iota(jnp.int32, (rows, bias.shape[1]), 0)

    def block(b, carry):
        limit = length - place * size.segment - plan[at.home + position * at.nblocks + b] * rows
        into = pl.ds(pl.multiple_of(b * rows, rows), rows)
        bias[into] = jnp.where(row < limit, 0.0, MASKED).astype(F32)
        return carry

    lax.fori_loop(0, at.nblocks, block, 0)


def attend_owner(size, asked, keys, values, column, bias, out, unroll=False):
    tokens, shared = size.tokens, size.shared
    scale = math.log2(math.e) / HD**0.5
    stat_row = lax.broadcasted_iota(jnp.int32, (STATS, shared * tokens), 0)

    def head(j, stats):
        cols = pl.ds(pl.multiple_of(column + j * HD, HD), HD)
        spans = [
            pl.ds(pl.multiple_of((j * shared + s) * HD, HD), HD) for s in range(shared)
        ]
        scores = lax.dot_general(
            keys[:, cols],
            jnp.concatenate([asked[:, span] for span in spans], axis=0),
            (((1,), (1,)), ((), ())),
            preferred_element_type=F32,
        )
        scores = scores * scale + bias[...]
        top = jnp.maximum(jnp.max(scores, axis=0, keepdims=True), FLOOR)
        weights = jnp.exp2(scores - top)
        total = jnp.sum(weights, axis=0, keepdims=True)
        summed = lax.dot_general(
            values[:, cols],
            weights.astype(BF16),
            (((0,), (0,)), ((), ())),
            preferred_element_type=F32,
        )
        out[pl.ds(pl.multiple_of(j * HD, HD), HD)] = summed.astype(BF16)
        for n, part in enumerate(split(top, 3) + split(total, 2)):
            stats = jnp.where(stat_row == j * PARTS + n, part, stats)
        return stats

    stats = jnp.zeros(stat_row.shape, F32)
    stats = lax.fori_loop(0, size.kv_own, head, stats, unroll=unroll)
    out[size.wide :] = stats.astype(BF16)


def attend_kernel(at, size, first, newest, pieces, partial, cuts, plan, *refs):
    count, some = len(newest), len(pieces)
    q_refs, (new_k, new_v), refs = refs[:some], refs[some : some + 2], refs[some + 2 :]
    total = some * len(cuts)
    outs, (kbuf, vbuf, qbuf, obuf, bias, sems) = refs[-6 - total : -6], refs[-6:]
    sources = refs[: -6 - total]
    place = plan[at.place]
    half = size.width // 2

    for n in range(count):
        slot, last = plan[at.slot + first + n], plan[at.last + first + n]
        bufs = [buf.at[n, pl.ds(0, size.segment)] for buf in (kbuf, vbuf)]
        marks = [sems.at[m, n] for m in range(2)]
        if partial:
            for m in range(2):
                pltpu.make_async_copy(sources[0].at[m], bufs[m], marks[m]).start()
        else:
            for code in range(-1, newest[n] + 1):

                @pl.when(last == code)
                def _():
                    pair = sources[2 * code + 2 : 2 * code + 4]
                    if code < 0:
                        for m in range(2):
                            pltpu.make_async_copy(pair[m].at[0, slot], bufs[m], marks[m]).start()
                    else:
                        for parcel, begin in zip(pair, (half, 0)):
                            place_pieces(parcel, bufs, marks, place, begin)

        for p in range(some):
            pltpu.make_async_copy(q_refs[p].at[0, slot], qbuf.at[n, p], sems.at[2, n]).start()

    for n in range(count):
        slot = plan[at.slot + first + n]
        spans = [(slice(None), slice(None))]
        if partial:
            spans = [own_columns(size, place, p, piece) for p, piece in enumerate(pieces)]
        place_new(new_k, slot, kbuf.at[n], spans)
        place_new(new_v, slot, vbuf.at[n], spans)

    place_new_bias(size, place, bias)

    def request(n, carry):
        place_bias(at, size, plan, first + n, place, bias)
        for m, buf in enumerate((kbuf, vbuf)):
            view = buf.at[n, pl.ds(0, size.segment)]
            pltpu.make_async_copy(view, view, sems.at[m, n]).wait()
        pltpu.make_async_copy(qbuf.at[n], qbuf.at[n], sems.at[2, n]).wait()

        def owner(p, carry):
            column = p * size.wide if partial else (place ^ (p + pieces[0])) * size.wide
            attend_owner(
                size,
                qbuf.at[n, p],
                kbuf.at[n],
                vbuf.at[n],
                column,
                bias,
                obuf.at[p, n],
            )
            return carry

        return lax.fori_loop(0, some, owner, carry)

    lax.fori_loop(0, count, request, 0)
    copies = []
    for n, out in enumerate(outs):
        p, cut = divmod(n, len(cuts))
        view = obuf.at[p, :, pl.ds(sum(cuts[:cut]), cuts[cut])]
        copies.append(pltpu.make_async_copy(view, out, sems.at[3, n]))
    for copy in copies:
        copy.start()
    for copy in copies:
        copy.wait()


def own_columns(size, place, p, piece):
    begin = pl.multiple_of((place ^ piece) * size.wide, size.wide)
    return pl.ds(p * size.wide, size.wide), pl.ds(begin, size.wide)


def split(value, parts):
    result = []
    for _ in range(parts):
        result.append(value.astype(BF16).astype(F32))
        value = value - result[-1]
    return result


def combined(size, pieces, out):
    tokens = size.tokens
    stats = [piece[size.wide :].astype(F32) for piece in pieces]
    for j in range(size.kv_own):
        rows = [[stat[n : n + 1] for n in range(j * PARTS, (j + 1) * PARTS)] for stat in stats]
        tops = [row[0] + row[1] + row[2] for row in rows]
        peak = functools.reduce(jnp.maximum, tops)
        factors = [jnp.exp2(top - peak) for top in tops]
        denom = sum((row[3] + row[4]) * factor for row, factor in zip(rows, factors))
        mixed = sum(
            piece[j * HD : (j + 1) * HD].astype(F32) * (factor / denom)
            for piece, factor in zip(pieces, factors)
        )
        mixed = mixed.T.astype(BF16)
        for s in range(size.shared):
            cols = slice((j * size.shared + s) * HD, (j * size.shared + s + 1) * HD)
            out[:, cols] = mixed[s * tokens : (s + 1) * tokens]


def finish_kernel(at, size, parcels, lots, settled, ready, plan, *refs):
    count = sum(lots)
    some = len(parcels)
    arrived, refs = refs[:some], refs[some:]
    sources, refs = refs[: 2 * len(parcels_before(ready))], refs[2 * len(parcels_before(ready)) :]
    query, new_k, new_v = refs[:3]
    pieces, refs = refs[3:-15], refs[-13:]
    attended, after = refs[0], refs[1:3]
    kbuf, vbuf, qbuf, pbuf, bias, mixed, full, sems, out_sems, in_sems = refs[3:]
    place, slot = plan[at.place], plan[at.slot + count]
    copies = [
        pltpu.make_async_copy(arrived[-1].at[m], buf.at[pl.ds(0, size.segment)], in_sems.at[m])
        for m, buf in enumerate((kbuf, vbuf))
    ]
    copies.append(pltpu.make_async_copy(query.at[0, slot], qbuf, in_sems.at[2]))
    for copy in copies:
        copy.start()
    pieces = iter(pieces)
    before = 0
    for lot, each in enumerate([*lots, 1]):
        for i in range(size.width):
            row = 0
            while row < pbuf.shape[2] and (lot < len(lots) or i):
                piece = next(pieces)
                into = pbuf.at[i, pl.ds(before, each), pl.ds(row, piece.shape[1])]
                pltpu.make_async_copy(piece, into, in_sems.at[3]).start()
                row += piece.shape[1]
        before += each
    for position in range(settled, count):
        bufs = [full.at[n, position - settled] for n in range(2)]
        marks = [sems.at[n, position - settled] for n in range(2)]
        stage(at, plan, position, ready[position], sources, bufs, marks)
    rows = size.segment // at.nblocks
    bufs = [full.at[n, count - settled] for n in range(2)]
    marks = [sems.at[n, count - settled] for n in range(2)]

    def block(b, carry):
        begin = pl.multiple_of(plan[at.perm + count * at.nblocks + b] * rows, rows)
        into = pl.ds(pl.multiple_of(b * rows, rows), rows)
        for parcel, ref in zip(parcels, arrived):
            place_pieces(ref, bufs, marks, place, parcel[0], pl.ds(begin, rows), into)
        return carry

    lax.fori_loop(0, at.nblocks, block, 0)
    spans = [own_columns(size, place, 0, 0)]
    place_new(new_k, slot, kbuf, spans)
    place_new(new_v, slot, vbuf, spans)
    place_bias(at, size, plan, count, place, bias)
    place_new_bias(size, place, bias)
    theirs = (pbuf.at[0, pl.ds(0, count)], pbuf.at[pl.ds(1, size.width - 1)])
    for view in theirs:
        pltpu.make_async_copy(view, view, in_sems.at[3]).wait()

    def request(n, carry):
        parts = [pbuf.at[i, n] for i in range(size.width)]
        combined(size, parts, mixed.at[n])
        there = attended.at[0, plan[at.slot + n]]
        pltpu.make_async_copy(mixed.at[n], there, in_sems.at[4]).start()
        return carry

    lax.fori_loop(0, count, request, 0)
    for position in range(settled, count + 1):
        there = plan[at.slot + position]
        for n in range(2):
            view, sem = full.at[n, position - settled], sems.at[n, position - settled]
            pltpu.make_async_copy(view, view, sem).wait()
            pltpu.make_async_copy(
                view, after[n].at[0, there], out_sems.at[n, position - settled]
            ).start()
    for copy in copies:
        copy.wait()
    attend_owner(size, qbuf, kbuf, vbuf, 0, bias, pbuf.at[0, count], True)
    lax.fori_loop(count, count + 1, request, 0)
    for position in range(settled, count + 1):
        there = plan[at.slot + position]
        for n in range(2):
            view = full.at[n, position - settled]
            pltpu.make_async_copy(
                view, after[n].at[0, there], out_sems.at[n, position - settled]
            ).wait()
    pltpu.make_async_copy(mixed, mixed, in_sems.at[4]).wait()


def parcels_before(ready):
    return range(-1, max(ready))


def shards(
    query, cache_keys, cache_values, new_keys, new_values, masks, movers, block_lists, lengths
):
    groups = lax.axis_size("group")
    width = lax.axis_size("ctx")
    _, requests, segment, features = cache_keys.shape
    tokens = query.shape[2]
    matchings, _, nblocks = block_lists.shape
    own = query.shape[3] // HD
    size = Heads(width, tokens, own, features, segment)
    at = Layout(requests, nblocks, matchings)
    ready = [max(-1, n - (requests - matchings)) for n in range(requests)]
    caches = (cache_keys, cache_values)
    big = pltpu.CompilerParams(vmem_limit_bytes=40 * 1024 * 1024)
    queries = size.shared * tokens
    result = jax.ShapeDtypeStruct((size.wide + STATS, queries), BF16)
    behind = -(-new_keys.shape[2] // 16) * 16
    scores = pltpu.VMEM((segment + behind, queries), F32)
    everyone = tuple(range(width))
    halves = [part for part in (everyone[width // 2 :], everyone[: width // 2]) if part]
    near = everyone[1 : width // 2]
    parcels = [part for part in (halves[0], near, (0,)) if part]

    def held(pieces):
        return jax.ShapeDtypeStruct((2, segment, len(pieces) * size.wide), BF16)

    plan, *scalars = pl.pallas_call(
        functools.partial(plan_kernel, at, halves),
        out_shape=(
            jax.ShapeDtypeStruct((at.size,), jnp.int32),
            *[jax.ShapeDtypeStruct((1,), jnp.int32)] * matchings,
            *map(held, halves),
        ),
        in_specs=[SMEM] * 4 + [ANY] * 2,
        out_specs=(SMEM, *[SMEM] * matchings, *[VMEM] * len(halves)),
        scratch_shapes=[pltpu.SemaphoreType.DMA((len(halves),))],
        name="plan",
    )(masks, movers, block_lists.transpose(0, 2, 1), lengths.T, *caches)
    indices, initial = scalars[:matchings], scalars[matchings:]

    def lasting(microseconds):
        return pl.CostEstimate(
            flops=0, bytes_accessed=int(microseconds * 3.7e6), transcendentals=0
        )

    def pick(step, choices, sources, after=()):
        return pl.pallas_call(
            functools.partial(pick_kernel, at, step, choices),
            out_shape=list(map(held, choices)),
            in_specs=[SMEM] + [ANY] * (len(sources) + len(after)),
            out_specs=[VMEM] * len(choices),
            scratch_shapes=[pltpu.SemaphoreType.DMA((len(choices),))],
            cost_estimate=lasting(2.5),
            name=f"pick_{step}",
        )(plan, *sources, *after)

    def attend(first, count, pieces, asked, fresh, sources, partial=False, after=(), cuts=None):
        newest = ready[first : first + count]
        if not partial:
            sources = sources[: 2 * (max(newest) + 2)]
        some = len(pieces)
        held = some * size.wide if partial else features
        cuts = cuts or [result.shape[0]]
        return pl.pallas_call(
            functools.partial(attend_kernel, at, size, first, newest, pieces, partial, cuts),
            out_shape=[
                jax.ShapeDtypeStruct((count, rows, queries), BF16) for _ in pieces for rows in cuts
            ],
            in_specs=[SMEM] + [ANY] * some + [VMEM] * 2 + [ANY] * (len(sources) + len(after)),
            out_specs=[ANY] * (some * len(cuts)),
            scratch_shapes=[
                pltpu.VMEM((count, segment + behind, held), BF16),
                pltpu.VMEM((count, segment + behind, held), BF16),
                pltpu.VMEM((count, some, tokens, own * HD), BF16),
                pltpu.VMEM((some, count, *result.shape), BF16),
                scores,
                pltpu.SemaphoreType.DMA((4, max(some * len(cuts), count))),
            ],
            compiler_params=big,
            cost_estimate=lasting(1 + 1.5 * some * count),
            name=f"attend_{first}_{count}_{some}",
        )(plan, *[asked[piece] for piece in pieces], *fresh, *sources, *after)

    def send_home(pieces, results):
        return [exchange(part, "ctx", piece) if piece else part for piece, part in zip(pieces, results)]

    def settle(positions, sources):
        count = len(positions)
        newest = [ready[n] for n in positions]
        used = sources[: 2 * (max(newest) + 2)]
        return pl.pallas_call(
            functools.partial(settle_kernel, at, newest),
            out_shape=[jax.ShapeDtypeStruct(cache_keys.shape, BF16)] * 2,
            in_specs=[SMEM] + [ANY] * len(used),
            out_specs=[ANY] * 2,
            scratch_shapes=[
                pltpu.VMEM((2, count, segment, features), BF16),
                pltpu.SemaphoreType.DMA((2, count)),
            ],
            compiler_params=big,
            cost_estimate=lasting(2 * count),
            name="settle",
        )(plan, *used)

    def pad_new():
        extra = behind - new_keys.shape[2]
        return [jnp.pad(new[0], ((0, 0), (0, extra), (0, 0))) for new in (new_keys, new_values)]

    def prepare(step, sources, arrived):
        return pick(step, halves[:1], [*sources, arrived[0], arrived[0]])[0]

    def first_branch(mask):
        arrived = [exchange(block, "group", mask) for block in initial]
        asked = [query] + [exchange(query, "ctx", piece) for piece in everyone[1:-1]]
        return arrived, prepare(1, caches, arrived), asked, pad_new()

    def middle_branch(step, positions, prepared, asked, fresh, sources, mask):
        moving = [prepared, *pick(step, halves[1:], sources)]
        arrived = [exchange(block, "group", mask) for block in moving]
        done = send_home(
            everyone, attend(positions[0], len(positions), everyone, asked, fresh, sources)
        )
        after = settle(positions, sources) if step == 1 else []
        return arrived, prepare(step + 1, sources, arrived), done, after

    def last_branch(step, first, prepared, asked, fresh, sources, mask):
        whole = attend(first, 1, everyone, asked, fresh, sources)
        moving = [prepared, *pick(step, parcels[1:], sources, whole[:1])]
        arrived = [exchange(block, "group", mask) for block in moving]
        done = send_home(everyone, whole)
        parts, after = {}, done[:1]
        for parcel, block in zip(parcels[:-1], arrived):
            cuts = [size.wide // 2, result.shape[0] - size.wide // 2] if parcel == near else None
            part = attend(requests - 1, 1, parcel, asked, fresh, [block], True, after, cuts)
            each = len(part) // len(parcel)
            for n, piece in enumerate(parcel):
                parts[piece] = [
                    exchange(array, "ctx", piece) for array in part[n * each : (n + 1) * each]
                ]
            after = [*part[:1], *done[1:]]
        return arrived, done, [array for piece in everyone[1:] for array in parts[piece]]

    def switch(step, branch, *given):
        return lax.switch(
            indices[step].reshape(()),
            [functools.partial(branch, *given, mask) for mask in range(1, groups)],
        )

    ahead = exchange(query, "ctx", width - 1)
    arrived, prepared, asked, fresh = switch(0, first_branch)
    asked = [*asked, ahead]
    sources = [*caches, *arrived]
    lots, done, after = [], [], None
    for step in range(1, matchings - 1):
        first = sum(lots)
        positions = range(first, ready.index(step - 1) + 1)
        arrived, prepared, part, settled = switch(
            step, middle_branch, step, positions, prepared, asked, fresh, sources
        )
        after = after or settled
        sources = sources + arrived
        lots.append(len(positions))
        done += part
    arrived, part, pieces = switch(
        matchings - 1, last_branch, matchings - 1, sum(lots), prepared, asked, fresh, sources
    )
    lots.append(1)
    pieces = [*done, *part, *pieces]
    ahead = 1 + len(arrived) + len(sources) + 3 + len(pieces)
    left = requests - lots[0]
    return pl.pallas_call(
        functools.partial(finish_kernel, at, size, parcels, lots, lots[0], ready),
        out_shape=[
            jax.ShapeDtypeStruct(array.shape, BF16) for array in (query, cache_keys, cache_values)
        ],
        in_specs=[SMEM]
        + [ANY] * (len(arrived) + len(sources) + 1)
        + [VMEM] * 2
        + [ANY] * (len(pieces) + 2),
        out_specs=[ANY] * 3,
        scratch_shapes=[
            pltpu.VMEM((segment + behind, size.wide), BF16),
            pltpu.VMEM((segment + behind, size.wide), BF16),
            pltpu.VMEM((tokens, own * HD), BF16),
            pltpu.VMEM((width, requests, *result.shape), BF16),
            scores,
            pltpu.VMEM((requests, tokens, own * HD), BF16),
            pltpu.VMEM((2, left, segment, features), BF16),
            pltpu.SemaphoreType.DMA((2, left)),
            pltpu.SemaphoreType.DMA((2, left)),
            pltpu.SemaphoreType.DMA((5,)),
        ],
        input_output_aliases={ahead: 1, ahead + 1: 2},
        compiler_params=big,
        name="finish",
    )(plan, *arrived, *sources, query, *fresh, *pieces, *after)


def solution(mesh):
    placed = (
        P("group", None, None, "ctx"),
        P("group", None, "ctx", None),
        P("group", None, "ctx", None),
        P("group", None, "ctx", None),
        P("group", None, "ctx", None),
        P(),
        P(),
        P(),
        P(),
    )
    return jax.shard_map(
        shards,
        mesh=mesh,
        in_specs=placed,
        out_specs=(
            P("group", None, None, "ctx"),
            P("group", None, "ctx", None),
            P("group", None, "ctx", None),
        ),
        check_vma=False,
    )
```

```python
import functools
import math

import jax
import jax.numpy as jnp
from jax import lax
from jax.experimental import pallas as pl
from jax.experimental.pallas import tpu as pltpu
from jax.sharding import PartitionSpec as P

HD = 128
LANES = 128
PARTS = 5
STATS = 16
MASKED = -1e30
FLOOR = -1e29
BF16 = jnp.bfloat16
F32 = jnp.float32
ANY = pl.BlockSpec(memory_space=pl.ANY)
SMEM = pl.BlockSpec(memory_space=pltpu.SMEM)
VMEM = pl.BlockSpec(memory_space=pltpu.VMEM)


def exchange(block, axis, mask):
    return lax.ppermute(block, axis, [(i, i ^ mask) for i in range(lax.axis_size(axis))])


class Layout:
    def __init__(self, requests, nblocks, matchings):
        self.nblocks = nblocks
        self.slot = 0
        self.last = requests
        self.count = 2 * requests
        self.perm = 3 * requests
        self.home = self.perm + requests * nblocks
        self.mover = self.home + requests * nblocks
        self.source = self.mover + matchings
        self.place = self.source + matchings
        self.size = self.place + 1


def copy_pieces(views, out, sem, place, first):
    wide = views[0].shape[1] // lax.axis_size("ctx")

    def piece(p, carry):
        begin = pl.multiple_of((place ^ (first + p)) * wide, wide)
        into = pl.ds(pl.multiple_of(p * wide, wide), wide)
        for m, view in enumerate(views):
            pltpu.make_async_copy(view.at[:, pl.ds(begin, wide)], out.at[m, :, into], sem).start()
        return carry

    lax.fori_loop(0, out.shape[2] // wide, piece, 0)


def place_pieces(parcel, bufs, sems, place, first, rows=None, into=None):
    rows = pl.ds(0, parcel.shape[1]) if rows is None else rows
    into = rows if into is None else into
    wide = bufs[0].shape[1] // lax.axis_size("ctx")

    def piece(p, carry):
        begin = pl.multiple_of((place ^ (first + p)) * wide, wide)
        origin = pl.ds(pl.multiple_of(p * wide, wide), wide)
        for m, buf in enumerate(bufs):
            pltpu.make_async_copy(
                parcel.at[m, rows, origin], buf.at[into, pl.ds(begin, wide)], sems[m]
            ).start()
        return carry

    lax.fori_loop(0, parcel.shape[2] // wide, piece, 0)


def plan_kernel(
    at, parcels, masks, movers, lists, lengths, keys, values, plan, *refs
):
    some = len(parcels)
    indices, outs, sems = refs[: -1 - some], refs[-1 - some : -1], refs[-1]
    matchings, nblocks, _ = lists.shape
    requests = lengths.shape[0]
    here = lax.axis_index("group")
    place = lax.axis_index("ctx")
    views = [keys.at[0, movers[0, here]], values.at[0, movers[0, here]]]
    for c, (out, pieces) in enumerate(zip(outs, parcels)):
        copy_pieces(views, out, sems.at[c], place, pieces[0])
    for step, index in enumerate(indices):
        index[0] = masks[step] - 1
    plan[at.place] = place
    traced = []
    for slot in range(requests):
        group, where = here, jnp.int32(slot)
        last = jnp.int32(-1)
        blocks = [jnp.int32(b) for b in range(nblocks)]
        for step in reversed(range(matchings)):
            hit = movers[step, group] == where
            partner = group ^ masks[step]
            last = jnp.where(jnp.logical_and(hit, last < 0), step, last)
            moved = []
            for block in blocks:
                origin = block
                for j in range(nblocks):
                    origin = jnp.where(
                        lists[step, j, group] == block, lists[step, j, partner], origin
                    )
                moved.append(jnp.where(hit, origin, block))
            blocks = moved
            where = jnp.where(hit, movers[step, partner], where)
            group = jnp.where(hit, partner, group)
        traced.append((last, lengths[where, group], blocks))
    for slot in range(requests):
        last, count, blocks = traced[slot]
        rank = jnp.int32(0)
        for other in range(requests):
            if other != slot:
                ahead = traced[other][0] * requests + other < last * requests + slot
                rank = rank + ahead.astype(jnp.int32)
        plan[at.slot + rank] = jnp.int32(slot)
        plan[at.last + rank] = last
        plan[at.count + rank] = count
        for b in range(nblocks):
            plan[at.perm + rank * nblocks + b] = blocks[b]
            plan[at.home + rank * nblocks + blocks[b]] = jnp.int32(b)
    for step in range(matchings):
        mover = movers[step, here]
        source = jnp.int32(-1)
        for earlier in range(step):
            source = jnp.where(movers[earlier, here] == mover, earlier, source)
        plan[at.mover + step] = mover
        plan[at.source + step] = source
    for c, out in enumerate(outs):
        pltpu.make_async_copy(out, out, sems.at[c]).wait()


def pick_kernel(at, step, choices, plan, *refs):
    sources, outs, sems = refs[: 2 * step + 2], refs[-1 - len(choices) : -1], refs[-1]
    mover, source, place = plan[at.mover + step], plan[at.source + step], plan[at.place]
    half = lax.axis_size("ctx") // 2
    for code in range(-1, step):
        pair = sources[2 * code + 2 : 2 * code + 4]

        @pl.when(source == code)
        def _():
            for c, (out, pieces) in enumerate(zip(outs, choices)):
                if code < 0:
                    views = [view.at[0, mover] for view in pair]
                    copy_pieces(views, out, sems.at[c], place, pieces[0])
                else:
                    far = pieces[0] >= half
                    begin = (pieces[0] - half * far) * (out.shape[2] // len(pieces))
                    view = pair[0 if far else 1].at[:, :, pl.ds(begin, out.shape[2])]
                    pltpu.make_async_copy(view, out, sems.at[c]).start()

    for c, out in enumerate(outs):
        pltpu.make_async_copy(out, out, sems.at[c]).wait()


def stage(at, plan, position, newest, sources, bufs, sems):
    rows = bufs[0].shape[0] // at.nblocks
    slot, last, place = plan[at.slot + position], plan[at.last + position], plan[at.place]
    half = lax.axis_size("ctx") // 2
    for code in range(-1, newest + 1):

        @pl.when(last == code)
        def _():
            pair = sources[2 * code + 2 : 2 * code + 4]

            def block(b, carry):
                begin = pl.multiple_of(plan[at.perm + position * at.nblocks + b] * rows, rows)
                into = pl.ds(pl.multiple_of(b * rows, rows), rows)
                if code < 0:
                    for n in range(2):
                        pltpu.make_async_copy(
                            pair[n].at[0, slot, pl.ds(begin, rows)], bufs[n].at[into], sems[n]
                        ).start()
                else:
                    for parcel, first in zip(pair, (half, 0)):
                        place_pieces(parcel, bufs, sems, place, first, pl.ds(begin, rows), into)
                return carry

            lax.fori_loop(0, at.nblocks, block, 0)


def settle_kernel(at, ready, plan, *refs):
    sources, outs, buf, sems = refs[:-4], refs[-4:-2], refs[-2], refs[-1]
    for position, newest in enumerate(ready):
        bufs = [buf.at[n, position] for n in range(2)]
        stage(at, plan, position, newest, sources, bufs, [sems.at[n, position] for n in range(2)])
    for position in range(len(ready)):
        slot = plan[at.slot + position]
        for n in range(2):
            view, sem = buf.at[n, position], sems.at[n, position]
            pltpu.make_async_copy(view, view, sem).wait()
            pltpu.make_async_copy(view, outs[n].at[0, slot], sem).start()
    for position in range(len(ready)):
        slot = plan[at.slot + position]
        for n in range(2):
            view, sem = buf.at[n, position], sems.at[n, position]
            pltpu.make_async_copy(view, outs[n].at[0, slot], sem).wait()


class Heads:
    def __init__(self, width, tokens, own, features, segment):
        self.width = width
        self.tokens = tokens
        self.own = own
        self.shared = own * width * HD // features
        self.kv_own = own // self.shared
        self.wide = self.kv_own * HD
        self.segment = segment


def place_new(new, slot, buf, spans):
    rows = new.shape[1]
    for cols, origin in spans:
        buf[buf.shape[0] - rows :, cols] = new[slot, :, origin]


def place_new_bias(size, place, bias):
    fresh = size.tokens // size.width
    shape = bias[size.segment :].shape
    row = lax.broadcasted_iota(jnp.int32, shape, 0)
    token = lax.broadcasted_iota(jnp.int32, shape, 1) % size.tokens
    allowed = jnp.logical_and(row < fresh, row + place * fresh <= token)
    bias[size.segment :] = jnp.where(allowed, 0.0, MASKED).astype(F32)


def place_bias(at, size, plan, position, place, bias):
    rows = size.segment // at.nblocks
    length = plan[at.count + position]
    row = lax.broadcasted_iota(jnp.int32, (rows, bias.shape[1]), 0)

    def block(b, carry):
        limit = length - place * size.segment - plan[at.home + position * at.nblocks + b] * rows
        into = pl.ds(pl.multiple_of(b * rows, rows), rows)
        bias[into] = jnp.where(row < limit, 0.0, MASKED).astype(F32)
        return carry

    lax.fori_loop(0, at.nblocks, block, 0)


def attend_owner(size, asked, keys, values, column, bias, out, unroll=False):
    tokens, shared = size.tokens, size.shared
    scale = math.log2(math.e) / HD**0.5
    stat_row = lax.broadcasted_iota(jnp.int32, (STATS, shared * tokens), 0)

    def head(j, stats):
        cols = pl.ds(pl.multiple_of(column + j * HD, HD), HD)
        spans = [
            pl.ds(pl.multiple_of((j * shared + s) * HD, HD), HD) for s in range(shared)
        ]
        scores = lax.dot_general(
            keys[:, cols],
            jnp.concatenate([asked[:, span] for span in spans], axis=0),
            (((1,), (1,)), ((), ())),
            preferred_element_type=F32,
        )
        scores = scores * scale + bias[...]
        top = jnp.maximum(jnp.max(scores, axis=0, keepdims=True), FLOOR)
        weights = jnp.exp2(scores - top)
        total = jnp.sum(weights, axis=0, keepdims=True)
        summed = lax.dot_general(
            values[:, cols],
            weights.astype(BF16),
            (((0,), (0,)), ((), ())),
            preferred_element_type=F32,
        )
        out[pl.ds(pl.multiple_of(j * HD, HD), HD)] = summed.astype(BF16)
        for n, part in enumerate(split(top, 3) + split(total, 2)):
            stats = jnp.where(stat_row == j * PARTS + n, part, stats)
        return stats

    stats = jnp.zeros(stat_row.shape, F32)
    stats = lax.fori_loop(0, size.kv_own, head, stats, unroll=unroll)
    out[size.wide :] = stats.astype(BF16)


def attend_kernel(at, size, first, newest, pieces, partial, cuts, plan, *refs):
    count, some = len(newest), len(pieces)
    q_refs, (new_k, new_v), refs = refs[:some], refs[some : some + 2], refs[some + 2 :]
    total = some * len(cuts)
    outs, (kbuf, vbuf, qbuf, obuf, bias, sems) = refs[-6 - total : -6], refs[-6:]
    sources = refs[: -6 - total]
    place = plan[at.place]
    half = size.width // 2

    for n in range(count):
        slot, last = plan[at.slot + first + n], plan[at.last + first + n]
        bufs = [buf.at[n, pl.ds(0, size.segment)] for buf in (kbuf, vbuf)]
        marks = [sems.at[m, n] for m in range(2)]
        if partial:
            for m in range(2):
                pltpu.make_async_copy(sources[0].at[m], bufs[m], marks[m]).start()
        else:
            for code in range(-1, newest[n] + 1):

                @pl.when(last == code)
                def _():
                    pair = sources[2 * code + 2 : 2 * code + 4]
                    if code < 0:
                        for m in range(2):
                            pltpu.make_async_copy(pair[m].at[0, slot], bufs[m], marks[m]).start()
                    else:
                        for parcel, begin in zip(pair, (half, 0)):
                            place_pieces(parcel, bufs, marks, place, begin)

        for p in range(some):
            pltpu.make_async_copy(q_refs[p].at[0, slot], qbuf.at[n, p], sems.at[2, n]).start()

    for n in range(count):
        slot = plan[at.slot + first + n]
        spans = [(slice(None), slice(None))]
        if partial:
            spans = [own_columns(size, place, p, piece) for p, piece in enumerate(pieces)]
        place_new(new_k, slot, kbuf.at[n], spans)
        place_new(new_v, slot, vbuf.at[n], spans)

    place_new_bias(size, place, bias)

    def request(n, carry):
        place_bias(at, size, plan, first + n, place, bias)
        for m, buf in enumerate((kbuf, vbuf)):
            view = buf.at[n, pl.ds(0, size.segment)]
            pltpu.make_async_copy(view, view, sems.at[m, n]).wait()
        pltpu.make_async_copy(qbuf.at[n], qbuf.at[n], sems.at[2, n]).wait()

        def owner(p, carry):
            column = p * size.wide if partial else (place ^ (p + pieces[0])) * size.wide
            attend_owner(
                size,
                qbuf.at[n, p],
                kbuf.at[n],
                vbuf.at[n],
                column,
                bias,
                obuf.at[p, n],
            )
            return carry

        return lax.fori_loop(0, some, owner, carry)

    lax.fori_loop(0, count, request, 0)
    copies = []
    for n, out in enumerate(outs):
        p, cut = divmod(n, len(cuts))
        view = obuf.at[p, :, pl.ds(sum(cuts[:cut]), cuts[cut])]
        copies.append(pltpu.make_async_copy(view, out, sems.at[3, n]))
    for copy in copies:
        copy.start()
    for copy in copies:
        copy.wait()


def own_columns(size, place, p, piece):
    begin = pl.multiple_of((place ^ piece) * size.wide, size.wide)
    return pl.ds(p * size.wide, size.wide), pl.ds(begin, size.wide)


def split(value, parts):
    result = []
    for _ in range(parts):
        result.append(value.astype(BF16).astype(F32))
        value = value - result[-1]
    return result


def combined(size, pieces, out):
    tokens = size.tokens
    stats = [piece[size.wide :].astype(F32) for piece in pieces]
    for j in range(size.kv_own):
        rows = [[stat[n : n + 1] for n in range(j * PARTS, (j + 1) * PARTS)] for stat in stats]
        tops = [row[0] + row[1] + row[2] for row in rows]
        peak = functools.reduce(jnp.maximum, tops)
        factors = [jnp.exp2(top - peak) for top in tops]
        denom = sum((row[3] + row[4]) * factor for row, factor in zip(rows, factors))
        mixed = sum(
            piece[j * HD : (j + 1) * HD].astype(F32) * (factor / denom)
            for piece, factor in zip(pieces, factors)
        )
        mixed = mixed.T.astype(BF16)
        for s in range(size.shared):
            cols = slice((j * size.shared + s) * HD, (j * size.shared + s + 1) * HD)
            out[:, cols] = mixed[s * tokens : (s + 1) * tokens]


def finish_kernel(at, size, parcels, lots, settled, ready, plan, *refs):
    count = sum(lots)
    some = len(parcels)
    arrived, refs = refs[:some], refs[some:]
    sources, refs = refs[: 2 * len(parcels_before(ready))], refs[2 * len(parcels_before(ready)) :]
    query, new_k, new_v = refs[:3]
    pieces, refs = refs[3:-15], refs[-13:]
    attended, after = refs[0], refs[1:3]
    kbuf, vbuf, qbuf, pbuf, bias, mixed, full, sems, out_sems, in_sems = refs[3:]
    place, slot = plan[at.place], plan[at.slot + count]
    copies = [
        pltpu.make_async_copy(arrived[-1].at[m], buf.at[pl.ds(0, size.segment)], in_sems.at[m])
        for m, buf in enumerate((kbuf, vbuf))
    ]
    copies.append(pltpu.make_async_copy(query.at[0, slot], qbuf, in_sems.at[2]))
    for copy in copies:
        copy.start()
    pieces = iter(pieces)
    before = 0
    for lot, each in enumerate([*lots, 1]):
        for i in range(size.width):
            row = 0
            while row < pbuf.shape[2] and (lot < len(lots) or i):
                piece = next(pieces)
                into = pbuf.at[i, pl.ds(before, each), pl.ds(row, piece.shape[1])]
                pltpu.make_async_copy(piece, into, in_sems.at[3]).start()
                row += piece.shape[1]
        before += each
    for position in range(settled, count):
        bufs = [full.at[n, position - settled] for n in range(2)]
        marks = [sems.at[n, position - settled] for n in range(2)]
        stage(at, plan, position, ready[position], sources, bufs, marks)
    rows = size.segment // at.nblocks
    bufs = [full.at[n, count - settled] for n in range(2)]
    marks = [sems.at[n, count - settled] for n in range(2)]

    def block(b, carry):
        begin = pl.multiple_of(plan[at.perm + count * at.nblocks + b] * rows, rows)
        into = pl.ds(pl.multiple_of(b * rows, rows), rows)
        for parcel, ref in zip(parcels, arrived):
            place_pieces(ref, bufs, marks, place, parcel[0], pl.ds(begin, rows), into)
        return carry

    lax.fori_loop(0, at.nblocks, block, 0)
    spans = [own_columns(size, place, 0, 0)]
    place_new(new_k, slot, kbuf, spans)
    place_new(new_v, slot, vbuf, spans)
    place_bias(at, size, plan, count, place, bias)
    place_new_bias(size, place, bias)
    theirs = (pbuf.at[0, pl.ds(0, count)], pbuf.at[pl.ds(1, size.width - 1)])
    for view in theirs:
        pltpu.make_async_copy(view, view, in_sems.at[3]).wait()

    def request(n, carry):
        parts = [pbuf.at[i, n] for i in range(size.width)]
        combined(size, parts, mixed.at[n])
        there = attended.at[0, plan[at.slot + n]]
        pltpu.make_async_copy(mixed.at[n], there, in_sems.at[4]).start()
        return carry

    lax.fori_loop(0, count, request, 0)
    for position in range(settled, count + 1):
        there = plan[at.slot + position]
        for n in range(2):
            view, sem = full.at[n, position - settled], sems.at[n, position - settled]
            pltpu.make_async_copy(view, view, sem).wait()
            pltpu.make_async_copy(
                view, after[n].at[0, there], out_sems.at[n, position - settled]
            ).start()
    for copy in copies:
        copy.wait()
    attend_owner(size, qbuf, kbuf, vbuf, 0, bias, pbuf.at[0, count], True)
    lax.fori_loop(count, count + 1, request, 0)
    for position in range(settled, count + 1):
        there = plan[at.slot + position]
        for n in range(2):
            view = full.at[n, position - settled]
            pltpu.make_async_copy(
                view, after[n].at[0, there], out_sems.at[n, position - settled]
            ).wait()
    pltpu.make_async_copy(mixed, mixed, in_sems.at[4]).wait()


def parcels_before(ready):
    return range(-1, max(ready))


def shards(
    query, cache_keys, cache_values, new_keys, new_values, masks, movers, block_lists, lengths
):
    groups = lax.axis_size("group")
    width = lax.axis_size("ctx")
    _, requests, segment, features = cache_keys.shape
    tokens = query.shape[2]
    matchings, _, nblocks = block_lists.shape
    own = query.shape[3] // HD
    size = Heads(width, tokens, own, features, segment)
    at = Layout(requests, nblocks, matchings)
    ready = [max(-1, n - (requests - matchings)) for n in range(requests)]
    caches = (cache_keys, cache_values)
    big = pltpu.CompilerParams(vmem_limit_bytes=40 * 1024 * 1024)
    queries = size.shared * tokens
    result = jax.ShapeDtypeStruct((size.wide + STATS, queries), BF16)
    behind = -(-new_keys.shape[2] // 16) * 16
    scores = pltpu.VMEM((segment + behind, queries), F32)
    everyone = tuple(range(width))
    halves = [part for part in (everyone[width // 2 :], everyone[: width // 2]) if part]
    near = everyone[1 : width // 2]
    parcels = [part for part in (halves[0], near, (0,)) if part]

    def held(pieces):
        return jax.ShapeDtypeStruct((2, segment, len(pieces) * size.wide), BF16)

    plan, *scalars = pl.pallas_call(
        functools.partial(plan_kernel, at, halves[:1]),
        out_shape=(
            jax.ShapeDtypeStruct((at.size,), jnp.int32),
            *[jax.ShapeDtypeStruct((1,), jnp.int32)] * matchings,
            held(halves[0]),
        ),
        in_specs=[SMEM] * 4 + [ANY] * 2,
        out_specs=(SMEM, *[SMEM] * matchings, VMEM),
        scratch_shapes=[pltpu.SemaphoreType.DMA((1,))],
        name="plan",
    )(masks, movers, block_lists.transpose(0, 2, 1), lengths.T, *caches)
    indices, initial = scalars[:matchings], scalars[matchings:]

    def lasting(microseconds):
        return pl.CostEstimate(
            flops=0, bytes_accessed=int(microseconds * 3.7e6), transcendentals=0
        )

    def pick(step, choices, sources, after=()):
        return pl.pallas_call(
            functools.partial(pick_kernel, at, step, choices),
            out_shape=list(map(held, choices)),
            in_specs=[SMEM] + [ANY] * (len(sources) + len(after)),
            out_specs=[VMEM] * len(choices),
            scratch_shapes=[pltpu.SemaphoreType.DMA((len(choices),))],
            cost_estimate=lasting(2.5),
            name=f"pick_{step}",
        )(plan, *sources, *after)

    def attend(first, count, pieces, asked, fresh, sources, partial=False, after=(), cuts=None):
        newest = ready[first : first + count]
        if not partial:
            sources = sources[: 2 * (max(newest) + 2)]
        some = len(pieces)
        held = some * size.wide if partial else features
        cuts = cuts or [result.shape[0]]
        return pl.pallas_call(
            functools.partial(attend_kernel, at, size, first, newest, pieces, partial, cuts),
            out_shape=[
                jax.ShapeDtypeStruct((count, rows, queries), BF16) for _ in pieces for rows in cuts
            ],
            in_specs=[SMEM] + [ANY] * some + [VMEM] * 2 + [ANY] * (len(sources) + len(after)),
            out_specs=[ANY] * (some * len(cuts)),
            scratch_shapes=[
                pltpu.VMEM((count, segment + behind, held), BF16),
                pltpu.VMEM((count, segment + behind, held), BF16),
                pltpu.VMEM((count, some, tokens, own * HD), BF16),
                pltpu.VMEM((some, count, *result.shape), BF16),
                scores,
                pltpu.SemaphoreType.DMA((4, max(some * len(cuts), count))),
            ],
            compiler_params=big,
            cost_estimate=lasting(1 + 1.5 * some * count),
            name=f"attend_{first}_{count}_{some}",
        )(plan, *[asked[piece] for piece in pieces], *fresh, *sources, *after)

    def send_home(pieces, results):
        return [exchange(part, "ctx", piece) if piece else part for piece, part in zip(pieces, results)]

    def settle(positions, sources):
        count = len(positions)
        newest = [ready[n] for n in positions]
        used = sources[: 2 * (max(newest) + 2)]
        return pl.pallas_call(
            functools.partial(settle_kernel, at, newest),
            out_shape=[jax.ShapeDtypeStruct(cache_keys.shape, BF16)] * 2,
            in_specs=[SMEM] + [ANY] * len(used),
            out_specs=[ANY] * 2,
            scratch_shapes=[
                pltpu.VMEM((2, count, segment, features), BF16),
                pltpu.SemaphoreType.DMA((2, count)),
            ],
            compiler_params=big,
            cost_estimate=lasting(2 * count),
            name="settle",
        )(plan, *used)

    def pad_new():
        extra = behind - new_keys.shape[2]
        return [jnp.pad(new[0], ((0, 0), (0, extra), (0, 0))) for new in (new_keys, new_values)]

    def prepare(step, sources, arrived):
        return pick(step, halves[:1], [*sources, arrived[0], arrived[0]])[0]

    def first_branch(mask):
        moving = [*initial, *pick(0, halves[1:], caches)]
        arrived = [exchange(block, "group", mask) for block in moving]
        asked = [query] + [exchange(query, "ctx", piece) for piece in everyone[1:-1]]
        return arrived, prepare(1, caches, arrived), asked, pad_new()

    def middle_branch(step, positions, prepared, asked, fresh, sources, mask):
        moving = [prepared, *pick(step, halves[1:], sources)]
        arrived = [exchange(block, "group", mask) for block in moving]
        done = send_home(
            everyone, attend(positions[0], len(positions), everyone, asked, fresh, sources)
        )
        after = settle(positions, sources) if step == 1 else []
        return arrived, prepare(step + 1, sources, arrived), done, after

    def last_branch(step, first, prepared, asked, fresh, sources, mask):
        whole = attend(first, 1, everyone, asked, fresh, sources)
        moving = [prepared, *pick(step, parcels[1:], sources, whole[:1])]
        arrived = [exchange(block, "group", mask) for block in moving]
        done = send_home(everyone, whole)
        parts, after = {}, done[:1]
        for parcel, block in zip(parcels[:-1], arrived):
            cuts = [size.wide // 2, result.shape[0] - size.wide // 2] if parcel == near else None
            part = attend(requests - 1, 1, parcel, asked, fresh, [block], True, after, cuts)
            each = len(part) // len(parcel)
            for n, piece in enumerate(parcel):
                parts[piece] = [
                    exchange(array, "ctx", piece) for array in part[n * each : (n + 1) * each]
                ]
            after = [*part[:1], *done[1:]]
        return arrived, done, [array for piece in everyone[1:] for array in parts[piece]]

    def switch(step, branch, *given):
        return lax.switch(
            indices[step].reshape(()),
            [functools.partial(branch, *given, mask) for mask in range(1, groups)],
        )

    ahead = exchange(query, "ctx", width - 1)
    arrived, prepared, asked, fresh = switch(0, first_branch)
    asked = [*asked, ahead]
    sources = [*caches, *arrived]
    lots, done, after = [], [], None
    for step in range(1, matchings - 1):
        first = sum(lots)
        positions = range(first, ready.index(step - 1) + 1)
        arrived, prepared, part, settled = switch(
            step, middle_branch, step, positions, prepared, asked, fresh, sources
        )
        after = after or settled
        sources = sources + arrived
        lots.append(len(positions))
        done += part
    arrived, part, pieces = switch(
        matchings - 1, last_branch, matchings - 1, sum(lots), prepared, asked, fresh, sources
    )
    lots.append(1)
    pieces = [*done, *part, *pieces]
    ahead = 1 + len(arrived) + len(sources) + 3 + len(pieces)
    left = requests - lots[0]
    return pl.pallas_call(
        functools.partial(finish_kernel, at, size, parcels, lots, lots[0], ready),
        out_shape=[
            jax.ShapeDtypeStruct(array.shape, BF16) for array in (query, cache_keys, cache_values)
        ],
        in_specs=[SMEM]
        + [ANY] * (len(arrived) + len(sources) + 1)
        + [VMEM] * 2
        + [ANY] * (len(pieces) + 2),
        out_specs=[ANY] * 3,
        scratch_shapes=[
            pltpu.VMEM((segment + behind, size.wide), BF16),
            pltpu.VMEM((segment + behind, size.wide), BF16),
            pltpu.VMEM((tokens, own * HD), BF16),
            pltpu.VMEM((width, requests, *result.shape), BF16),
            scores,
            pltpu.VMEM((requests, tokens, own * HD), BF16),
            pltpu.VMEM((2, left, segment, features), BF16),
            pltpu.SemaphoreType.DMA((2, left)),
            pltpu.SemaphoreType.DMA((2, left)),
            pltpu.SemaphoreType.DMA((5,)),
        ],
        input_output_aliases={ahead: 1, ahead + 1: 2},
        compiler_params=big,
        name="finish",
    )(plan, *arrived, *sources, query, *fresh, *pieces, *after)


def solution(mesh):
    placed = (
        P("group", None, None, "ctx"),
        P("group", None, "ctx", None),
        P("group", None, "ctx", None),
        P("group", None, "ctx", None),
        P("group", None, "ctx", None),
        P(),
        P(),
        P(),
        P(),
    )
    return jax.shard_map(
        shards,
        mesh=mesh,
        in_specs=placed,
        out_specs=(
            P("group", None, None, "ctx"),
            P("group", None, "ctx", None),
            P("group", None, "ctx", None),
        ),
        check_vma=False,
    )
```

```python
import functools
import math

import jax
import jax.numpy as jnp
from jax import lax
from jax.experimental import pallas as pl
from jax.experimental.pallas import tpu as pltpu
from jax.sharding import PartitionSpec as P

HD = 128
LANES = 128
PARTS = 5
STATS = 16
MASKED = -1e30
FLOOR = -1e29
BF16 = jnp.bfloat16
F32 = jnp.float32
ANY = pl.BlockSpec(memory_space=pl.ANY)
SMEM = pl.BlockSpec(memory_space=pltpu.SMEM)
VMEM = pl.BlockSpec(memory_space=pltpu.VMEM)


def exchange(block, axis, mask):
    return lax.ppermute(block, axis, [(i, i ^ mask) for i in range(lax.axis_size(axis))])


class Layout:
    def __init__(self, requests, nblocks, matchings):
        self.nblocks = nblocks
        self.slot = 0
        self.last = requests
        self.count = 2 * requests
        self.perm = 3 * requests
        self.home = self.perm + requests * nblocks
        self.mover = self.home + requests * nblocks
        self.source = self.mover + matchings
        self.place = self.source + matchings
        self.size = self.place + 1


def copy_pieces(views, out, sem, place, first):
    wide = views[0].shape[1] // lax.axis_size("ctx")

    def piece(p, carry):
        begin = pl.multiple_of((place ^ (first + p)) * wide, wide)
        into = pl.ds(pl.multiple_of(p * wide, wide), wide)
        for m, view in enumerate(views):
            pltpu.make_async_copy(view.at[:, pl.ds(begin, wide)], out.at[m, :, into], sem).start()
        return carry

    lax.fori_loop(0, out.shape[2] // wide, piece, 0)


def place_pieces(parcel, bufs, sems, place, first, rows=None, into=None):
    rows = pl.ds(0, parcel.shape[1]) if rows is None else rows
    into = rows if into is None else into
    wide = bufs[0].shape[1] // lax.axis_size("ctx")

    def piece(p, carry):
        begin = pl.multiple_of((place ^ (first + p)) * wide, wide)
        origin = pl.ds(pl.multiple_of(p * wide, wide), wide)
        for m, buf in enumerate(bufs):
            pltpu.make_async_copy(
                parcel.at[m, rows, origin], buf.at[into, pl.ds(begin, wide)], sems[m]
            ).start()
        return carry

    lax.fori_loop(0, parcel.shape[2] // wide, piece, 0)


def plan_kernel(
    at, parcels, masks, movers, lists, lengths, keys, values, plan, *refs
):
    some = len(parcels)
    indices, outs, sems = refs[: -1 - some], refs[-1 - some : -1], refs[-1]
    matchings, nblocks, _ = lists.shape
    requests = lengths.shape[0]
    here = lax.axis_index("group")
    place = lax.axis_index("ctx")
    views = [keys.at[0, movers[0, here]], values.at[0, movers[0, here]]]
    for c, (out, pieces) in enumerate(zip(outs, parcels)):
        copy_pieces(views, out, sems.at[c], place, pieces[0])
    for step, index in enumerate(indices):
        index[0] = masks[step] - 1
    plan[at.place] = place
    traced = []
    for slot in range(requests):
        group, where = here, jnp.int32(slot)
        last = jnp.int32(-1)
        blocks = [jnp.int32(b) for b in range(nblocks)]
        for step in reversed(range(matchings)):
            hit = movers[step, group] == where
            partner = group ^ masks[step]
            last = jnp.where(jnp.logical_and(hit, last < 0), step, last)
            moved = []
            for block in blocks:
                origin = block
                for j in range(nblocks):
                    origin = jnp.where(
                        lists[step, j, group] == block, lists[step, j, partner], origin
                    )
                moved.append(jnp.where(hit, origin, block))
            blocks = moved
            where = jnp.where(hit, movers[step, partner], where)
            group = jnp.where(hit, partner, group)
        traced.append((last, lengths[where, group], blocks))
    for slot in range(requests):
        last, count, blocks = traced[slot]
        rank = jnp.int32(0)
        for other in range(requests):
            if other != slot:
                ahead = traced[other][0] * requests + other < last * requests + slot
                rank = rank + ahead.astype(jnp.int32)
        plan[at.slot + rank] = jnp.int32(slot)
        plan[at.last + rank] = last
        plan[at.count + rank] = count
        for b in range(nblocks):
            plan[at.perm + rank * nblocks + b] = blocks[b]
            plan[at.home + rank * nblocks + blocks[b]] = jnp.int32(b)
    for step in range(matchings):
        mover = movers[step, here]
        source = jnp.int32(-1)
        for earlier in range(step):
            source = jnp.where(movers[earlier, here] == mover, earlier, source)
        plan[at.mover + step] = mover
        plan[at.source + step] = source
    for c, out in enumerate(outs):
        pltpu.make_async_copy(out, out, sems.at[c]).wait()


def pick_kernel(at, step, choices, plan, *refs):
    sources, outs, sems = refs[: 2 * step + 2], refs[-1 - len(choices) : -1], refs[-1]
    mover, source, place = plan[at.mover + step], plan[at.source + step], plan[at.place]
    half = lax.axis_size("ctx") // 2
    for code in range(-1, step):
        pair = sources[2 * code + 2 : 2 * code + 4]

        @pl.when(source == code)
        def _():
            for c, (out, pieces) in enumerate(zip(outs, choices)):
                if code < 0:
                    views = [view.at[0, mover] for view in pair]
                    copy_pieces(views, out, sems.at[c], place, pieces[0])
                else:
                    far = pieces[0] >= half
                    begin = (pieces[0] - half * far) * (out.shape[2] // len(pieces))
                    view = pair[0 if far else 1].at[:, :, pl.ds(begin, out.shape[2])]
                    pltpu.make_async_copy(view, out, sems.at[c]).start()

    for c, out in enumerate(outs):
        pltpu.make_async_copy(out, out, sems.at[c]).wait()


def stage(at, plan, position, newest, sources, bufs, sems):
    rows = bufs[0].shape[0] // at.nblocks
    slot, last, place = plan[at.slot + position], plan[at.last + position], plan[at.place]
    half = lax.axis_size("ctx") // 2
    for code in range(-1, newest + 1):

        @pl.when(last == code)
        def _():
            pair = sources[2 * code + 2 : 2 * code + 4]

            def block(b, carry):
                begin = pl.multiple_of(plan[at.perm + position * at.nblocks + b] * rows, rows)
                into = pl.ds(pl.multiple_of(b * rows, rows), rows)
                if code < 0:
                    for n in range(2):
                        pltpu.make_async_copy(
                            pair[n].at[0, slot, pl.ds(begin, rows)], bufs[n].at[into], sems[n]
                        ).start()
                else:
                    for parcel, first in zip(pair, (half, 0)):
                        place_pieces(parcel, bufs, sems, place, first, pl.ds(begin, rows), into)
                return carry

            lax.fori_loop(0, at.nblocks, block, 0)


def settle_kernel(at, first, ready, plan, *refs):
    sources, outs, buf, sems = refs[:-4], refs[-4:-2], refs[-2], refs[-1]
    for position, newest in enumerate(ready):
        bufs = [buf.at[n, position] for n in range(2)]
        stage(at, plan, first + position, newest, sources, bufs, [sems.at[n, position] for n in range(2)])
    for position in range(len(ready)):
        slot = plan[at.slot + first + position]
        for n in range(2):
            view, sem = buf.at[n, position], sems.at[n, position]
            pltpu.make_async_copy(view, view, sem).wait()
            pltpu.make_async_copy(view, outs[n].at[0, slot], sem).start()
    for position in range(len(ready)):
        slot = plan[at.slot + first + position]
        for n in range(2):
            view, sem = buf.at[n, position], sems.at[n, position]
            pltpu.make_async_copy(view, outs[n].at[0, slot], sem).wait()


class Heads:
    def __init__(self, width, tokens, own, features, segment):
        self.width = width
        self.tokens = tokens
        self.own = own
        self.shared = own * width * HD // features
        self.kv_own = own // self.shared
        self.wide = self.kv_own * HD
        self.segment = segment


def place_new(new, slot, buf, spans):
    rows = new.shape[1]
    for cols, origin in spans:
        buf[buf.shape[0] - rows :, cols] = new[slot, :, origin]


def place_new_bias(size, place, bias):
    fresh = size.tokens // size.width
    shape = bias[size.segment :].shape
    row = lax.broadcasted_iota(jnp.int32, shape, 0)
    token = lax.broadcasted_iota(jnp.int32, shape, 1) % size.tokens
    allowed = jnp.logical_and(row < fresh, row + place * fresh <= token)
    bias[size.segment :] = jnp.where(allowed, 0.0, MASKED).astype(F32)


def place_bias(at, size, plan, position, place, bias):
    rows = size.segment // at.nblocks
    length = plan[at.count + position]
    row = lax.broadcasted_iota(jnp.int32, (rows, bias.shape[1]), 0)

    def block(b, carry):
        limit = length - place * size.segment - plan[at.home + position * at.nblocks + b] * rows
        into = pl.ds(pl.multiple_of(b * rows, rows), rows)
        bias[into] = jnp.where(row < limit, 0.0, MASKED).astype(F32)
        return carry

    lax.fori_loop(0, at.nblocks, block, 0)


def attend_owner(size, asked, keys, values, column, bias, out, unroll=False):
    tokens, shared = size.tokens, size.shared
    scale = math.log2(math.e) / HD**0.5
    stat_row = lax.broadcasted_iota(jnp.int32, (STATS, shared * tokens), 0)

    def head(j, stats):
        cols = pl.ds(pl.multiple_of(column + j * HD, HD), HD)
        spans = [
            pl.ds(pl.multiple_of((j * shared + s) * HD, HD), HD) for s in range(shared)
        ]
        scores = lax.dot_general(
            keys[:, cols],
            jnp.concatenate([asked[:, span] for span in spans], axis=0),
            (((1,), (1,)), ((), ())),
            preferred_element_type=F32,
        )
        scores = scores * scale + bias[...]
        top = jnp.maximum(jnp.max(scores, axis=0, keepdims=True), FLOOR)
        weights = jnp.exp2(scores - top)
        total = jnp.sum(weights, axis=0, keepdims=True)
        summed = lax.dot_general(
            values[:, cols],
            weights.astype(BF16),
            (((0,), (0,)), ((), ())),
            preferred_element_type=F32,
        )
        out[pl.ds(pl.multiple_of(j * HD, HD), HD)] = summed.astype(BF16)
        for n, part in enumerate(split(top, 3) + split(total, 2)):
            stats = jnp.where(stat_row == j * PARTS + n, part, stats)
        return stats

    stats = jnp.zeros(stat_row.shape, F32)
    stats = lax.fori_loop(0, size.kv_own, head, stats, unroll=unroll)
    out[size.wide :] = stats.astype(BF16)


def attend_kernel(at, size, first, newest, pieces, partial, cuts, plan, *refs):
    count, some = len(newest), len(pieces)
    q_refs, (new_k, new_v), refs = refs[:some], refs[some : some + 2], refs[some + 2 :]
    total = some * len(cuts)
    outs, (kbuf, vbuf, qbuf, obuf, bias, sems) = refs[-6 - total : -6], refs[-6:]
    sources = refs[: -6 - total]
    place = plan[at.place]
    half = size.width // 2

    for n in range(count):
        slot, last = plan[at.slot + first + n], plan[at.last + first + n]
        bufs = [buf.at[n, pl.ds(0, size.segment)] for buf in (kbuf, vbuf)]
        marks = [sems.at[m, n] for m in range(2)]
        if partial:
            for m in range(2):
                pltpu.make_async_copy(sources[0].at[m], bufs[m], marks[m]).start()
        else:
            for code in range(-1, newest[n] + 1):

                @pl.when(last == code)
                def _():
                    pair = sources[2 * code + 2 : 2 * code + 4]
                    if code < 0:
                        for m in range(2):
                            pltpu.make_async_copy(pair[m].at[0, slot], bufs[m], marks[m]).start()
                    else:
                        for parcel, begin in zip(pair, (half, 0)):
                            place_pieces(parcel, bufs, marks, place, begin)

        for p in range(some):
            pltpu.make_async_copy(q_refs[p].at[0, slot], qbuf.at[n, p], sems.at[2, n]).start()

    for n in range(count):
        slot = plan[at.slot + first + n]
        spans = [(slice(None), slice(None))]
        if partial:
            spans = [own_columns(size, place, p, piece) for p, piece in enumerate(pieces)]
        place_new(new_k, slot, kbuf.at[n], spans)
        place_new(new_v, slot, vbuf.at[n], spans)

    place_new_bias(size, place, bias)

    def request(n, carry):
        place_bias(at, size, plan, first + n, place, bias)
        for m, buf in enumerate((kbuf, vbuf)):
            view = buf.at[n, pl.ds(0, size.segment)]
            pltpu.make_async_copy(view, view, sems.at[m, n]).wait()
        pltpu.make_async_copy(qbuf.at[n], qbuf.at[n], sems.at[2, n]).wait()

        def owner(p, carry):
            column = p * size.wide if partial else (place ^ (p + pieces[0])) * size.wide
            attend_owner(
                size,
                qbuf.at[n, p],
                kbuf.at[n],
                vbuf.at[n],
                column,
                bias,
                obuf.at[p, n],
            )
            return carry

        return lax.fori_loop(0, some, owner, carry)

    lax.fori_loop(0, count, request, 0)
    copies = []
    for n, out in enumerate(outs):
        p, cut = divmod(n, len(cuts))
        view = obuf.at[p, :, pl.ds(sum(cuts[:cut]), cuts[cut])]
        copies.append(pltpu.make_async_copy(view, out, sems.at[3, n]))
    for copy in copies:
        copy.start()
    for copy in copies:
        copy.wait()


def own_columns(size, place, p, piece):
    begin = pl.multiple_of((place ^ piece) * size.wide, size.wide)
    return pl.ds(p * size.wide, size.wide), pl.ds(begin, size.wide)


def split(value, parts):
    result = []
    for _ in range(parts):
        result.append(value.astype(BF16).astype(F32))
        value = value - result[-1]
    return result


def combined(size, pieces, out):
    tokens = size.tokens
    stats = [piece[size.wide :].astype(F32) for piece in pieces]
    for j in range(size.kv_own):
        rows = [[stat[n : n + 1] for n in range(j * PARTS, (j + 1) * PARTS)] for stat in stats]
        tops = [row[0] + row[1] + row[2] for row in rows]
        peak = functools.reduce(jnp.maximum, tops)
        factors = [jnp.exp2(top - peak) for top in tops]
        denom = sum((row[3] + row[4]) * factor for row, factor in zip(rows, factors))
        mixed = sum(
            piece[j * HD : (j + 1) * HD].astype(F32) * (factor / denom)
            for piece, factor in zip(pieces, factors)
        )
        mixed = mixed.T.astype(BF16)
        for s in range(size.shared):
            cols = slice((j * size.shared + s) * HD, (j * size.shared + s + 1) * HD)
            out[:, cols] = mixed[s * tokens : (s + 1) * tokens]


def finish_kernel(at, size, parcels, lots, settled, ready, plan, *refs):
    count = sum(lots)
    some = len(parcels)
    arrived, refs = refs[:some], refs[some:]
    sources, refs = refs[: 2 * len(parcels_before(ready))], refs[2 * len(parcels_before(ready)) :]
    query, new_k, new_v = refs[:3]
    pieces, refs = refs[3:-15], refs[-13:]
    attended, after = refs[0], refs[1:3]
    kbuf, vbuf, qbuf, pbuf, bias, mixed, full, sems, out_sems, in_sems = refs[3:]
    place, slot = plan[at.place], plan[at.slot + count]
    copies = [
        pltpu.make_async_copy(arrived[-1].at[m], buf.at[pl.ds(0, size.segment)], in_sems.at[m])
        for m, buf in enumerate((kbuf, vbuf))
    ]
    copies.append(pltpu.make_async_copy(query.at[0, slot], qbuf, in_sems.at[2]))
    for copy in copies:
        copy.start()
    pieces = iter(pieces)
    before = 0
    for lot, each in enumerate([*lots, 1]):
        for i in range(size.width):
            row = 0
            while row < pbuf.shape[2] and (lot < len(lots) or i):
                piece = next(pieces)
                into = pbuf.at[i, pl.ds(before, each), pl.ds(row, piece.shape[1])]
                pltpu.make_async_copy(piece, into, in_sems.at[3]).start()
                row += piece.shape[1]
        before += each
    for position in range(settled, count):
        bufs = [full.at[n, position - settled] for n in range(2)]
        marks = [sems.at[n, position - settled] for n in range(2)]
        stage(at, plan, position, ready[position], sources, bufs, marks)
    rows = size.segment // at.nblocks
    bufs = [full.at[n, count - settled] for n in range(2)]
    marks = [sems.at[n, count - settled] for n in range(2)]

    def block(b, carry):
        begin = pl.multiple_of(plan[at.perm + count * at.nblocks + b] * rows, rows)
        into = pl.ds(pl.multiple_of(b * rows, rows), rows)
        for parcel, ref in zip(parcels, arrived):
            place_pieces(ref, bufs, marks, place, parcel[0], pl.ds(begin, rows), into)
        return carry

    lax.fori_loop(0, at.nblocks, block, 0)
    spans = [own_columns(size, place, 0, 0)]
    place_new(new_k, slot, kbuf, spans)
    place_new(new_v, slot, vbuf, spans)
    place_bias(at, size, plan, count, place, bias)
    place_new_bias(size, place, bias)
    theirs = (pbuf.at[0, pl.ds(0, count)], pbuf.at[pl.ds(1, size.width - 1)])
    for view in theirs:
        pltpu.make_async_copy(view, view, in_sems.at[3]).wait()

    def request(n, carry):
        parts = [pbuf.at[i, n] for i in range(size.width)]
        combined(size, parts, mixed.at[n])
        there = attended.at[0, plan[at.slot + n]]
        pltpu.make_async_copy(mixed.at[n], there, in_sems.at[4]).start()
        return carry

    lax.fori_loop(0, count, request, 0)
    for position in range(settled, count + 1):
        there = plan[at.slot + position]
        for n in range(2):
            view, sem = full.at[n, position - settled], sems.at[n, position - settled]
            pltpu.make_async_copy(view, view, sem).wait()
            pltpu.make_async_copy(
                view, after[n].at[0, there], out_sems.at[n, position - settled]
            ).start()
    for copy in copies:
        copy.wait()
    attend_owner(size, qbuf, kbuf, vbuf, 0, bias, pbuf.at[0, count], True)
    lax.fori_loop(count, count + 1, request, 0)
    for position in range(settled, count + 1):
        there = plan[at.slot + position]
        for n in range(2):
            view = full.at[n, position - settled]
            pltpu.make_async_copy(
                view, after[n].at[0, there], out_sems.at[n, position - settled]
            ).wait()
    pltpu.make_async_copy(mixed, mixed, in_sems.at[4]).wait()


def parcels_before(ready):
    return range(-1, max(ready))


def shards(
    query, cache_keys, cache_values, new_keys, new_values, masks, movers, block_lists, lengths
):
    groups = lax.axis_size("group")
    width = lax.axis_size("ctx")
    _, requests, segment, features = cache_keys.shape
    tokens = query.shape[2]
    matchings, _, nblocks = block_lists.shape
    own = query.shape[3] // HD
    size = Heads(width, tokens, own, features, segment)
    at = Layout(requests, nblocks, matchings)
    ready = [max(-1, n - (requests - matchings)) for n in range(requests)]
    caches = (cache_keys, cache_values)
    big = pltpu.CompilerParams(vmem_limit_bytes=40 * 1024 * 1024)
    queries = size.shared * tokens
    result = jax.ShapeDtypeStruct((size.wide + STATS, queries), BF16)
    behind = -(-new_keys.shape[2] // 16) * 16
    scores = pltpu.VMEM((segment + behind, queries), F32)
    everyone = tuple(range(width))
    halves = [part for part in (everyone[width // 2 :], everyone[: width // 2]) if part]
    near = everyone[1 : width // 2]
    parcels = [part for part in (halves[0], near, (0,)) if part]

    def held(pieces):
        return jax.ShapeDtypeStruct((2, segment, len(pieces) * size.wide), BF16)

    plan, *scalars = pl.pallas_call(
        functools.partial(plan_kernel, at, halves[:1]),
        out_shape=(
            jax.ShapeDtypeStruct((at.size,), jnp.int32),
            *[jax.ShapeDtypeStruct((1,), jnp.int32)] * matchings,
            held(halves[0]),
        ),
        in_specs=[SMEM] * 4 + [ANY] * 2,
        out_specs=(SMEM, *[SMEM] * matchings, VMEM),
        scratch_shapes=[pltpu.SemaphoreType.DMA((1,))],
        name="plan",
    )(masks, movers, block_lists.transpose(0, 2, 1), lengths.T, *caches)
    indices, initial = scalars[:matchings], scalars[matchings:]

    def lasting(microseconds):
        return pl.CostEstimate(
            flops=0, bytes_accessed=int(microseconds * 3.7e6), transcendentals=0
        )

    def pick(step, choices, sources, after=()):
        return pl.pallas_call(
            functools.partial(pick_kernel, at, step, choices),
            out_shape=list(map(held, choices)),
            in_specs=[SMEM] + [ANY] * (len(sources) + len(after)),
            out_specs=[VMEM] * len(choices),
            scratch_shapes=[pltpu.SemaphoreType.DMA((len(choices),))],
            cost_estimate=lasting(2.5),
            name=f"pick_{step}",
        )(plan, *sources, *after)

    def attend(first, count, pieces, asked, fresh, sources, partial=False, after=(), cuts=None):
        newest = ready[first : first + count]
        if not partial:
            sources = sources[: 2 * (max(newest) + 2)]
        some = len(pieces)
        held = some * size.wide if partial else features
        cuts = cuts or [result.shape[0]]
        return pl.pallas_call(
            functools.partial(attend_kernel, at, size, first, newest, pieces, partial, cuts),
            out_shape=[
                jax.ShapeDtypeStruct((count, rows, queries), BF16) for _ in pieces for rows in cuts
            ],
            in_specs=[SMEM] + [ANY] * some + [VMEM] * 2 + [ANY] * (len(sources) + len(after)),
            out_specs=[ANY] * (some * len(cuts)),
            scratch_shapes=[
                pltpu.VMEM((count, segment + behind, held), BF16),
                pltpu.VMEM((count, segment + behind, held), BF16),
                pltpu.VMEM((count, some, tokens, own * HD), BF16),
                pltpu.VMEM((some, count, *result.shape), BF16),
                scores,
                pltpu.SemaphoreType.DMA((4, max(some * len(cuts), count))),
            ],
            compiler_params=big,
            cost_estimate=lasting(1 + 1.5 * some * count),
            name=f"attend_{first}_{count}_{some}",
        )(plan, *[asked[piece] for piece in pieces], *fresh, *sources, *after)

    def send_home(pieces, results):
        return [exchange(part, "ctx", piece) if piece else part for piece, part in zip(pieces, results)]

    def settle(positions, sources, after=()):
        count = len(positions)
        newest = [ready[n] for n in positions]
        used = sources[: 2 * (max(newest) + 2)]
        return pl.pallas_call(
            functools.partial(settle_kernel, at, positions[0], newest),
            out_shape=[jax.ShapeDtypeStruct(cache_keys.shape, BF16)] * 2,
            in_specs=[SMEM] + [ANY] * (len(used) + len(after)),
            out_specs=[ANY] * 2,
            input_output_aliases={1 + len(used) + n: n for n in range(len(after))},
            scratch_shapes=[
                pltpu.VMEM((2, count, segment, features), BF16),
                pltpu.SemaphoreType.DMA((2, count)),
            ],
            compiler_params=big,
            cost_estimate=lasting(2 * count),
            name="settle",
        )(plan, *used, *after)

    def pad_new():
        extra = behind - new_keys.shape[2]
        return [jnp.pad(new[0], ((0, 0), (0, extra), (0, 0))) for new in (new_keys, new_values)]

    def prepare(step, sources, arrived):
        return pick(step, halves[:1], [*sources, arrived[0], arrived[0]])[0]

    def first_branch(mask):
        moving = [*initial, *pick(0, halves[1:], caches)]
        arrived = [exchange(block, "group", mask) for block in moving]
        asked = [query] + [exchange(query, "ctx", piece) for piece in everyone[1:-1]]
        return arrived, prepare(1, caches, arrived), asked, pad_new()

    def middle_branch(step, positions, prepared, asked, fresh, sources, mask):
        moving = [prepared, *pick(step, halves[1:], sources)]
        arrived = [exchange(block, "group", mask) for block in moving]
        done = send_home(
            everyone, attend(positions[0], len(positions), everyone, asked, fresh, sources)
        )
        after = settle(positions, sources) if step == 1 else []
        return arrived, prepare(step + 1, sources, arrived), done, after

    def last_branch(step, first, prepared, asked, fresh, sources, settled, mask):
        whole = attend(first, 1, everyone, asked, fresh, sources)
        moving = [prepared, *pick(step, parcels[1:], sources, whole[:1])]
        arrived = [exchange(block, "group", mask) for block in moving]
        done = send_home(everyone, whole)
        parts, after = {}, done[:1]
        for parcel, block in zip(parcels[:-1], arrived):
            cuts = [size.wide // 2, result.shape[0] - size.wide // 2] if parcel == near else None
            part = attend(requests - 1, 1, parcel, asked, fresh, [block], True, after, cuts)
            each = len(part) // len(parcel)
            for n, piece in enumerate(parcel):
                parts[piece] = [
                    exchange(array, "ctx", piece) for array in part[n * each : (n + 1) * each]
                ]
            after = [*part[:1], *done[1:]]
        settled = settle(range(first, requests - 1), sources, settled)
        return arrived, done, [array for piece in everyone[1:] for array in parts[piece]], settled

    def switch(step, branch, *given):
        return lax.switch(
            indices[step].reshape(()),
            [functools.partial(branch, *given, mask) for mask in range(1, groups)],
        )

    ahead = exchange(query, "ctx", width - 1)
    arrived, prepared, asked, fresh = switch(0, first_branch)
    asked = [*asked, ahead]
    sources = [*caches, *arrived]
    lots, done, after = [], [], None
    for step in range(1, matchings - 1):
        first = sum(lots)
        positions = range(first, ready.index(step - 1) + 1)
        arrived, prepared, part, settled = switch(
            step, middle_branch, step, positions, prepared, asked, fresh, sources
        )
        after = after or settled
        sources = sources + arrived
        lots.append(len(positions))
        done += part
    arrived, part, pieces, after = switch(
        matchings - 1, last_branch, matchings - 1, sum(lots), prepared, asked, fresh, sources, after
    )
    lots.append(1)
    pieces = [*done, *part, *pieces]
    ahead = 1 + len(arrived) + len(sources) + 3 + len(pieces)
    left = 1
    return pl.pallas_call(
        functools.partial(finish_kernel, at, size, parcels, lots, requests - 1, ready),
        out_shape=[
            jax.ShapeDtypeStruct(array.shape, BF16) for array in (query, cache_keys, cache_values)
        ],
        in_specs=[SMEM]
        + [ANY] * (len(arrived) + len(sources) + 1)
        + [VMEM] * 2
        + [ANY] * (len(pieces) + 2),
        out_specs=[ANY] * 3,
        scratch_shapes=[
            pltpu.VMEM((segment + behind, size.wide), BF16),
            pltpu.VMEM((segment + behind, size.wide), BF16),
            pltpu.VMEM((tokens, own * HD), BF16),
            pltpu.VMEM((width, requests, *result.shape), BF16),
            scores,
            pltpu.VMEM((requests, tokens, own * HD), BF16),
            pltpu.VMEM((2, left, segment, features), BF16),
            pltpu.SemaphoreType.DMA((2, left)),
            pltpu.SemaphoreType.DMA((2, left)),
            pltpu.SemaphoreType.DMA((5,)),
        ],
        input_output_aliases={ahead: 1, ahead + 1: 2},
        compiler_params=big,
        name="finish",
    )(plan, *arrived, *sources, query, *fresh, *pieces, *after)


def solution(mesh):
    placed = (
        P("group", None, None, "ctx"),
        P("group", None, "ctx", None),
        P("group", None, "ctx", None),
        P("group", None, "ctx", None),
        P("group", None, "ctx", None),
        P(),
        P(),
        P(),
        P(),
    )
    return jax.shard_map(
        shards,
        mesh=mesh,
        in_specs=placed,
        out_specs=(
            P("group", None, None, "ctx"),
            P("group", None, "ctx", None),
            P("group", None, "ctx", None),
        ),
        check_vma=False,
    )
```

```python
import functools
import math

import jax
import jax.numpy as jnp
from jax import lax
from jax.experimental import pallas as pl
from jax.experimental.pallas import tpu as pltpu
from jax.sharding import PartitionSpec as P

HD = 128
LANES = 128
PARTS = 5
STATS = 16
MASKED = -1e30
FLOOR = -1e29
BF16 = jnp.bfloat16
F32 = jnp.float32
ANY = pl.BlockSpec(memory_space=pl.ANY)
SMEM = pl.BlockSpec(memory_space=pltpu.SMEM)
VMEM = pl.BlockSpec(memory_space=pltpu.VMEM)


def exchange(block, axis, mask):
    return lax.ppermute(block, axis, [(i, i ^ mask) for i in range(lax.axis_size(axis))])


class Layout:
    def __init__(self, requests, nblocks, matchings):
        self.nblocks = nblocks
        self.slot = 0
        self.last = requests
        self.count = 2 * requests
        self.perm = 3 * requests
        self.home = self.perm + requests * nblocks
        self.mover = self.home + requests * nblocks
        self.source = self.mover + matchings
        self.place = self.source + matchings
        self.size = self.place + 1


def copy_pieces(views, out, sem, place, first):
    wide = views[0].shape[1] // lax.axis_size("ctx")

    def piece(p, carry):
        begin = pl.multiple_of((place ^ (first + p)) * wide, wide)
        into = pl.ds(pl.multiple_of(p * wide, wide), wide)
        for m, view in enumerate(views):
            pltpu.make_async_copy(view.at[:, pl.ds(begin, wide)], out.at[m, :, into], sem).start()
        return carry

    lax.fori_loop(0, out.shape[2] // wide, piece, 0)


def place_pieces(parcel, bufs, sems, place, first, rows=None, into=None):
    rows = pl.ds(0, parcel.shape[1]) if rows is None else rows
    into = rows if into is None else into
    wide = bufs[0].shape[1] // lax.axis_size("ctx")

    def piece(p, carry):
        begin = pl.multiple_of((place ^ (first + p)) * wide, wide)
        origin = pl.ds(pl.multiple_of(p * wide, wide), wide)
        for m, buf in enumerate(bufs):
            pltpu.make_async_copy(
                parcel.at[m, rows, origin], buf.at[into, pl.ds(begin, wide)], sems[m]
            ).start()
        return carry

    lax.fori_loop(0, parcel.shape[2] // wide, piece, 0)


def plan_kernel(
    at, parcels, masks, movers, lists, lengths, keys, values, plan, *refs
):
    some = len(parcels)
    indices, outs, sems = refs[: -1 - some], refs[-1 - some : -1], refs[-1]
    matchings, nblocks, _ = lists.shape
    requests = lengths.shape[0]
    here = lax.axis_index("group")
    place = lax.axis_index("ctx")
    views = [keys.at[0, movers[0, here]], values.at[0, movers[0, here]]]
    for c, (out, pieces) in enumerate(zip(outs, parcels)):
        copy_pieces(views, out, sems.at[c], place, pieces[0])
    for step, index in enumerate(indices):
        index[0] = masks[step] - 1
    plan[at.place] = place
    traced = []
    for slot in range(requests):
        group, where = here, jnp.int32(slot)
        last = jnp.int32(-1)
        blocks = [jnp.int32(b) for b in range(nblocks)]
        for step in reversed(range(matchings)):
            hit = movers[step, group] == where
            partner = group ^ masks[step]
            last = jnp.where(jnp.logical_and(hit, last < 0), step, last)
            moved = []
            for block in blocks:
                origin = block
                for j in range(nblocks):
                    origin = jnp.where(
                        lists[step, j, group] == block, lists[step, j, partner], origin
                    )
                moved.append(jnp.where(hit, origin, block))
            blocks = moved
            where = jnp.where(hit, movers[step, partner], where)
            group = jnp.where(hit, partner, group)
        traced.append((last, lengths[where, group], blocks))
    for slot in range(requests):
        last, count, blocks = traced[slot]
        rank = jnp.int32(0)
        for other in range(requests):
            if other != slot:
                ahead = traced[other][0] * requests + other < last * requests + slot
                rank = rank + ahead.astype(jnp.int32)
        plan[at.slot + rank] = jnp.int32(slot)
        plan[at.last + rank] = last
        plan[at.count + rank] = count
        for b in range(nblocks):
            plan[at.perm + rank * nblocks + b] = blocks[b]
            plan[at.home + rank * nblocks + blocks[b]] = jnp.int32(b)
    for step in range(matchings):
        mover = movers[step, here]
        source = jnp.int32(-1)
        for earlier in range(step):
            source = jnp.where(movers[earlier, here] == mover, earlier, source)
        plan[at.mover + step] = mover
        plan[at.source + step] = source
    for c, out in enumerate(outs):
        pltpu.make_async_copy(out, out, sems.at[c]).wait()


def pick_kernel(at, step, choices, plan, *refs):
    sources, outs, sems = refs[: 2 * step + 2], refs[-1 - len(choices) : -1], refs[-1]
    mover, source, place = plan[at.mover + step], plan[at.source + step], plan[at.place]
    half = lax.axis_size("ctx") // 2
    for code in range(-1, step):
        pair = sources[2 * code + 2 : 2 * code + 4]

        @pl.when(source == code)
        def _():
            for c, (out, pieces) in enumerate(zip(outs, choices)):
                if code < 0:
                    views = [view.at[0, mover] for view in pair]
                    copy_pieces(views, out, sems.at[c], place, pieces[0])
                else:
                    far = pieces[0] >= half
                    begin = (pieces[0] - half * far) * (out.shape[2] // len(pieces))
                    view = pair[0 if far else 1].at[:, :, pl.ds(begin, out.shape[2])]
                    pltpu.make_async_copy(view, out, sems.at[c]).start()

    for c, out in enumerate(outs):
        pltpu.make_async_copy(out, out, sems.at[c]).wait()


def stage(at, plan, position, newest, sources, bufs, sems):
    rows = bufs[0].shape[0] // at.nblocks
    slot, last, place = plan[at.slot + position], plan[at.last + position], plan[at.place]
    half = lax.axis_size("ctx") // 2
    for code in range(-1, newest + 1):

        @pl.when(last == code)
        def _():
            pair = sources[2 * code + 2 : 2 * code + 4]

            def block(b, carry):
                begin = pl.multiple_of(plan[at.perm + position * at.nblocks + b] * rows, rows)
                into = pl.ds(pl.multiple_of(b * rows, rows), rows)
                if code < 0:
                    for n in range(2):
                        pltpu.make_async_copy(
                            pair[n].at[0, slot, pl.ds(begin, rows)], bufs[n].at[into], sems[n]
                        ).start()
                else:
                    for parcel, first in zip(pair, (half, 0)):
                        place_pieces(parcel, bufs, sems, place, first, pl.ds(begin, rows), into)
                return carry

            lax.fori_loop(0, at.nblocks, block, 0)


def settle_kernel(at, first, ready, plan, *refs):
    sources, outs, buf, sems = refs[:-4], refs[-4:-2], refs[-2], refs[-1]
    for position, newest in enumerate(ready):
        bufs = [buf.at[n, position] for n in range(2)]
        stage(at, plan, first + position, newest, sources, bufs, [sems.at[n, position] for n in range(2)])
    for position in range(len(ready)):
        slot = plan[at.slot + first + position]
        for n in range(2):
            view, sem = buf.at[n, position], sems.at[n, position]
            pltpu.make_async_copy(view, view, sem).wait()
            pltpu.make_async_copy(view, outs[n].at[0, slot], sem).start()
    for position in range(len(ready)):
        slot = plan[at.slot + first + position]
        for n in range(2):
            view, sem = buf.at[n, position], sems.at[n, position]
            pltpu.make_async_copy(view, outs[n].at[0, slot], sem).wait()


class Heads:
    def __init__(self, width, tokens, own, features, segment):
        self.width = width
        self.tokens = tokens
        self.own = own
        self.shared = own * width * HD // features
        self.kv_own = own // self.shared
        self.wide = self.kv_own * HD
        self.segment = segment


def place_new(new, slot, buf, spans):
    rows = new.shape[1]
    for cols, origin in spans:
        buf[buf.shape[0] - rows :, cols] = new[slot, :, origin]


def place_new_bias(size, place, bias):
    fresh = size.tokens // size.width
    shape = bias[size.segment :].shape
    row = lax.broadcasted_iota(jnp.int32, shape, 0)
    token = lax.broadcasted_iota(jnp.int32, shape, 1) % size.tokens
    allowed = jnp.logical_and(row < fresh, row + place * fresh <= token)
    bias[size.segment :] = jnp.where(allowed, 0.0, MASKED).astype(F32)


def place_bias(at, size, plan, position, place, bias):
    rows = size.segment // at.nblocks
    length = plan[at.count + position]
    row = lax.broadcasted_iota(jnp.int32, (rows, bias.shape[1]), 0)

    def block(b, carry):
        limit = length - place * size.segment - plan[at.home + position * at.nblocks + b] * rows
        into = pl.ds(pl.multiple_of(b * rows, rows), rows)
        bias[into] = jnp.where(row < limit, 0.0, MASKED).astype(F32)
        return carry

    lax.fori_loop(0, at.nblocks, block, 0)


def attend_owner(size, asked, keys, values, column, bias, out, unroll=False):
    tokens, shared = size.tokens, size.shared
    scale = math.log2(math.e) / HD**0.5
    stat_row = lax.broadcasted_iota(jnp.int32, (STATS, shared * tokens), 0)

    def head(j, stats):
        cols = pl.ds(pl.multiple_of(column + j * HD, HD), HD)
        spans = [
            pl.ds(pl.multiple_of((j * shared + s) * HD, HD), HD) for s in range(shared)
        ]
        scores = lax.dot_general(
            keys[:, cols],
            jnp.concatenate([asked[:, span] for span in spans], axis=0),
            (((1,), (1,)), ((), ())),
            preferred_element_type=F32,
        )
        scores = scores * scale + bias[...]
        top = jnp.maximum(jnp.max(scores, axis=0, keepdims=True), FLOOR)
        weights = jnp.exp2(scores - top)
        total = jnp.sum(weights, axis=0, keepdims=True)
        summed = lax.dot_general(
            values[:, cols],
            weights.astype(BF16),
            (((0,), (0,)), ((), ())),
            preferred_element_type=F32,
        )
        out[pl.ds(pl.multiple_of(j * HD, HD), HD)] = summed.astype(BF16)
        for n, part in enumerate(split(top, 3) + split(total, 2)):
            stats = jnp.where(stat_row == j * PARTS + n, part, stats)
        return stats

    stats = jnp.zeros(stat_row.shape, F32)
    stats = lax.fori_loop(0, size.kv_own, head, stats, unroll=unroll)
    out[size.wide :] = stats.astype(BF16)


def attend_kernel(at, size, first, newest, pieces, partial, cuts, plan, *refs):
    count, some = len(newest), len(pieces)
    q_refs, (new_k, new_v), refs = refs[:some], refs[some : some + 2], refs[some + 2 :]
    total = some * len(cuts)
    outs, (kbuf, vbuf, qbuf, obuf, bias, sems) = refs[-6 - total : -6], refs[-6:]
    sources = refs[: -6 - total]
    place = plan[at.place]
    half = size.width // 2

    for n in range(count):
        slot, last = plan[at.slot + first + n], plan[at.last + first + n]
        bufs = [buf.at[n, pl.ds(0, size.segment)] for buf in (kbuf, vbuf)]
        marks = [sems.at[m, n] for m in range(2)]
        if partial:
            for m in range(2):
                pltpu.make_async_copy(sources[0].at[m], bufs[m], marks[m]).start()
        else:
            for code in range(-1, newest[n] + 1):

                @pl.when(last == code)
                def _():
                    pair = sources[2 * code + 2 : 2 * code + 4]
                    if code < 0:
                        for m in range(2):
                            pltpu.make_async_copy(pair[m].at[0, slot], bufs[m], marks[m]).start()
                    else:
                        for parcel, begin in zip(pair, (half, 0)):
                            place_pieces(parcel, bufs, marks, place, begin)

        for p in range(some):
            pltpu.make_async_copy(q_refs[p].at[0, slot], qbuf.at[n, p], sems.at[2, n]).start()

    for n in range(count):
        slot = plan[at.slot + first + n]
        spans = [(slice(None), slice(None))]
        if partial:
            spans = [own_columns(size, place, p, piece) for p, piece in enumerate(pieces)]
        place_new(new_k, slot, kbuf.at[n], spans)
        place_new(new_v, slot, vbuf.at[n], spans)

    place_new_bias(size, place, bias)

    def request(n, carry):
        place_bias(at, size, plan, first + n, place, bias)
        for m, buf in enumerate((kbuf, vbuf)):
            view = buf.at[n, pl.ds(0, size.segment)]
            pltpu.make_async_copy(view, view, sems.at[m, n]).wait()
        pltpu.make_async_copy(qbuf.at[n], qbuf.at[n], sems.at[2, n]).wait()

        def owner(p, carry):
            column = p * size.wide if partial else (place ^ (p + pieces[0])) * size.wide
            attend_owner(
                size,
                qbuf.at[n, p],
                kbuf.at[n],
                vbuf.at[n],
                column,
                bias,
                obuf.at[p, n],
            )
            return carry

        return lax.fori_loop(0, some, owner, carry)

    lax.fori_loop(0, count, request, 0)
    copies = []
    for n, out in enumerate(outs):
        p, cut = divmod(n, len(cuts))
        view = obuf.at[p, :, pl.ds(sum(cuts[:cut]), cuts[cut])]
        copies.append(pltpu.make_async_copy(view, out, sems.at[3, n]))
    for copy in copies:
        copy.start()
    for copy in copies:
        copy.wait()


def own_columns(size, place, p, piece):
    begin = pl.multiple_of((place ^ piece) * size.wide, size.wide)
    return pl.ds(p * size.wide, size.wide), pl.ds(begin, size.wide)


def split(value, parts):
    result = []
    for _ in range(parts):
        result.append(value.astype(BF16).astype(F32))
        value = value - result[-1]
    return result


def combined(size, pieces, out):
    tokens = size.tokens
    stats = [piece[size.wide :].astype(F32) for piece in pieces]
    for j in range(size.kv_own):
        rows = [[stat[n : n + 1] for n in range(j * PARTS, (j + 1) * PARTS)] for stat in stats]
        tops = [row[0] + row[1] + row[2] for row in rows]
        peak = functools.reduce(jnp.maximum, tops)
        factors = [jnp.exp2(top - peak) for top in tops]
        denom = sum((row[3] + row[4]) * factor for row, factor in zip(rows, factors))
        mixed = sum(
            piece[j * HD : (j + 1) * HD].astype(F32) * (factor / denom)
            for piece, factor in zip(pieces, factors)
        )
        mixed = mixed.T.astype(BF16)
        for s in range(size.shared):
            cols = slice((j * size.shared + s) * HD, (j * size.shared + s + 1) * HD)
            out[:, cols] = mixed[s * tokens : (s + 1) * tokens]


def finish_kernel(at, size, parcels, lots, settled, ready, plan, *refs):
    count = sum(lots)
    some = len(parcels)
    arrived, refs = refs[:some], refs[some:]
    sources, refs = refs[: 2 * len(parcels_before(ready))], refs[2 * len(parcels_before(ready)) :]
    query, new_k, new_v = refs[:3]
    pieces, refs = refs[3:-15], refs[-13:]
    attended, after = refs[0], refs[1:3]
    kbuf, vbuf, qbuf, pbuf, bias, mixed, full, sems, out_sems, in_sems = refs[3:]
    place, slot = plan[at.place], plan[at.slot + count]
    copies = [
        pltpu.make_async_copy(arrived[-1].at[m], buf.at[pl.ds(0, size.segment)], in_sems.at[m])
        for m, buf in enumerate((kbuf, vbuf))
    ]
    copies.append(pltpu.make_async_copy(query.at[0, slot], qbuf, in_sems.at[2]))
    for copy in copies:
        copy.start()
    pieces = iter(pieces)
    before = 0
    for lot, each in enumerate([*lots, 1]):
        for i in range(size.width):
            row = 0
            while row < pbuf.shape[2] and (lot < len(lots) or i):
                piece = next(pieces)
                into = pbuf.at[i, pl.ds(before, each), pl.ds(row, piece.shape[1])]
                pltpu.make_async_copy(piece, into, in_sems.at[3]).start()
                row += piece.shape[1]
        before += each
    for position in range(settled, count):
        bufs = [full.at[n, position - settled] for n in range(2)]
        marks = [sems.at[n, position - settled] for n in range(2)]
        stage(at, plan, position, ready[position], sources, bufs, marks)
    rows = size.segment // at.nblocks
    bufs = [full.at[n, count - settled] for n in range(2)]
    marks = [sems.at[n, count - settled] for n in range(2)]

    def block(b, carry):
        begin = pl.multiple_of(plan[at.perm + count * at.nblocks + b] * rows, rows)
        into = pl.ds(pl.multiple_of(b * rows, rows), rows)
        for parcel, ref in zip(parcels, arrived):
            place_pieces(ref, bufs, marks, place, parcel[0], pl.ds(begin, rows), into)
        return carry

    lax.fori_loop(0, at.nblocks, block, 0)
    spans = [own_columns(size, place, 0, 0)]
    place_new(new_k, slot, kbuf, spans)
    place_new(new_v, slot, vbuf, spans)
    place_bias(at, size, plan, count, place, bias)
    place_new_bias(size, place, bias)
    for copy in copies:
        copy.wait()
    attend_owner(size, qbuf, kbuf, vbuf, 0, bias, pbuf.at[0, count], True)
    for position in range(settled, count + 1):
        there = plan[at.slot + position]
        for n in range(2):
            view, sem = full.at[n, position - settled], sems.at[n, position - settled]
            pltpu.make_async_copy(view, view, sem).wait()
            pltpu.make_async_copy(
                view, after[n].at[0, there], out_sems.at[n, position - settled]
            ).start()
    theirs = (pbuf.at[0, pl.ds(0, count)], pbuf.at[pl.ds(1, size.width - 1)])
    for view in theirs:
        pltpu.make_async_copy(view, view, in_sems.at[3]).wait()

    def request(n, carry):
        parts = [pbuf.at[i, n] for i in range(size.width)]
        combined(size, parts, mixed.at[n])
        there = attended.at[0, plan[at.slot + n]]
        pltpu.make_async_copy(mixed.at[n], there, in_sems.at[4]).start()
        return carry

    lax.fori_loop(0, count + 1, request, 0)
    for position in range(settled, count + 1):
        there = plan[at.slot + position]
        for n in range(2):
            view = full.at[n, position - settled]
            pltpu.make_async_copy(
                view, after[n].at[0, there], out_sems.at[n, position - settled]
            ).wait()
    pltpu.make_async_copy(mixed, mixed, in_sems.at[4]).wait()


def parcels_before(ready):
    return range(-1, max(ready))


def shards(
    query, cache_keys, cache_values, new_keys, new_values, masks, movers, block_lists, lengths
):
    groups = lax.axis_size("group")
    width = lax.axis_size("ctx")
    _, requests, segment, features = cache_keys.shape
    tokens = query.shape[2]
    matchings, _, nblocks = block_lists.shape
    own = query.shape[3] // HD
    size = Heads(width, tokens, own, features, segment)
    at = Layout(requests, nblocks, matchings)
    ready = [max(-1, n - (requests - matchings)) for n in range(requests)]
    caches = (cache_keys, cache_values)
    big = pltpu.CompilerParams(vmem_limit_bytes=40 * 1024 * 1024)
    queries = size.shared * tokens
    result = jax.ShapeDtypeStruct((size.wide + STATS, queries), BF16)
    behind = -(-new_keys.shape[2] // 16) * 16
    scores = pltpu.VMEM((segment + behind, queries), F32)
    everyone = tuple(range(width))
    halves = [part for part in (everyone[width // 2 :], everyone[: width // 2]) if part]
    near = everyone[1 : width // 2]
    parcels = [part for part in (halves[0], near, (0,)) if part]

    def held(pieces):
        return jax.ShapeDtypeStruct((2, segment, len(pieces) * size.wide), BF16)

    plan, *scalars = pl.pallas_call(
        functools.partial(plan_kernel, at, halves[:1]),
        out_shape=(
            jax.ShapeDtypeStruct((at.size,), jnp.int32),
            *[jax.ShapeDtypeStruct((1,), jnp.int32)] * matchings,
            held(halves[0]),
        ),
        in_specs=[SMEM] * 4 + [ANY] * 2,
        out_specs=(SMEM, *[SMEM] * matchings, VMEM),
        scratch_shapes=[pltpu.SemaphoreType.DMA((1,))],
        name="plan",
    )(masks, movers, block_lists.transpose(0, 2, 1), lengths.T, *caches)
    indices, initial = scalars[:matchings], scalars[matchings:]

    def lasting(microseconds):
        return pl.CostEstimate(
            flops=0, bytes_accessed=int(microseconds * 3.7e6), transcendentals=0
        )

    def pick(step, choices, sources, after=()):
        return pl.pallas_call(
            functools.partial(pick_kernel, at, step, choices),
            out_shape=list(map(held, choices)),
            in_specs=[SMEM] + [ANY] * (len(sources) + len(after)),
            out_specs=[VMEM] * len(choices),
            scratch_shapes=[pltpu.SemaphoreType.DMA((len(choices),))],
            cost_estimate=lasting(2.5),
            name=f"pick_{step}",
        )(plan, *sources, *after)

    def attend(first, count, pieces, asked, fresh, sources, partial=False, after=(), cuts=None):
        newest = ready[first : first + count]
        if not partial:
            sources = sources[: 2 * (max(newest) + 2)]
        some = len(pieces)
        held = some * size.wide if partial else features
        cuts = cuts or [result.shape[0]]
        return pl.pallas_call(
            functools.partial(attend_kernel, at, size, first, newest, pieces, partial, cuts),
            out_shape=[
                jax.ShapeDtypeStruct((count, rows, queries), BF16) for _ in pieces for rows in cuts
            ],
            in_specs=[SMEM] + [ANY] * some + [VMEM] * 2 + [ANY] * (len(sources) + len(after)),
            out_specs=[ANY] * (some * len(cuts)),
            scratch_shapes=[
                pltpu.VMEM((count, segment + behind, held), BF16),
                pltpu.VMEM((count, segment + behind, held), BF16),
                pltpu.VMEM((count, some, tokens, own * HD), BF16),
                pltpu.VMEM((some, count, *result.shape), BF16),
                scores,
                pltpu.SemaphoreType.DMA((4, max(some * len(cuts), count))),
            ],
            compiler_params=big,
            cost_estimate=lasting(1 + 1.5 * some * count),
            name=f"attend_{first}_{count}_{some}",
        )(plan, *[asked[piece] for piece in pieces], *fresh, *sources, *after)

    def send_home(pieces, results):
        return [exchange(part, "ctx", piece) if piece else part for piece, part in zip(pieces, results)]

    def settle(positions, sources, after=()):
        count = len(positions)
        newest = [ready[n] for n in positions]
        used = sources[: 2 * (max(newest) + 2)]
        return pl.pallas_call(
            functools.partial(settle_kernel, at, positions[0], newest),
            out_shape=[jax.ShapeDtypeStruct(cache_keys.shape, BF16)] * 2,
            in_specs=[SMEM] + [ANY] * (len(used) + len(after)),
            out_specs=[ANY] * 2,
            input_output_aliases={1 + len(used) + n: n for n in range(len(after))},
            scratch_shapes=[
                pltpu.VMEM((2, count, segment, features), BF16),
                pltpu.SemaphoreType.DMA((2, count)),
            ],
            compiler_params=big,
            cost_estimate=lasting(2 * count),
            name="settle",
        )(plan, *used, *after)

    def pad_new():
        extra = behind - new_keys.shape[2]
        return [jnp.pad(new[0], ((0, 0), (0, extra), (0, 0))) for new in (new_keys, new_values)]

    def prepare(step, sources, arrived):
        return pick(step, halves[:1], [*sources, arrived[0], arrived[0]])[0]

    def first_branch(mask):
        moving = [*initial, *pick(0, halves[1:], caches)]
        arrived = [exchange(block, "group", mask) for block in moving]
        asked = [query] + [exchange(query, "ctx", piece) for piece in everyone[1:-1]]
        return arrived, prepare(1, caches, arrived), asked, pad_new()

    def middle_branch(step, positions, prepared, asked, fresh, sources, mask):
        moving = [prepared, *pick(step, halves[1:], sources)]
        arrived = [exchange(block, "group", mask) for block in moving]
        done = send_home(
            everyone, attend(positions[0], len(positions), everyone, asked, fresh, sources)
        )
        after = settle(positions, sources) if step == 1 else []
        return arrived, prepare(step + 1, sources, arrived), done, after

    def last_branch(step, first, prepared, asked, fresh, sources, settled, mask):
        whole = attend(first, 1, everyone, asked, fresh, sources)
        moving = [prepared, *pick(step, parcels[1:], sources, whole[:1])]
        arrived = [exchange(block, "group", mask) for block in moving]
        done = send_home(everyone, whole)
        parts, after = {}, done[:1]
        for parcel, block in zip(parcels[:-1], arrived):
            cuts = [size.wide // 2, result.shape[0] - size.wide // 2] if parcel == near else None
            part = attend(requests - 1, 1, parcel, asked, fresh, [block], True, after, cuts)
            each = len(part) // len(parcel)
            for n, piece in enumerate(parcel):
                parts[piece] = [
                    exchange(array, "ctx", piece) for array in part[n * each : (n + 1) * each]
                ]
            after = [*part[:1], *done[1:]]
        settled = settle(range(first, requests - 1), sources, settled)
        return arrived, done, [array for piece in everyone[1:] for array in parts[piece]], settled

    def switch(step, branch, *given):
        return lax.switch(
            indices[step].reshape(()),
            [functools.partial(branch, *given, mask) for mask in range(1, groups)],
        )

    ahead = exchange(query, "ctx", width - 1)
    arrived, prepared, asked, fresh = switch(0, first_branch)
    asked = [*asked, ahead]
    sources = [*caches, *arrived]
    lots, done, after = [], [], None
    for step in range(1, matchings - 1):
        first = sum(lots)
        positions = range(first, ready.index(step - 1) + 1)
        arrived, prepared, part, settled = switch(
            step, middle_branch, step, positions, prepared, asked, fresh, sources
        )
        after = after or settled
        sources = sources + arrived
        lots.append(len(positions))
        done += part
    arrived, part, pieces, after = switch(
        matchings - 1, last_branch, matchings - 1, sum(lots), prepared, asked, fresh, sources, after
    )
    lots.append(1)
    pieces = [*done, *part, *pieces]
    ahead = 1 + len(arrived) + len(sources) + 3 + len(pieces)
    left = 1
    return pl.pallas_call(
        functools.partial(finish_kernel, at, size, parcels, lots, requests - 1, ready),
        out_shape=[
            jax.ShapeDtypeStruct(array.shape, BF16) for array in (query, cache_keys, cache_values)
        ],
        in_specs=[SMEM]
        + [ANY] * (len(arrived) + len(sources) + 1)
        + [VMEM] * 2
        + [ANY] * (len(pieces) + 2),
        out_specs=[ANY] * 3,
        scratch_shapes=[
            pltpu.VMEM((segment + behind, size.wide), BF16),
            pltpu.VMEM((segment + behind, size.wide), BF16),
            pltpu.VMEM((tokens, own * HD), BF16),
            pltpu.VMEM((width, requests, *result.shape), BF16),
            scores,
            pltpu.VMEM((requests, tokens, own * HD), BF16),
            pltpu.VMEM((2, left, segment, features), BF16),
            pltpu.SemaphoreType.DMA((2, left)),
            pltpu.SemaphoreType.DMA((2, left)),
            pltpu.SemaphoreType.DMA((5,)),
        ],
        input_output_aliases={ahead: 1, ahead + 1: 2},
        compiler_params=big,
        name="finish",
    )(plan, *arrived, *sources, query, *fresh, *pieces, *after)


def solution(mesh):
    placed = (
        P("group", None, None, "ctx"),
        P("group", None, "ctx", None),
        P("group", None, "ctx", None),
        P("group", None, "ctx", None),
        P("group", None, "ctx", None),
        P(),
        P(),
        P(),
        P(),
    )
    return jax.shard_map(
        shards,
        mesh=mesh,
        in_specs=placed,
        out_specs=(
            P("group", None, None, "ctx"),
            P("group", None, "ctx", None),
            P("group", None, "ctx", None),
        ),
        check_vma=False,
    )
```
